32 devices in a mesh: section: 4 (over y, core), blk: 8 (over z, x).
Axes of the slice: x: 2, y: 2, z: 4, core: 2. Of those that a mesh axis runs over, the one named last changes fastest.
Arguments:
- residual: float32 [1536, 32, 128], P(('section', 'blk')), may hold values from -6 to 6
- kin_inverse: float32 [1536, 32, 32], P(('section', 'blk'))
- cell_weight: float32 [1536, 128], P(('section', 'blk')), may hold values from 0.5 to 1
- upwind_frac: float32 [1536, 4, 128], P(('section', 'blk')), may hold values from 0.2 to 0.7
- block_level: int32 [1536], P(('section', 'blk')), may hold values from 0 to 5, as said below
- send_in: int32 [32, 5, 8], P(('section', 'blk')), may hold values from 0 to 48, as said below
- send_down: int32 [32, 5, 8], P(('section', 'blk')), may hold values from 0 to 48, as said below
- upwind_slot: int32 [1536, 4], P(('section', 'blk')), may hold values from 0 to 128, as said below
Outputs:
- newton_step: float32 [1536, 32, 128], P(('section', 'blk'))
The draws below stay inside these ranges and needn't reach their ends.
Inputs may be any that keep to these rules, and one draw needn't show every extreme that they name: `block_level`: on each device the blocks of levels 0 to 5 number 48 * 8 / 24, 6 / 24, 4 / 24, 3 / 24, 2 / 24 and 1 / 24 in some cyclic order of the levels, so one level holds 16 blocks of every device. `send_in`: an entry other than 48 names a block of level l on the sending device, for entry [d, l, i]. About half of the entries are none; for every section and level some device receives a block from every device of its section. `send_down`: as send_in, for the owner i of the next section. The last section sends none; for every other section and level some device of the next section receives a block from every device of the sending section. `upwind_slot`: every source of a block has a lower level than the block (a slot of send level l counts as level l), and a slot that is named holds a block; blocks of level 0 have none.
All inputs are finite; a program needn't handle non-finite values.
Results may differ from the reference program's by a relative error of at most 0.0001.
Values sent between devices are 32-bit elements; how exact they have to be, the bound alone decides.
No kernel may reach another device: no remote copies, remote signals or barrier semaphores. Data moves between devices by JAX's collectives and lax.ppermute only.
A program may use at most 64 MiB of HBM per device.

```python
import math
import jax
import jax.numpy as jnp
import numpy as np
from jax import lax

SPEC = 32
CELLS = 128
LEVELS = 6
UPW = 4
BLK_DEV = 48
BLOCKS = 1536
N_SECTION = 4
N_BLK = 8


def routing(key):
    devices = N_SECTION * N_BLK
    rounds = LEVELS - 1
    keys = jax.random.split(key, 10)
    pattern = np.repeat(np.arange(LEVELS), np.array([8, 6, 4, 3, 2, 1]) * (BLK_DEV // 24))
    offset = jax.random.randint(keys[0], (devices, 1), 0, LEVELS)
    cyclic = (jnp.asarray(pattern, jnp.int32)[None, :] + offset) % LEVELS
    local_iota = jnp.arange(BLK_DEV, dtype=jnp.int32)
    shuffle = jax.random.randint(keys[1], (devices, BLK_DEV), 0, 1 << 20) * BLK_DEV + local_iota[None, :]
    order = jnp.argsort(shuffle, axis=1)
    levels = jnp.take_along_axis(cyclic, order, axis=1).astype(jnp.int32)
    round_ids = jnp.arange(rounds, dtype=jnp.int32)
    eligible = levels[:, None, None, :] == round_ids[None, :, None, None]
    section_of = (jnp.arange(devices, dtype=jnp.int32) // N_BLK)[:, None, None]
    peer_ids = jnp.arange(N_BLK, dtype=jnp.int32)[None, None, :]

    def pick(key_pick, key_fill, key_star):
        scores = jax.random.randint(key_pick, (devices, rounds, N_BLK, BLK_DEV), 0, 1 << 20) * BLK_DEV + local_iota
        chosen = jnp.argmax(jnp.where(eligible, scores, -1), axis=-1).astype(jnp.int32)
        coin = jax.random.randint(key_fill, (devices, rounds, N_BLK), 0, 2) == 1
        star = jax.random.randint(key_star, (N_SECTION, rounds), 0, N_BLK)
        forced = star[section_of[:, 0, 0]][:, :, None] == peer_ids
        return jnp.where(coin | forced, chosen, BLK_DEV).astype(jnp.int32)
    send_in = pick(keys[2], keys[3], keys[4])
    send_down = jnp.where(section_of == N_SECTION - 1, BLK_DEV, pick(keys[5], keys[6], keys[7])).astype(jnp.int32)
    in_view = send_in.reshape(N_SECTION, N_BLK, rounds, N_BLK).transpose(0, 3, 2, 1)
    filled_in = (in_view != BLK_DEV).reshape(devices, rounds * N_BLK)
    down_view = send_down.reshape(N_SECTION, N_BLK, rounds, N_BLK).transpose(0, 3, 2, 1)
    down_view = jnp.concatenate([jnp.full((1, N_BLK, rounds, N_BLK), BLK_DEV, jnp.int32), down_view[:-1]], axis=0)
    filled_down = (down_view != BLK_DEV).reshape(devices, rounds * N_BLK)
    filled = jnp.concatenate([filled_in, filled_down], axis=1)
    candidates = 2 * rounds * N_BLK
    cand_level = jnp.tile(jnp.repeat(round_ids, N_BLK), 2)
    cand_iota = jnp.arange(candidates, dtype=jnp.int32)
    usable = filled[:, None, :] & (cand_level[None, None, :] < levels[:, :, None])
    remote_scores = jax.random.randint(keys[8], (devices, BLK_DEV, candidates), 0, 1 << 20) * candidates + cand_iota
    masked = jnp.where(usable, remote_scores, -1 - cand_iota)
    top_values, top_index = lax.top_k(masked, UPW - 1)
    remote_slot = jnp.where(top_values >= 0, BLK_DEV + 1 + top_index, BLK_DEV)
    lower = levels[:, None, :] < levels[:, :, None]
    local_scores = jax.random.randint(keys[9], (devices, BLK_DEV, BLK_DEV), 0, 1 << 20) * BLK_DEV + local_iota
    local_pick = jnp.argmax(jnp.where(lower, local_scores, -1), axis=-1)
    local_slot = jnp.where(jnp.any(lower, axis=-1), local_pick, BLK_DEV)
    upwind = jnp.concatenate([local_slot[:, :, None], remote_slot], axis=-1).reshape(devices * BLK_DEV, UPW)
    return (levels.reshape(-1), send_in, send_down, upwind.astype(jnp.int32))


def draw_block_level(key, part):
    return routing(jax.random.fold_in(key, 11))[0]


def draw_send_in(key, part):
    return routing(jax.random.fold_in(key, 11))[1]


def draw_send_down(key, part):
    return routing(jax.random.fold_in(key, 11))[2]


def draw_upwind_slot(key, part):
    return routing(jax.random.fold_in(key, 11))[3]


def draw_kin_inverse(key, part):
    key_diag, key_off = jax.random.split(key)
    count = BLK_DEV * N_SECTION * N_BLK
    diagonal = jax.random.uniform(key_diag, (count, SPEC), jnp.float32, 0.6, 1.0)
    spread = jax.random.normal(key_off, (count, SPEC, SPEC), jnp.float32) * (0.35 / math.sqrt(SPEC))
    return spread + diagonal[:, :, None] * jnp.eye(SPEC, dtype=jnp.float32)[None, :, :]


def block_levels(key, dims, cuts, least, high):
    factor_of = 1.0
    for position, shards_of in cuts:
        heights = jax.random.uniform(jax.random.fold_in(jax.random.fold_in(key, 6), position), (shards_of,), jnp.float32, least / len(cuts), high / len(cuts))
        factor_of = factor_of * jnp.repeat(jnp.exp(heights), dims[position] // shards_of).reshape((-1,) + (1,) * (len(dims) - 1 - position))
    return factor_of


def noise(key, dims, scale, limit, shards=(), kind=jnp.bfloat16):
    drawn = scale * jax.random.normal(key, dims, jnp.float32)
    if shards:
        drawn = drawn * block_levels(key, dims, shards, -0.22, 0.18)
    return jnp.clip(drawn, -limit, limit).astype(kind)


def setup_inputs(seed: int = 0) -> dict:
    key_list = jax.random.split(jax.random.key(seed), 9)
    return {
        "residual": noise(key_list[0], (BLOCKS, SPEC, CELLS), 1.0, 6.0, ((0, 32),), jnp.float32),
        "kin_inverse": draw_kin_inverse(jax.random.fold_in(key_list[8], 71), 0),
        "cell_weight": jnp.clip(jnp.exp(math.log(1.0) - 0.6931472 * jax.random.uniform(key_list[2], (BLOCKS, CELLS), jnp.float32) ** block_levels(key_list[2], (BLOCKS, CELLS), ((0, 32),), -0.2, 0.2)), 0.5, 1.0),
        "upwind_frac": jnp.clip(0.2 + 0.5 * jax.random.uniform(key_list[3], (BLOCKS, UPW, CELLS), jnp.float32) ** block_levels(key_list[3], (BLOCKS, UPW, CELLS), ((0, 32),), -0.2, 0.2), 0.2, 0.7),
        "block_level": draw_block_level(jax.random.fold_in(key_list[8], 71), 0),
        "send_in": draw_send_in(jax.random.fold_in(key_list[8], 71), 0),
        "send_down": draw_send_down(jax.random.fold_in(key_list[8], 71), 0),
        "upwind_slot": draw_upwind_slot(jax.random.fold_in(key_list[8], 71), 0),
    }


def resolve(send_in, send_down, upwind_slot):
    rounds = LEVELS - 1
    block_ids = jnp.arange(BLOCKS, dtype=jnp.int32)[:, None]
    device_id = block_ids // BLK_DEV
    section_id = device_id // N_BLK
    owner_id = device_id % N_BLK
    base_in = BLK_DEV + 1
    base_down = base_in + rounds * N_BLK
    in_part = jnp.clip(upwind_slot - base_in, 0, rounds * N_BLK - 1).astype(jnp.int32)
    peer_dev = section_id * N_BLK + in_part % N_BLK
    peer_local = send_in.reshape(-1)[((peer_dev * rounds + in_part // N_BLK) * N_BLK + owner_id).astype(jnp.int32)]
    down_part = jnp.clip(upwind_slot - base_down, 0, rounds * N_BLK - 1).astype(jnp.int32)
    upper_dev = jnp.maximum(section_id - 1, 0) * N_BLK + down_part % N_BLK
    upper_local = send_down.reshape(-1)[((upper_dev * rounds + down_part // N_BLK) * N_BLK + owner_id).astype(jnp.int32)]
    local_ids = jnp.where(upwind_slot < BLK_DEV, device_id * BLK_DEV + upwind_slot, BLOCKS)
    peer_ids = jnp.where(peer_local < BLK_DEV, peer_dev * BLK_DEV + peer_local, BLOCKS)
    upper_ids = jnp.where((upper_local < BLK_DEV) & (section_id > 0), upper_dev * BLK_DEV + upper_local, BLOCKS)
    chosen = jnp.where(upwind_slot <= BLK_DEV, local_ids, jnp.where(upwind_slot < base_down, peer_ids, upper_ids))
    return chosen.astype(jnp.int32)


def reference(residual, kin_inverse, cell_weight, upwind_frac, block_level, send_in, send_down, upwind_slot):
    source_ids = resolve(send_in, send_down, upwind_slot)
    padding = jnp.zeros((1, SPEC, CELLS), jnp.float32)
    solution = jnp.concatenate([jnp.zeros((BLOCKS, SPEC, CELLS), jnp.float32), padding], axis=0)
    for level_id in range(LEVELS):
        inflow = residual
        for neighbour in range(UPW):
            inflow = inflow + upwind_frac[:, neighbour, None, :] * solution[source_ids[:, neighbour]]
        solved = cell_weight[:, None, :] * jnp.einsum("bij,bjc->bic", kin_inverse, inflow, precision=lax.Precision.HIGHEST)
        updated = jnp.where((block_level == level_id)[:, None, None], solved, solution[:BLOCKS])
        solution = jnp.concatenate([updated, padding], axis=0)
    return solution[:BLOCKS]
```

```python
import functools

import jax
import jax.numpy as jnp
from jax import lax
from jax.experimental import pallas as pl
from jax.experimental.pallas import tpu as pltpu
from jax.sharding import PartitionSpec as P

GROUP = 8


def passed_along(value, axis, steps):
    count = lax.axis_size(axis)
    leading, last = (max(0, -steps), min(count, count - steps))
    return lax.ppermute(value, axis, [(source, source + steps) for source in range(leading, last)])


def solve_level(level, blocks, upw, rounds, groups, *refs):
    refs = list(refs)
    numbers = refs.pop(0)
    residual, kin, weight, frac = (refs.pop(0) for _ in range(4))
    if level > 0:
        from_peers, from_above, _ = (refs.pop(0) for _ in range(3))
    pool = refs.pop(0)
    last = refs.pop(0)
    chosen = refs.pop(0)
    slots_at = blocks
    peers_at = slots_at + blocks * upw
    downs_at = peers_at + rounds * groups

    if level == 0:
        pool[blocks] = jnp.zeros(pool.shape[1:], pool.dtype)
    else:
        first = blocks + 1 + (level - 1) * groups
        pool[pl.ds(first, groups)] = from_peers[...]
        pool[pl.ds(first + rounds * groups, groups)] = from_above[...]

    def listed(block, count):
        chosen[count] = block
        return count + jnp.where(numbers[block] == level, 1, 0)

    count = lax.fori_loop(0, blocks, listed, 0)

    def solve_group(group, carry):
        ids = [chosen[jnp.minimum(group * GROUP + i, count - 1)] for i in range(GROUP)]
        solved = []
        for block in ids:
            inflow = residual[block]
            if level > 0:
                parts = frac[block]
                for k in range(upw):
                    inflow = inflow + parts[k : k + 1, :] * pool[numbers[slots_at + block * upw + k]]
            mixed = jnp.dot(
                kin[block], inflow, precision=lax.Precision.HIGHEST, preferred_element_type=jnp.float32
            )
            solved.append(weight[pl.ds(block, 1), :] * mixed)
        for block, value in zip(ids, solved):
            pool[block] = value
        return carry

    lax.fori_loop(0, (count + GROUP - 1) // GROUP, solve_group, 0)

    if level < rounds:
        for j in range(groups):
            last[j, 0] = pool[numbers[peers_at + level * groups + j]]
            last[j, 1] = pool[numbers[downs_at + level * groups + j]]
    else:
        last[...] = pool[pl.ds(0, blocks)]


def shards(
    residual, kin_inverse, cell_weight, upwind_frac, block_level, send_in, send_down, upwind_slot
):
    blocks, species, cells = residual.shape
    groups = lax.axis_size("blk")
    rounds = send_in.shape[1]
    upw = upwind_slot.shape[1]
    numbers = jnp.concatenate(
        [block_level, upwind_slot.reshape(-1), send_in.reshape(-1), send_down.reshape(-1)]
    )
    slots = blocks + 1 + 2 * rounds * groups
    smem = pl.BlockSpec(memory_space=pltpu.SMEM)
    vmem = pl.BlockSpec(memory_space=pltpu.VMEM)
    pool = None
    for level in range(rounds + 1):
        operands = [numbers, residual, kin_inverse, cell_weight, upwind_frac]
        aliases = {}
        if level > 0:
            aliases = {7: 0}
            operands += [from_peers, from_above, pool]
        if level < rounds:
            last = jax.ShapeDtypeStruct((groups, 2, species, cells), jnp.float32)
        else:
            last = jax.ShapeDtypeStruct((blocks, species, cells), jnp.float32)
        pool, out = pl.pallas_call(
            functools.partial(solve_level, level, blocks, upw, rounds, groups),
            in_specs=[smem] + [vmem] * (len(operands) - 1),
            out_specs=[vmem, vmem],
            out_shape=[jax.ShapeDtypeStruct((slots, species, cells), jnp.float32), last],
            scratch_shapes=[pltpu.SMEM((blocks + 1,), jnp.int32)],
            input_output_aliases=aliases,
            compiler_params=pltpu.CompilerParams(vmem_limit_bytes=40 * 1024 * 1024),
            name="solve_level",
        )(*operands)
        if level < rounds:
            arrived = lax.all_to_all(out, "blk", split_axis=0, concat_axis=0, tiled=True)
            from_peers = arrived[:, 0]
            from_above = passed_along(arrived[:, 1], "section", 1)
    return out


def solution(mesh):
    return jax.shard_map(
        shards,
        mesh=mesh,
        in_specs=(
            P(("section", "blk"), None, None),
            P(("section", "blk"), None, None),
            P(("section", "blk"), None),
            P(("section", "blk"), None, None),
            P(("section", "blk")),
            P(("section", "blk"), None, None),
            P(("section", "blk"), None, None),
            P(("section", "blk"), None),
        ),
        out_specs=P(("section", "blk"), None, None),
        check_vma=False,
    )
```

```python
import functools

import jax
import jax.numpy as jnp
from jax import lax
from jax.experimental import pallas as pl
from jax.experimental.pallas import tpu as pltpu
from jax.sharding import PartitionSpec as P

GROUP = 8


def solve_level(level, blocks, upw, rounds, sections, groups, *refs):
    refs = list(refs)
    numbers = refs.pop(0)
    residual, kin, weight, frac = (refs.pop(0) for _ in range(4))
    if level > 0:
        arrived, _ = (refs.pop(0) for _ in range(2))
    pool = refs.pop(0)
    last = refs.pop(0)
    chosen = refs.pop(0)
    slots_at = blocks
    peers_at = slots_at + blocks * upw
    downs_at = peers_at + rounds * groups
    section = numbers[downs_at + rounds * groups]
    above = lax.rem(section + sections - 1, sections)
    below = lax.rem(section + 1, sections)

    if level == 0:
        pool[blocks] = jnp.zeros(pool.shape[1:], pool.dtype)
    else:
        first = blocks + 1 + (level - 1) * groups
        pool[pl.ds(first, groups)] = arrived[pl.ds(section * groups, groups)]
        pool[pl.ds(first + rounds * groups, groups)] = arrived[pl.ds(above * groups, groups)]

    def listed(block, count):
        chosen[count] = block
        return count + jnp.where(numbers[block] == level, 1, 0)

    count = lax.fori_loop(0, blocks, listed, 0)

    def solve_group(group, carry):
        ids = [chosen[jnp.minimum(group * GROUP + i, count - 1)] for i in range(GROUP)]
        solved = []
        for block in ids:
            inflow = residual[block]
            if level > 0:
                parts = frac[block]
                for k in range(upw):
                    inflow = inflow + parts[k : k + 1, :] * pool[numbers[slots_at + block * upw + k]]
            mixed = jnp.dot(
                kin[block], inflow, precision=lax.Precision.HIGHEST, preferred_element_type=jnp.float32
            )
            solved.append(weight[pl.ds(block, 1), :] * mixed)
        for block, value in zip(ids, solved):
            pool[block] = value
        return carry

    lax.fori_loop(0, (count + GROUP - 1) // GROUP, solve_group, 0)

    if level < rounds:
        for j in range(groups):
            last[section * groups + j] = pool[numbers[peers_at + level * groups + j]]
            last[below * groups + j] = pool[numbers[downs_at + level * groups + j]]
    else:
        last[...] = pool[pl.ds(0, blocks)]


def shards(
    residual, kin_inverse, cell_weight, upwind_frac, block_level, send_in, send_down, upwind_slot
):
    blocks, species, cells = residual.shape
    sections, groups = lax.axis_size("section"), lax.axis_size("blk")
    rounds = send_in.shape[1]
    upw = upwind_slot.shape[1]
    numbers = jnp.concatenate(
        [block_level, upwind_slot.reshape(-1), send_in.reshape(-1), send_down.reshape(-1), lax.axis_index("section")[None]]
    )
    slots = blocks + 1 + 2 * rounds * groups
    smem = pl.BlockSpec(memory_space=pltpu.SMEM)
    vmem = pl.BlockSpec(memory_space=pltpu.VMEM)
    pool = None
    for level in range(rounds + 1):
        operands = [numbers, residual, kin_inverse, cell_weight, upwind_frac]
        aliases = {}
        if level > 0:
            aliases = {6: 0}
            operands += [arrived, pool]
        if level < rounds:
            last = jax.ShapeDtypeStruct((sections * groups, species, cells), jnp.float32)
        else:
            last = jax.ShapeDtypeStruct((blocks, species, cells), jnp.float32)
        pool, out = pl.pallas_call(
            functools.partial(solve_level, level, blocks, upw, rounds, sections, groups),
            in_specs=[smem] + [vmem] * (len(operands) - 1),
            out_specs=[vmem, vmem],
            out_shape=[jax.ShapeDtypeStruct((slots, species, cells), jnp.float32), last],
            scratch_shapes=[pltpu.SMEM((blocks + 1,), jnp.int32)],
            input_output_aliases=aliases,
            compiler_params=pltpu.CompilerParams(vmem_limit_bytes=40 * 1024 * 1024),
            name="solve_level",
        )(*operands)
        if level < rounds:
            arrived = lax.all_to_all(out, ("section", "blk"), split_axis=0, concat_axis=0, tiled=True)
    return out


def solution(mesh):
    return jax.shard_map(
        shards,
        mesh=mesh,
        in_specs=(
            P(("section", "blk"), None, None),
            P(("section", "blk"), None, None),
            P(("section", "blk"), None),
            P(("section", "blk"), None, None),
            P(("section", "blk")),
            P(("section", "blk"), None, None),
            P(("section", "blk"), None, None),
            P(("section", "blk"), None),
        ),
        out_specs=P(("section", "blk"), None, None),
        check_vma=False,
    )
```

```python
import functools

import jax
import jax.numpy as jnp
from jax import lax
from jax.experimental import pallas as pl
from jax.experimental.pallas import tpu as pltpu
from jax.sharding import PartitionSpec as P

GROUP = 8


def passed_along(value, axis, steps):
    count = lax.axis_size(axis)
    leading, last = (max(0, -steps), min(count, count - steps))
    return lax.ppermute(value, axis, [(source, source + steps) for source in range(leading, last)])


def solve_level(level, blocks, upw, rounds, groups, *refs):
    refs = list(refs)
    numbers = refs.pop(0)
    residual, kin, weight, frac = (refs.pop(0) for _ in range(4))
    if level > 0:
        from_peers, from_above, _ = (refs.pop(0) for _ in range(3))
    pool = refs.pop(0)
    to_peers = refs.pop(0)
    to_below = refs.pop(0) if level < rounds else None
    chosen = refs.pop(0)
    slots_at = blocks
    peers_at = slots_at + blocks * upw
    downs_at = peers_at + rounds * groups

    if level == 0:
        pool[blocks] = jnp.zeros(pool.shape[1:], pool.dtype)
    else:
        first = blocks + 1 + (level - 1) * groups
        pool[pl.ds(first, groups)] = from_peers[...]
        pool[pl.ds(first + rounds * groups, groups)] = from_above[...]

    def listed(block, count):
        chosen[count] = block
        return count + jnp.where(numbers[block] == level, 1, 0)

    count = lax.fori_loop(0, blocks, listed, 0)

    def solve_group(group, carry):
        ids = [chosen[jnp.minimum(group * GROUP + i, count - 1)] for i in range(GROUP)]
        solved = []
        for block in ids:
            inflow = residual[block]
            if level > 0:
                parts = frac[block]
                for k in range(upw):
                    inflow = inflow + parts[k : k + 1, :] * pool[numbers[slots_at + block * upw + k]]
            mixed = jnp.dot(
                kin[block], inflow, precision=lax.Precision.HIGHEST, preferred_element_type=jnp.float32
            )
            solved.append(weight[pl.ds(block, 1), :] * mixed)
        for block, value in zip(ids, solved):
            pool[block] = value
        return carry

    lax.fori_loop(0, (count + GROUP - 1) // GROUP, solve_group, 0)

    if level < rounds:
        for j in range(groups):
            to_peers[j] = pool[numbers[peers_at + level * groups + j]]
            to_below[j] = pool[numbers[downs_at + level * groups + j]]
    else:
        to_peers[...] = pool[pl.ds(0, blocks)]


def shards(
    residual, kin_inverse, cell_weight, upwind_frac, block_level, send_in, send_down, upwind_slot
):
    blocks, species, cells = residual.shape
    groups = lax.axis_size("blk")
    rounds = send_in.shape[1]
    upw = upwind_slot.shape[1]
    numbers = jnp.concatenate(
        [block_level, upwind_slot.reshape(-1), send_in.reshape(-1), send_down.reshape(-1)]
    )
    slots = blocks + 1 + 2 * rounds * groups
    smem = pl.BlockSpec(memory_space=pltpu.SMEM)
    vmem = pl.BlockSpec(memory_space=pltpu.VMEM)
    pool = None
    for level in range(rounds + 1):
        operands = [numbers, residual, kin_inverse, cell_weight, upwind_frac]
        aliases = {}
        if level > 0:
            aliases = {7: 0}
            operands += [from_peers, from_above, pool]
        if level < rounds:
            outs = [jax.ShapeDtypeStruct((groups, species, cells), jnp.float32)] * 2
        else:
            outs = [jax.ShapeDtypeStruct((blocks, species, cells), jnp.float32)]
        pool, *outs = pl.pallas_call(
            functools.partial(solve_level, level, blocks, upw, rounds, groups),
            in_specs=[smem] + [vmem] * (len(operands) - 1),
            out_specs=[vmem] * (len(outs) + 1),
            out_shape=[jax.ShapeDtypeStruct((slots, species, cells), jnp.float32)] + outs,
            scratch_shapes=[pltpu.SMEM((blocks + 1,), jnp.int32)],
            input_output_aliases=aliases,
            compiler_params=pltpu.CompilerParams(vmem_limit_bytes=40 * 1024 * 1024),
            name="solve_level",
        )(*operands)
        if level < rounds:
            shifted = passed_along(outs[1], "section", 1)
            from_peers = lax.all_to_all(outs[0], "blk", split_axis=0, concat_axis=0, tiled=True)
            from_above = lax.all_to_all(shifted, "blk", split_axis=0, concat_axis=0, tiled=True)
    return outs[0]


def solution(mesh):
    return jax.shard_map(
        shards,
        mesh=mesh,
        in_specs=(
            P(("section", "blk"), None, None),
            P(("section", "blk"), None, None),
            P(("section", "blk"), None),
            P(("section", "blk"), None, None),
            P(("section", "blk")),
            P(("section", "blk"), None, None),
            P(("section", "blk"), None, None),
            P(("section", "blk"), None),
        ),
        out_specs=P(("section", "blk"), None, None),
        check_vma=False,
    )
```

```python
import functools

import jax
import jax.numpy as jnp
from jax import lax
from jax.experimental import pallas as pl
from jax.experimental.pallas import tpu as pltpu
from jax.sharding import PartitionSpec as P

GROUP = 8


def split_of(groups):
    columns = max(c for c in range(1, groups + 1) if groups % c == 0 and c * c <= groups)
    return groups // columns, columns


def moved(value, sections, rows, columns, steps):
    groups = rows * columns
    pairs = []
    for section in range(max(0, -steps[0]), min(sections, sections - steps[0])):
        for row in range(rows):
            for column in range(columns):
                target = (row + steps[1]) % rows * columns + (column + steps[2]) % columns
                pairs.append((section * groups + row * columns + column, (section + steps[0]) * groups + target))
    return lax.ppermute(value, ("section", "blk"), pairs)


def solve_level(level, blocks, upw, rounds, rows, columns, *refs):
    refs = list(refs)
    groups = rows * columns
    numbers = refs.pop(0)
    residual, kin, weight, frac = (refs.pop(0) for _ in range(4))
    if level > 0:
        arrived = [refs.pop(0) for _ in range(rows)]
        refs.pop(0)
    pool = refs.pop(0)
    outs = [refs.pop(0) for _ in range(2 * columns if level < rounds else 1)]
    chosen = refs.pop(0)
    slots_at = blocks
    peers_at = slots_at + blocks * upw
    downs_at = peers_at + rounds * groups
    row = numbers[downs_at + rounds * groups]
    column = numbers[downs_at + rounds * groups + 1]

    def wrapped(value, count):
        return jnp.where(value >= count, value - count, value)

    if level == 0:
        pool[blocks] = jnp.zeros(pool.shape[1:], pool.dtype)
    else:
        peers_first = blocks + 1 + (level - 1) * groups
        downs_first = peers_first + rounds * groups
        for row_step in range(rows):
            from_row = wrapped(row + rows - row_step, rows)
            for column_step in range(columns):
                source = from_row * columns + wrapped(column + columns - column_step, columns)
                pool[peers_first + source] = arrived[row_step][column_step]
                pool[downs_first + source] = arrived[row_step][columns + column_step]

    def listed(block, count):
        chosen[count] = block
        return count + jnp.where(numbers[block] == level, 1, 0)

    count = lax.fori_loop(0, blocks, listed, 0)

    def solve_group(group, carry):
        ids = [chosen[jnp.minimum(group * GROUP + i, count - 1)] for i in range(GROUP)]
        solved = []
        for block in ids:
            inflow = residual[block]
            if level > 0:
                parts = frac[block]
                for k in range(upw):
                    inflow = inflow + parts[k : k + 1, :] * pool[numbers[slots_at + block * upw + k]]
            mixed = jnp.dot(
                kin[block], inflow, precision=lax.Precision.HIGHEST, preferred_element_type=jnp.float32
            )
            solved.append(weight[pl.ds(block, 1), :] * mixed)
        for block, value in zip(ids, solved):
            pool[block] = value
        return carry

    lax.fori_loop(0, (count + GROUP - 1) // GROUP, solve_group, 0)

    if level < rounds:
        for row_step in range(rows):
            to_row = wrapped(row + row_step, rows)
            for column_step in range(columns):
                target = to_row * columns + wrapped(column + column_step, columns)
                outs[column_step][row_step] = pool[numbers[peers_at + level * groups + target]]
                outs[columns + column_step][row_step] = pool[numbers[downs_at + level * groups + target]]
    else:
        outs[0][...] = pool[pl.ds(0, blocks)]


def shards(
    residual, kin_inverse, cell_weight, upwind_frac, block_level, send_in, send_down, upwind_slot
):
    blocks, species, cells = residual.shape
    sections, groups = lax.axis_size("section"), lax.axis_size("blk")
    rows, columns = split_of(groups)
    rounds = send_in.shape[1]
    upw = upwind_slot.shape[1]
    here = lax.axis_index("blk")
    numbers = jnp.concatenate(
        [
            block_level,
            upwind_slot.reshape(-1),
            send_in.reshape(-1),
            send_down.reshape(-1),
            jnp.stack([here // columns, here % columns]),
        ]
    )
    slots = blocks + 1 + 2 * rounds * groups
    smem = pl.BlockSpec(memory_space=pltpu.SMEM)
    vmem = pl.BlockSpec(memory_space=pltpu.VMEM)
    pool = None
    arrived = []
    for level in range(rounds + 1):
        operands = [numbers, residual, kin_inverse, cell_weight, upwind_frac]
        aliases = {}
        if level > 0:
            operands += arrived + [pool]
            aliases = {len(operands) - 1: 0}
        if level < rounds:
            outs = [jax.ShapeDtypeStruct((rows, species, cells), jnp.float32)] * (2 * columns)
        else:
            outs = [jax.ShapeDtypeStruct((blocks, species, cells), jnp.float32)]
        pool, *outs = pl.pallas_call(
            functools.partial(solve_level, level, blocks, upw, rounds, rows, columns),
            in_specs=[smem] + [vmem] * (len(operands) - 1),
            out_specs=[vmem] * (len(outs) + 1),
            out_shape=[jax.ShapeDtypeStruct((slots, species, cells), jnp.float32)] + outs,
            scratch_shapes=[pltpu.SMEM((blocks + 1,), jnp.int32)],
            input_output_aliases=aliases,
            compiler_params=pltpu.CompilerParams(vmem_limit_bytes=40 * 1024 * 1024),
            name="solve_level",
        )(*operands)
        if level < rounds:
            turned = [outs[0]]
            turned += [moved(outs[c], sections, rows, columns, (0, 0, c)) for c in range(1, columns)]
            turned += [moved(outs[columns + c], sections, rows, columns, (1, 0, c)) for c in range(columns)]
            arrived = [jnp.stack([part[step] for part in turned]) for step in range(rows)]
            arrived = arrived[:1] + [
                moved(arrived[step], sections, rows, columns, (0, step, 0)) for step in range(1, rows)
            ]
    return outs[0]


def solution(mesh):
    return jax.shard_map(
        shards,
        mesh=mesh,
        in_specs=(
            P(("section", "blk"), None, None),
            P(("section", "blk"), None, None),
            P(("section", "blk"), None),
            P(("section", "blk"), None, None),
            P(("section", "blk")),
            P(("section", "blk"), None, None),
            P(("section", "blk"), None, None),
            P(("section", "blk"), None),
        ),
        out_specs=P(("section", "blk"), None, None),
        check_vma=False,
    )
```

```python
import functools

import jax
import jax.numpy as jnp
from jax import lax
from jax.experimental import pallas as pl
from jax.experimental.pallas import tpu as pltpu
from jax.sharding import PartitionSpec as P

GROUP = 8


def split_of(groups):
    columns = max(c for c in range(1, groups + 1) if groups % c == 0 and c * c <= groups)
    return groups // columns, columns


def moved(value, sections, rows, columns, steps):
    groups = rows * columns
    pairs = []
    for section in range(sections):
        for row in range(rows):
            for column in range(columns):
                target = (row + steps[1]) % rows * columns + (column + steps[2]) % columns
                below = (section + steps[0]) % sections
                pairs.append((section * groups + row * columns + column, below * groups + target))
    return lax.ppermute(value, ("section", "blk"), pairs)


def wrapped(value, count):
    return jnp.where(value >= count, value - count, value)


def list_level(level, blocks, levels, chosen):
    def listed(block, count):
        chosen[count] = block
        return count + jnp.where(levels[block] == level, 1, 0)

    return lax.fori_loop(0, blocks, listed, 0)


def solve_group(group, count, chosen, inflow_of, kin, weight, pool):
    ids = [chosen[jnp.minimum(group * GROUP + i, count - 1)] for i in range(GROUP)]
    solved = []
    for block in ids:
        mixed = jnp.dot(
            kin[block], inflow_of(block), precision=lax.Precision.HIGHEST, preferred_element_type=jnp.float32
        )
        solved.append(weight[pl.ds(block, 1), :] * mixed)
    for block, value in zip(ids, solved):
        pool[block] = value


def fill_sends(level, rows, columns, blocks, peers, downs, pool, outs):
    here = lax.axis_index("blk")
    row, column = here // columns, lax.rem(here, columns)
    ends = lax.axis_index("section") == lax.axis_size("section") - 1
    for row_step in range(rows):
        to_row = wrapped(row + row_step, rows)
        for column_step in range(columns):
            target = to_row * columns + wrapped(column + column_step, columns)
            outs[column_step][row_step] = pool[peers[level, 0, target]]
            outs[columns + column_step][row_step] = pool[jnp.where(ends, blocks, downs[level, 0, target])]


def first_level(rows, columns, *refs):
    refs = list(refs)
    sources = [refs.pop(0) for _ in range(6)]
    pool, kin = refs.pop(0), refs.pop(0)
    outs = [refs.pop(0) for _ in range(2 * columns)]
    chosen, *held, sems = refs
    levels, kin_here, residual, weight, peers, downs = held
    copies = [pltpu.make_async_copy(sources[i], held[i], sems.at[i]) for i in range(6)]
    for copy in copies:
        copy.start()
    blocks = residual.shape[0]
    pool[blocks] = jnp.zeros(pool.shape[1:], pool.dtype)
    copies[0].wait()
    count = list_level(0, blocks, levels, chosen)
    copies[1].wait()
    for i in range(kin.shape[1]):
        kin[:, i, :] = jnp.transpose(kin_here[i])
    for copy in copies[2:]:
        copy.wait()

    def group_body(group, carry):
        solve_group(group, count, chosen, lambda block: residual[block], kin, weight, pool)
        return carry

    lax.fori_loop(0, (count + GROUP - 1) // GROUP, group_body, 0)
    fill_sends(0, rows, columns, blocks, peers, downs, pool, outs)


def later_level(level, rows, columns, levels, peers, downs, slots, residual, kin, weight, frac, *refs):
    refs = list(refs)
    arrived = [refs.pop(0) for _ in range(rows)]
    refs.pop(0)
    pool = refs.pop(0)
    *outs, chosen = refs
    blocks, upw = residual.shape[0], slots.shape[0]
    rounds, groups = peers.shape[0], rows * columns
    here = lax.axis_index("blk")
    row, column = here // columns, lax.rem(here, columns)
    peers_first = blocks + 1 + (level - 1) * groups
    downs_first = peers_first + rounds * groups
    for row_step in range(rows):
        from_row = wrapped(row + rows - row_step, rows)
        for column_step in range(columns):
            source = from_row * columns + wrapped(column + columns - column_step, columns)
            pool[peers_first + source] = arrived[row_step][column_step]
            pool[downs_first + source] = arrived[row_step][columns + column_step]
    count = list_level(level, blocks, levels, chosen)

    def inflow_of(block):
        inflow = residual[block]
        parts = frac[block]
        for k in range(upw):
            inflow = inflow + parts[k : k + 1, :] * pool[slots[k, block]]
        return inflow

    def group_body(group, carry):
        solve_group(group, count, chosen, inflow_of, kin, weight, pool)
        return carry

    lax.fori_loop(0, (count + GROUP - 1) // GROUP, group_body, 0)
    if level < rounds:
        fill_sends(level, rows, columns, blocks, peers, downs, pool, outs)
    else:
        outs[0][...] = pool[pl.ds(0, blocks)]


def shards(
    residual, kin_inverse, cell_weight, upwind_frac, block_level, send_in, send_down, upwind_slot
):
    blocks, species, cells = residual.shape
    sections, groups = lax.axis_size("section"), lax.axis_size("blk")
    rows, columns = split_of(groups)
    rounds = send_in.shape[1]
    peers = send_in.transpose(1, 0, 2)
    downs = send_down.transpose(1, 0, 2)
    slots = upwind_slot.transpose(1, 0)
    kin_turned = kin_inverse.transpose(1, 2, 0)
    smem = pl.BlockSpec(memory_space=pltpu.SMEM)
    vmem = pl.BlockSpec(memory_space=pltpu.VMEM)
    hbm = pl.BlockSpec(memory_space=pltpu.HBM)
    params = pltpu.CompilerParams(vmem_limit_bytes=40 * 1024 * 1024)
    pool_shape = jax.ShapeDtypeStruct((blocks + 1 + 2 * rounds * groups, species, cells), jnp.float32)
    kin_shape = jax.ShapeDtypeStruct((blocks, species, species), jnp.float32)
    send_shapes = [jax.ShapeDtypeStruct((rows, species, cells), jnp.float32)] * (2 * columns)
    chosen = pltpu.SMEM((blocks + 1,), jnp.int32)
    to_first = (block_level, kin_turned, residual, cell_weight, peers, downs)
    pool, kin, *outs = pl.pallas_call(
        functools.partial(first_level, rows, columns),
        in_specs=[hbm] * 6,
        out_specs=[vmem] * (2 + 2 * columns),
        out_shape=[pool_shape, kin_shape] + send_shapes,
        scratch_shapes=[
            chosen,
            pltpu.SMEM(block_level.shape, jnp.int32),
            pltpu.VMEM(kin_turned.shape, jnp.float32),
            pltpu.VMEM(residual.shape, jnp.float32),
            pltpu.VMEM(cell_weight.shape, jnp.float32),
            pltpu.SMEM(peers.shape, jnp.int32),
            pltpu.SMEM(downs.shape, jnp.int32),
            pltpu.SemaphoreType.DMA((6,)),
        ],
        compiler_params=params,
        name="first_level",
    )(*(pltpu.with_memory_space_constraint(x, pltpu.HBM) for x in to_first))
    for level in range(1, rounds + 1):
        turned = [moved(outs[columns + c], sections, rows, columns, (1, 0, c)) for c in range(columns)]
        turned = [moved(outs[c], sections, rows, columns, (0, 0, c)) for c in range(1, columns)] + turned
        turned = [outs[0]] + turned
        arrived = [jnp.stack([part[step] for part in turned]) for step in range(rows)]
        arrived = arrived[:1] + [
            moved(arrived[step], sections, rows, columns, (0, step, 0)) for step in range(1, rows)
        ]
        if level < rounds:
            out_shapes = send_shapes
        else:
            out_shapes = [jax.ShapeDtypeStruct(residual.shape, jnp.float32)]
        operands = [block_level, peers, downs, slots, residual, kin, cell_weight, upwind_frac] + arrived + [pool]
        pool, *outs = pl.pallas_call(
            functools.partial(later_level, level, rows, columns),
            in_specs=[smem] * 4 + [vmem] * (len(operands) - 4),
            out_specs=[vmem] * (1 + len(out_shapes)),
            out_shape=[pool_shape] + out_shapes,
            scratch_shapes=[chosen],
            input_output_aliases={len(operands) - 1: 0},
            compiler_params=params,
            name="later_level",
        )(*operands)
    return outs[0]


def solution(mesh):
    return jax.shard_map(
        shards,
        mesh=mesh,
        in_specs=(
            P(("section", "blk"), None, None),
            P(("section", "blk"), None, None),
            P(("section", "blk"), None),
            P(("section", "blk"), None, None),
            P(("section", "blk")),
            P(("section", "blk"), None, None),
            P(("section", "blk"), None, None),
            P(("section", "blk"), None),
        ),
        out_specs=P(("section", "blk"), None, None),
        check_vma=False,
    )
```

```python
import functools

import jax
import jax.numpy as jnp
from jax import lax
from jax.experimental import pallas as pl
from jax.experimental.pallas import tpu as pltpu
from jax.sharding import PartitionSpec as P

GROUP = 8


def split_of(groups):
    columns = max(c for c in range(1, groups + 1) if groups % c == 0 and c * c <= groups)
    return groups // columns, columns


def moved(value, sections, rows, columns, steps):
    groups = rows * columns
    pairs = []
    for section in range(sections):
        for row in range(rows):
            for column in range(columns):
                target = (row + steps[1]) % rows * columns + (column + steps[2]) % columns
                below = (section + steps[0]) % sections
                pairs.append((section * groups + row * columns + column, below * groups + target))
    return lax.ppermute(value, ("section", "blk"), pairs)


def row_steps(rows):
    return sorted(range(1, rows), key=lambda step: -min(step, rows - step))


def wrapped(value, count):
    return jnp.where(value >= count, value - count, value)


def list_level(level, blocks, levels, chosen):
    def listed(block, count):
        chosen[count] = block
        return count + jnp.where(levels[block] == level, 1, 0)

    return lax.fori_loop(0, blocks, listed, 0)


def solve_group(group, count, chosen, inflow_of, kin, weight, pool):
    ids = [chosen[jnp.minimum(group * GROUP + i, count - 1)] for i in range(GROUP)]
    solved = []
    for block in ids:
        mixed = jnp.dot(
            kin[block], inflow_of(block), precision=lax.Precision.HIGHEST, preferred_element_type=jnp.float32
        )
        solved.append(weight[pl.ds(block, 1), :] * mixed)
    for block, value in zip(ids, solved):
        pool[block] = value


def fill_sends(level, rows, columns, blocks, peers, downs, pool, outs):
    here = lax.axis_index("blk")
    row, column = here // columns, lax.rem(here, columns)
    ends = lax.axis_index("section") == lax.axis_size("section") - 1
    for row_step in range(rows):
        to_row = wrapped(row + row_step, rows)
        for column_step in range(columns):
            target = to_row * columns + wrapped(column + column_step, columns)
            outs[columns + row_step][column_step] = pool[peers[level, 0, target]]
            outs[column_step][row_step] = pool[jnp.where(ends, blocks, downs[level, 0, target])]


def first_level(rows, columns, *refs):
    refs = list(refs)
    levels_in, kin_in, residual_in, weight_in, peers_in, downs_in, slots_in, frac_in = (refs.pop(0) for _ in range(8))
    pool, kin, levels_out, peers_out, downs_out, slots_out, residual, weight, frac = (refs.pop(0) for _ in range(9))
    outs = [refs.pop(0) for _ in range(rows + columns)]
    chosen, levels, kin_here, peers, downs, sems = refs
    pairs = [(levels_in, levels), (kin_in, kin_here), (residual_in, residual), (weight_in, weight)]
    pairs += [(peers_in, peers), (downs_in, downs)]
    pairs += [(levels_in, levels_out), (peers_in, peers_out), (downs_in, downs_out)]
    pairs += [(slots_in, slots_out), (frac_in, frac)]
    copies = [pltpu.make_async_copy(source, target, sems.at[i]) for i, (source, target) in enumerate(pairs)]
    for copy in copies:
        copy.start()
    blocks = residual.shape[0]
    pool[blocks] = jnp.zeros(pool.shape[1:], pool.dtype)
    copies[0].wait()
    count = list_level(0, blocks, levels, chosen)
    copies[1].wait()
    for i in range(kin.shape[1]):
        kin[:, i, :] = jnp.transpose(kin_here[i])
    for copy in copies[2:6]:
        copy.wait()

    def group_body(group, carry):
        solve_group(group, count, chosen, lambda block: residual[block], kin, weight, pool)
        return carry

    lax.fori_loop(0, (count + GROUP - 1) // GROUP, group_body, 0)
    fill_sends(0, rows, columns, blocks, peers, downs, pool, outs)
    for copy in copies[6:]:
        copy.wait()


def later_level(level, rows, columns, levels, peers, downs, slots, residual, weight, frac, kin, *refs):
    refs = list(refs)
    down_columns = [refs.pop(0) for _ in range(columns)]
    over_rows = [refs.pop(0) for _ in range(rows)]
    over_rows = dict(zip([0] + row_steps(rows), over_rows))
    down_rows = {step: refs.pop(0) for step in row_steps(rows)}
    over_columns = [None] + [refs.pop(0) for _ in range(1, columns)]
    refs.pop(0)
    pool = refs.pop(0)
    *outs, chosen = refs
    blocks, upw = residual.shape[0], slots.shape[0]
    rounds, groups = peers.shape[0], rows * columns
    here = lax.axis_index("blk")
    row, column = here // columns, lax.rem(here, columns)
    peers_first = blocks + 1 + (level - 1) * groups
    downs_first = peers_first + rounds * groups
    for row_step in range(rows):
        from_row = wrapped(row + rows - row_step, rows)
        for column_step in range(columns):
            source = from_row * columns + wrapped(column + columns - column_step, columns)
            peer = over_columns[column_step].at[row_step] if column_step else over_rows[row_step].at[0]
            down = down_rows[row_step].at[column_step] if row_step else down_columns[column_step].at[0]
            pool[peers_first + source] = peer[...]
            pool[downs_first + source] = down[...]
    count = list_level(level, blocks, levels, chosen)

    def inflow_of(block):
        inflow = residual[block]
        parts = frac[block]
        for k in range(upw):
            inflow = inflow + parts[k : k + 1, :] * pool[slots[k, block]]
        return inflow

    def group_body(group, carry):
        solve_group(group, count, chosen, inflow_of, kin, weight, pool)
        return carry

    lax.fori_loop(0, (count + GROUP - 1) // GROUP, group_body, 0)
    if level < rounds:
        fill_sends(level, rows, columns, blocks, peers, downs, pool, outs)
    else:
        outs[0][...] = pool[pl.ds(0, blocks)]


def shards(
    residual, kin_inverse, cell_weight, upwind_frac, block_level, send_in, send_down, upwind_slot
):
    blocks, species, cells = residual.shape
    sections, groups = lax.axis_size("section"), lax.axis_size("blk")
    rows, columns = split_of(groups)
    rounds = send_in.shape[1]
    peers = send_in.transpose(1, 0, 2)
    downs = send_down.transpose(1, 0, 2)
    slots = upwind_slot.transpose(1, 0)
    kin_turned = kin_inverse.transpose(1, 2, 0)
    smem = pl.BlockSpec(memory_space=pltpu.SMEM)
    vmem = pl.BlockSpec(memory_space=pltpu.VMEM)
    hbm = pl.BlockSpec(memory_space=pltpu.HBM)
    params = pltpu.CompilerParams(vmem_limit_bytes=40 * 1024 * 1024)
    pool_shape = jax.ShapeDtypeStruct((blocks + 1 + 2 * rounds * groups, species, cells), jnp.float32)
    kin_shape = jax.ShapeDtypeStruct((blocks, species, species), jnp.float32)
    send_shapes = [jax.ShapeDtypeStruct((rows, species, cells), jnp.float32)] * columns
    send_shapes += [jax.ShapeDtypeStruct((columns, species, cells), jnp.float32)] * rows
    chosen = pltpu.SMEM((blocks + 1,), jnp.int32)
    to_first = (block_level, kin_turned, residual, cell_weight, peers, downs, slots, upwind_frac)
    held = (block_level, peers, downs, slots, residual, cell_weight, upwind_frac)
    held_shapes = [jax.ShapeDtypeStruct(x.shape, x.dtype) for x in held]
    pool, kin, *outs = pl.pallas_call(
        functools.partial(first_level, rows, columns),
        in_specs=[hbm] * len(to_first),
        out_specs=[vmem] * (2 + len(held) + rows + columns),
        out_shape=[pool_shape, kin_shape] + held_shapes + send_shapes,
        scratch_shapes=[
            chosen,
            pltpu.SMEM(block_level.shape, jnp.int32),
            pltpu.VMEM(kin_turned.shape, jnp.float32),
            pltpu.SMEM(peers.shape, jnp.int32),
            pltpu.SMEM(downs.shape, jnp.int32),
            pltpu.SemaphoreType.DMA((11,)),
        ],
        compiler_params=params,
        name="first_level",
    )(*(pltpu.with_memory_space_constraint(x, pltpu.HBM) for x in to_first))
    held, outs = outs[: len(held)], outs[len(held) :]
    for level in range(1, rounds + 1):
        down_columns = [moved(outs[c], sections, rows, columns, (1, 0, c)) for c in range(columns)]
        over_rows = {0: outs[columns]}
        for step in row_steps(rows):
            over_rows[step] = moved(outs[columns + step], sections, rows, columns, (0, step, 0))
        down_rows = []
        for step in row_steps(rows):
            part = jnp.stack([down_columns[c][step] for c in range(columns)])
            down_rows.append(moved(part, sections, rows, columns, (0, step, 0)))
        over_columns = []
        for c in range(1, columns):
            part = jnp.stack([over_rows[step][c] for step in range(rows)])
            part, down_rows[0] = lax.optimization_barrier((part, down_rows[0]))
            over_columns.append(moved(part, sections, rows, columns, (0, 0, c)))
        arrived = down_columns + list(over_rows.values()) + down_rows + over_columns
        if level < rounds:
            out_shapes = send_shapes
        else:
            out_shapes = [jax.ShapeDtypeStruct(residual.shape, residual.dtype)]
        operands = held + [kin] + arrived + [pool]
        pool, *outs = pl.pallas_call(
            functools.partial(later_level, level, rows, columns),
            in_specs=[smem] * 4 + [vmem] * (len(operands) - 4),
            out_specs=[vmem] * (1 + len(out_shapes)),
            out_shape=[pool_shape] + out_shapes,
            scratch_shapes=[chosen],
            input_output_aliases={len(operands) - 1: 0},
            compiler_params=params,
            name="later_level",
        )(*operands)
    return outs[0]


def solution(mesh):
    return jax.shard_map(
        shards,
        mesh=mesh,
        in_specs=(
            P(("section", "blk"), None, None),
            P(("section", "blk"), None, None),
            P(("section", "blk"), None),
            P(("section", "blk"), None, None),
            P(("section", "blk")),
            P(("section", "blk"), None, None),
            P(("section", "blk"), None, None),
            P(("section", "blk"), None),
        ),
        out_specs=P(("section", "blk"), None, None),
        check_vma=False,
    )
```

```python
import functools

import jax
import jax.numpy as jnp
from jax import lax
from jax.experimental import pallas as pl
from jax.experimental.pallas import tpu as pltpu
from jax.sharding import PartitionSpec as P

GROUP = 8


def split_of(groups):
    columns = max(c for c in range(1, groups + 1) if groups % c == 0 and c * c <= groups)
    return groups // columns, columns


def moved(value, sections, rows, columns, steps):
    groups = rows * columns
    pairs = []
    for section in range(sections):
        for row in range(rows):
            for column in range(columns):
                target = (row + steps[1]) % rows * columns + (column + steps[2]) % columns
                below = (section + steps[0]) % sections
                pairs.append((section * groups + row * columns + column, below * groups + target))
    return lax.ppermute(value, ("section", "blk"), pairs)


def wrapped(value, count):
    return jnp.where(value >= count, value - count, value)


def list_level(level, blocks, levels, chosen):
    def listed(block, count):
        chosen[count] = block
        return count + jnp.where(levels[block] == level, 1, 0)

    return lax.fori_loop(0, blocks, listed, 0)


def solve_group(group, count, chosen, inflow_of, kin, weight, pool):
    ids = [chosen[jnp.minimum(group * GROUP + i, count - 1)] for i in range(GROUP)]
    solved = []
    for block in ids:
        mixed = jnp.dot(
            kin[block], inflow_of(block), precision=lax.Precision.HIGHEST, preferred_element_type=jnp.float32
        )
        solved.append(weight[pl.ds(block, 1), :] * mixed)
    for block, value in zip(ids, solved):
        pool[block] = value


def fill_sends(level, rows, columns, blocks, peers, downs, pool, outs):
    column = lax.rem(lax.axis_index("blk"), columns)
    ends = lax.axis_index("section") == lax.axis_size("section") - 1
    for row in range(rows):
        for column_step in range(columns):
            target = row * columns + wrapped(column + column_step, columns)
            outs[column_step][row] = pool[peers[level, 0, target]]
            outs[columns + column_step][row] = pool[jnp.where(ends, blocks, downs[level, 0, target])]


def first_level(rows, columns, *refs):
    refs = list(refs)
    levels_in, kin_in, residual_in, weight_in, peers_in, downs_in, slots_in, frac_in = (refs.pop(0) for _ in range(8))
    pool, kin, levels_out, peers_out, downs_out, slots_out, residual, weight, frac = (refs.pop(0) for _ in range(9))
    outs = [refs.pop(0) for _ in range(2 * columns)]
    chosen, levels, kin_here, peers, downs, sems = refs
    pairs = [(levels_in, levels), (kin_in, kin_here), (residual_in, residual), (weight_in, weight)]
    pairs += [(peers_in, peers), (downs_in, downs)]
    pairs += [(levels_in, levels_out), (peers_in, peers_out), (downs_in, downs_out)]
    pairs += [(slots_in, slots_out), (frac_in, frac)]
    copies = [pltpu.make_async_copy(source, target, sems.at[i]) for i, (source, target) in enumerate(pairs)]
    for copy in copies:
        copy.start()
    blocks = residual.shape[0]
    pool[blocks] = jnp.zeros(pool.shape[1:], pool.dtype)
    copies[0].wait()
    count = list_level(0, blocks, levels, chosen)
    copies[1].wait()
    for i in range(kin.shape[1]):
        kin[:, i, :] = jnp.transpose(kin_here[i])
    for copy in copies[2:6]:
        copy.wait()

    def group_body(group, carry):
        solve_group(group, count, chosen, lambda block: residual[block], kin, weight, pool)
        return carry

    lax.fori_loop(0, (count + GROUP - 1) // GROUP, group_body, 0)
    fill_sends(0, rows, columns, blocks, peers, downs, pool, outs)
    for copy in copies[6:]:
        copy.wait()


def later_level(level, rows, columns, levels, peers, downs, slots, residual, weight, frac, kin, *refs):
    refs = list(refs)
    arrived, _ = (refs.pop(0) for _ in range(2))
    pool = refs.pop(0)
    *outs, chosen = refs
    blocks, upw = residual.shape[0], slots.shape[0]
    rounds, groups = peers.shape[0], rows * columns
    column = lax.rem(lax.axis_index("blk"), columns)
    peers_first = blocks + 1 + (level - 1) * groups
    downs_first = peers_first + rounds * groups
    for row in range(rows):
        for column_step in range(columns):
            source = row * columns + wrapped(column + columns - column_step, columns)
            pool[peers_first + source] = arrived[row, column_step]
            pool[downs_first + source] = arrived[row, columns + column_step]
    count = list_level(level, blocks, levels, chosen)

    def inflow_of(block):
        inflow = residual[block]
        parts = frac[block]
        for k in range(upw):
            inflow = inflow + parts[k : k + 1, :] * pool[slots[k, block]]
        return inflow

    def group_body(group, carry):
        solve_group(group, count, chosen, inflow_of, kin, weight, pool)
        return carry

    lax.fori_loop(0, (count + GROUP - 1) // GROUP, group_body, 0)
    if level < rounds:
        fill_sends(level, rows, columns, blocks, peers, downs, pool, outs)
    else:
        outs[0][...] = pool[pl.ds(0, blocks)]


def shards(
    residual, kin_inverse, cell_weight, upwind_frac, block_level, send_in, send_down, upwind_slot
):
    blocks, species, cells = residual.shape
    sections, groups = lax.axis_size("section"), lax.axis_size("blk")
    rows, columns = split_of(groups)
    rounds = send_in.shape[1]
    peers = send_in.transpose(1, 0, 2)
    downs = send_down.transpose(1, 0, 2)
    slots = upwind_slot.transpose(1, 0)
    kin_turned = kin_inverse.transpose(1, 2, 0)
    smem = pl.BlockSpec(memory_space=pltpu.SMEM)
    vmem = pl.BlockSpec(memory_space=pltpu.VMEM)
    hbm = pl.BlockSpec(memory_space=pltpu.HBM)
    params = pltpu.CompilerParams(vmem_limit_bytes=40 * 1024 * 1024)
    pool_shape = jax.ShapeDtypeStruct((blocks + 1 + 2 * rounds * groups, species, cells), jnp.float32)
    kin_shape = jax.ShapeDtypeStruct((blocks, species, species), jnp.float32)
    send_shapes = [jax.ShapeDtypeStruct((rows, species, cells), jnp.float32)] * (2 * columns)
    chosen = pltpu.SMEM((blocks + 1,), jnp.int32)
    to_first = (block_level, kin_turned, residual, cell_weight, peers, downs, slots, upwind_frac)
    held = (block_level, peers, downs, slots, residual, cell_weight, upwind_frac)
    held_shapes = [jax.ShapeDtypeStruct(x.shape, x.dtype) for x in held]
    pool, kin, *outs = pl.pallas_call(
        functools.partial(first_level, rows, columns),
        in_specs=[hbm] * len(to_first),
        out_specs=[vmem] * (2 + len(held) + len(send_shapes)),
        out_shape=[pool_shape, kin_shape] + held_shapes + send_shapes,
        scratch_shapes=[
            chosen,
            pltpu.SMEM(block_level.shape, jnp.int32),
            pltpu.VMEM(kin_turned.shape, jnp.float32),
            pltpu.SMEM(peers.shape, jnp.int32),
            pltpu.SMEM(downs.shape, jnp.int32),
            pltpu.SemaphoreType.DMA((11,)),
        ],
        compiler_params=params,
        name="first_level",
    )(*(pltpu.with_memory_space_constraint(x, pltpu.HBM) for x in to_first))
    held, outs = outs[: len(held)], outs[len(held) :]
    for level in range(1, rounds + 1):
        turned = [moved(outs[columns + c], sections, rows, columns, (1, 0, c)) for c in range(columns)]
        turned = [moved(outs[c], sections, rows, columns, (0, 0, c)) for c in range(1, columns)] + turned
        turned = jnp.stack([outs[0]] + turned, axis=1)
        same_column = [[row * columns + c for row in range(rows)] for c in range(columns)]
        arrived = lax.all_to_all(
            turned, "blk", split_axis=0, concat_axis=0, axis_index_groups=same_column, tiled=True
        )
        if level < rounds:
            out_shapes = send_shapes
        else:
            out_shapes = [jax.ShapeDtypeStruct(residual.shape, residual.dtype)]
        operands = held + [kin, arrived, pool]
        pool, *outs = pl.pallas_call(
            functools.partial(later_level, level, rows, columns),
            in_specs=[smem] * 4 + [vmem] * (len(operands) - 4),
            out_specs=[vmem] * (1 + len(out_shapes)),
            out_shape=[pool_shape] + out_shapes,
            scratch_shapes=[chosen],
            input_output_aliases={len(operands) - 1: 0},
            compiler_params=params,
            name="later_level",
        )(*operands)
    return outs[0]


def solution(mesh):
    return jax.shard_map(
        shards,
        mesh=mesh,
        in_specs=(
            P(("section", "blk"), None, None),
            P(("section", "blk"), None, None),
            P(("section", "blk"), None),
            P(("section", "blk"), None, None),
            P(("section", "blk")),
            P(("section", "blk"), None, None),
            P(("section", "blk"), None, None),
            P(("section", "blk"), None),
        ),
        out_specs=P(("section", "blk"), None, None),
        check_vma=False,
    )
```

```python
import functools

import jax
import jax.numpy as jnp
from jax import lax
from jax.experimental import pallas as pl
from jax.experimental.pallas import tpu as pltpu
from jax.sharding import PartitionSpec as P

GROUP = 8


def split_of(groups):
    columns = max(c for c in range(1, groups + 1) if groups % c == 0 and c * c <= groups)
    return groups // columns, columns


def stepped(row, step, rows, back=False):
    if rows & (rows - 1) == 0:
        return row ^ step
    return (row + (rows - step if back else step)) % rows


def moved(value, sections, rows, columns, steps):
    groups = rows * columns
    pairs = []
    for section in range(sections):
        for row in range(rows):
            for column in range(columns):
                target = stepped(row, steps[1], rows) * columns + (column + steps[2]) % columns
                below = (section + steps[0]) % sections
                pairs.append((section * groups + row * columns + column, below * groups + target))
    return lax.ppermute(value, ("section", "blk"), pairs)


def row_order(rows):
    return sorted(range(rows), reverse=True)


def wrapped(value, count):
    return jnp.where(value >= count, value - count, value)


def list_level(level, blocks, levels, chosen):
    def listed(block, count):
        chosen[count] = block
        return count + jnp.where(levels[block] == level, 1, 0)

    return lax.fori_loop(0, blocks, listed, 0)


def solve_group(group, count, chosen, inflow_of, kin, weight, pool):
    ids = [chosen[jnp.minimum(group * GROUP + i, count - 1)] for i in range(GROUP)]
    solved = []
    for block in ids:
        mixed = jnp.dot(
            kin[block], inflow_of(block), precision=lax.Precision.HIGHEST, preferred_element_type=jnp.float32
        )
        solved.append(weight[pl.ds(block, 1), :] * mixed)
    for block, value in zip(ids, solved):
        pool[block] = value


def fill_sends(level, rows, columns, blocks, peers, downs, pool, outs):
    here = lax.axis_index("blk")
    row, column = here // columns, lax.rem(here, columns)
    ends = lax.axis_index("section") == lax.axis_size("section") - 1
    for row_step in range(rows):
        to_row = stepped(row, row_step, rows)
        for column_step in range(columns):
            target = to_row * columns + wrapped(column + column_step, columns)
            outs[column_step][row_step] = pool[jnp.where(ends, blocks, downs[level, 0, target])]
            outs[columns + column_step][row_step] = pool[peers[level, 0, target]]


def first_level(rows, columns, *refs):
    refs = list(refs)
    levels_in, kin_in, residual_in, weight_in, peers_in, downs_in, slots_in, frac_in = (refs.pop(0) for _ in range(8))
    pool, kin, levels_out, peers_out, downs_out, slots_out, residual, weight, frac = (refs.pop(0) for _ in range(9))
    outs = [refs.pop(0) for _ in range(2 * columns)]
    chosen, levels, kin_here, peers, downs, sems = refs
    pairs = [(levels_in, levels), (kin_in, kin_here), (residual_in, residual), (weight_in, weight)]
    pairs += [(peers_in, peers), (downs_in, downs)]
    pairs += [(levels_in, levels_out), (peers_in, peers_out), (downs_in, downs_out)]
    pairs += [(slots_in, slots_out), (frac_in, frac)]
    copies = [pltpu.make_async_copy(source, target, sems.at[i]) for i, (source, target) in enumerate(pairs)]
    for copy in copies:
        copy.start()
    blocks = residual.shape[0]
    pool[blocks] = jnp.zeros(pool.shape[1:], pool.dtype)
    copies[0].wait()
    count = list_level(0, blocks, levels, chosen)
    copies[1].wait()
    for i in range(kin.shape[1]):
        kin[:, i, :] = jnp.transpose(kin_here[i])
    for copy in copies[2:6]:
        copy.wait()

    def group_body(group, carry):
        solve_group(group, count, chosen, lambda block: residual[block], kin, weight, pool)
        return carry

    lax.fori_loop(0, (count + GROUP - 1) // GROUP, group_body, 0)
    fill_sends(0, rows, columns, blocks, peers, downs, pool, outs)
    for copy in copies[6:]:
        copy.wait()


def later_level(level, rows, columns, levels, peers, downs, slots, residual, weight, frac, kin, *refs):
    refs = list(refs)
    arrived = [refs.pop(0) for _ in range(rows)]
    refs.pop(0)
    pool = refs.pop(0)
    *outs, chosen = refs
    blocks, upw = residual.shape[0], slots.shape[0]
    rounds, groups = peers.shape[0], rows * columns
    here = lax.axis_index("blk")
    row, column = here // columns, lax.rem(here, columns)
    peers_first = blocks + 1 + (level - 1) * groups
    downs_first = peers_first + rounds * groups
    for part, row_step in zip(arrived, row_order(rows)):
        from_row = stepped(row, row_step, rows, back=True)
        for column_step in range(columns):
            source = from_row * columns + wrapped(column + columns - column_step, columns)
            pool[downs_first + source] = part[column_step]
            pool[peers_first + source] = part[columns + column_step]
    count = list_level(level, blocks, levels, chosen)

    def inflow_of(block):
        inflow = residual[block]
        parts = frac[block]
        for k in range(upw):
            inflow = inflow + parts[k : k + 1, :] * pool[slots[k, block]]
        return inflow

    def group_body(group, carry):
        solve_group(group, count, chosen, inflow_of, kin, weight, pool)
        return carry

    lax.fori_loop(0, (count + GROUP - 1) // GROUP, group_body, 0)
    if level < rounds:
        fill_sends(level, rows, columns, blocks, peers, downs, pool, outs)
    else:
        outs[0][...] = pool[pl.ds(0, blocks)]


def shards(
    residual, kin_inverse, cell_weight, upwind_frac, block_level, send_in, send_down, upwind_slot
):
    blocks, species, cells = residual.shape
    sections, groups = lax.axis_size("section"), lax.axis_size("blk")
    rows, columns = split_of(groups)
    rounds = send_in.shape[1]
    peers = send_in.transpose(1, 0, 2)
    downs = send_down.transpose(1, 0, 2)
    slots = upwind_slot.transpose(1, 0)
    kin_turned = kin_inverse.transpose(1, 2, 0)
    smem = pl.BlockSpec(memory_space=pltpu.SMEM)
    vmem = pl.BlockSpec(memory_space=pltpu.VMEM)
    hbm = pl.BlockSpec(memory_space=pltpu.HBM)
    params = pltpu.CompilerParams(vmem_limit_bytes=40 * 1024 * 1024)
    pool_shape = jax.ShapeDtypeStruct((blocks + 1 + 2 * rounds * groups, species, cells), jnp.float32)
    kin_shape = jax.ShapeDtypeStruct((blocks, species, species), jnp.float32)
    send_shapes = [jax.ShapeDtypeStruct((rows, species, cells), jnp.float32)] * (2 * columns)
    chosen = pltpu.SMEM((blocks + 1,), jnp.int32)
    to_first = (block_level, kin_turned, residual, cell_weight, peers, downs, slots, upwind_frac)
    held = (block_level, peers, downs, slots, residual, cell_weight, upwind_frac)
    held_shapes = [jax.ShapeDtypeStruct(x.shape, x.dtype) for x in held]
    pool, kin, *outs = pl.pallas_call(
        functools.partial(first_level, rows, columns),
        in_specs=[hbm] * len(to_first),
        out_specs=[vmem] * (2 + len(held) + len(send_shapes)),
        out_shape=[pool_shape, kin_shape] + held_shapes + send_shapes,
        scratch_shapes=[
            chosen,
            pltpu.SMEM(block_level.shape, jnp.int32),
            pltpu.VMEM(kin_turned.shape, jnp.float32),
            pltpu.SMEM(peers.shape, jnp.int32),
            pltpu.SMEM(downs.shape, jnp.int32),
            pltpu.SemaphoreType.DMA((11,)),
        ],
        compiler_params=params,
        name="first_level",
    )(*(pltpu.with_memory_space_constraint(x, pltpu.HBM) for x in to_first))
    held, outs = outs[: len(held)], outs[len(held) :]
    for level in range(1, rounds + 1):
        turned = [moved(outs[c], sections, rows, columns, (1, 0, c)) for c in range(columns)]
        turned.append(outs[columns])
        turned += [moved(outs[columns + c], sections, rows, columns, (0, 0, c)) for c in range(1, columns)]
        arrived = []
        for step in row_order(rows):
            part = jnp.stack([value[step] for value in turned])
            arrived.append(moved(part, sections, rows, columns, (0, step, 0)) if step else part)
        if level < rounds:
            out_shapes = send_shapes
        else:
            out_shapes = [jax.ShapeDtypeStruct(residual.shape, residual.dtype)]
        operands = held + [kin] + arrived + [pool]
        pool, *outs = pl.pallas_call(
            functools.partial(later_level, level, rows, columns),
            in_specs=[smem] * 4 + [vmem] * (len(operands) - 4),
            out_specs=[vmem] * (1 + len(out_shapes)),
            out_shape=[pool_shape] + out_shapes,
            scratch_shapes=[chosen],
            input_output_aliases={len(operands) - 1: 0},
            compiler_params=params,
            name="later_level",
        )(*operands)
    return outs[0]


def solution(mesh):
    return jax.shard_map(
        shards,
        mesh=mesh,
        in_specs=(
            P(("section", "blk"), None, None),
            P(("section", "blk"), None, None),
            P(("section", "blk"), None),
            P(("section", "blk"), None, None),
            P(("section", "blk")),
            P(("section", "blk"), None, None),
            P(("section", "blk"), None, None),
            P(("section", "blk"), None),
        ),
        out_specs=P(("section", "blk"), None, None),
        check_vma=False,
    )
```

```python
import functools

import jax
import jax.numpy as jnp
from jax import lax
from jax.experimental import pallas as pl
from jax.experimental.pallas import tpu as pltpu
from jax.sharding import PartitionSpec as P

GROUP = 8


def split_of(groups):
    columns = max(c for c in range(1, groups + 1) if groups % c == 0 and c * c <= groups)
    return groups // columns, columns


def stepped(row, step, rows, back=False):
    if rows & (rows - 1) == 0:
        return row ^ step
    return (row + (rows - step if back else step)) % rows


def moved(value, sections, rows, columns, steps):
    groups = rows * columns
    pairs = []
    for section in range(sections):
        for row in range(rows):
            for column in range(columns):
                target = stepped(row, steps[1], rows) * columns + (column + steps[2]) % columns
                below = (section + steps[0]) % sections
                pairs.append((section * groups + row * columns + column, below * groups + target))
    return lax.ppermute(value, ("section", "blk"), pairs)


def halves_of(rows):
    return rows // 2 if rows > 1 and rows & (rows - 1) == 0 else rows


def last_steps(rows, columns):
    half = halves_of(rows)
    across = [(row, 0) for row in range(rows - 1, half - 1, -1)]
    aside = [(row, column) for row in range(half - 1, -1, -1) for column in range(1, columns)]
    return across + aside + [(row, 0) for row in range(half - 1, 0, -1)]


def wrapped(value, count):
    return jnp.where(value >= count, value - count, value)


def list_level(level, blocks, levels, chosen):
    def listed(block, count):
        chosen[count] = block
        return count + jnp.where(levels[block] == level, 1, 0)

    return lax.fori_loop(0, blocks, listed, 0)


def solve_group(group, count, chosen, inflow_of, kin, weight, pool):
    ids = [chosen[jnp.minimum(group * GROUP + i, count - 1)] for i in range(GROUP)]
    solved = []
    for block in ids:
        mixed = jnp.dot(
            kin[block], inflow_of(block), precision=lax.Precision.HIGHEST, preferred_element_type=jnp.float32
        )
        solved.append(weight[pl.ds(block, 1), :] * mixed)
    for block, value in zip(ids, solved):
        pool[block] = value


def fill_sends(level, rows, columns, blocks, peers, downs, pool, outs):
    here = lax.axis_index("blk")
    row, column = here // columns, lax.rem(here, columns)
    ends = lax.axis_index("section") == lax.axis_size("section") - 1
    half = halves_of(rows)
    for row_step in range(rows):
        to_row = stepped(row, row_step, rows)
        for column_step in range(columns):
            target = to_row * columns + wrapped(column + column_step, columns)
            outs[column_step][row_step] = pool[jnp.where(ends, blocks, downs[level, 0, target])]
            part = outs[columns + row_step // half]
            part[row_step % half * columns + column_step] = pool[peers[level, 0, target]]


def first_level(rows, columns, *refs):
    refs = list(refs)
    levels_in, kin_in, residual_in, weight_in, peers_in, downs_in, slots_in, frac_in = (refs.pop(0) for _ in range(8))
    pool, kin, levels_out, peers_out, downs_out, slots_out, residual, weight, frac = (refs.pop(0) for _ in range(9))
    outs = [refs.pop(0) for _ in range(columns + rows // halves_of(rows))]
    chosen, levels, kin_here, peers, downs, sems = refs
    pairs = [(levels_in, levels), (kin_in, kin_here), (residual_in, residual), (weight_in, weight)]
    pairs += [(peers_in, peers), (downs_in, downs)]
    pairs += [(levels_in, levels_out), (peers_in, peers_out), (downs_in, downs_out)]
    pairs += [(slots_in, slots_out), (frac_in, frac)]
    copies = [pltpu.make_async_copy(source, target, sems.at[i]) for i, (source, target) in enumerate(pairs)]
    for copy in copies:
        copy.start()
    blocks = residual.shape[0]
    pool[blocks] = jnp.zeros(pool.shape[1:], pool.dtype)
    copies[0].wait()
    count = list_level(0, blocks, levels, chosen)
    copies[1].wait()
    for i in range(kin.shape[1]):
        kin[:, i, :] = jnp.transpose(kin_here[i])
    for copy in copies[2:6]:
        copy.wait()

    def group_body(group, carry):
        solve_group(group, count, chosen, lambda block: residual[block], kin, weight, pool)
        return carry

    lax.fori_loop(0, (count + GROUP - 1) // GROUP, group_body, 0)
    fill_sends(0, rows, columns, blocks, peers, downs, pool, outs)
    for copy in copies[6:]:
        copy.wait()


def later_level(level, rows, columns, levels, peers, downs, slots, residual, weight, frac, kin, *refs):
    refs = list(refs)
    half, steps = halves_of(rows), last_steps(rows, columns)
    arrived = {step: refs.pop(0) for step in steps}
    from_above = [refs.pop(0) for _ in range(columns)]
    from_halves = [refs.pop(0) for _ in range(rows // half)]
    refs.pop(0)
    pool = refs.pop(0)
    *outs, chosen = refs
    blocks, upw = residual.shape[0], slots.shape[0]
    rounds, groups = peers.shape[0], rows * columns
    here = lax.axis_index("blk")
    row, column = here // columns, lax.rem(here, columns)
    peers_first = blocks + 1 + (level - 1) * groups
    downs_first = peers_first + rounds * groups
    for row_step in range(rows):
        from_row = stepped(row, row_step, rows, back=True)
        for column_step in range(columns):
            source = from_row * columns + wrapped(column + columns - column_step, columns)
            down = arrived[row_step, 0].at[column_step] if row_step else from_above[column_step].at[0]
            at_half, rest = row_step // half, row_step % half
            if rest or column_step:
                peer = arrived[rest, column_step].at[at_half if column_step else columns + at_half]
            else:
                peer = from_halves[at_half].at[0]
            pool[downs_first + source] = down[...]
            pool[peers_first + source] = peer[...]
    count = list_level(level, blocks, levels, chosen)

    def inflow_of(block):
        inflow = residual[block]
        parts = frac[block]
        for k in range(upw):
            inflow = inflow + parts[k : k + 1, :] * pool[slots[k, block]]
        return inflow

    def group_body(group, carry):
        solve_group(group, count, chosen, inflow_of, kin, weight, pool)
        return carry

    lax.fori_loop(0, (count + GROUP - 1) // GROUP, group_body, 0)
    if level < rounds:
        fill_sends(level, rows, columns, blocks, peers, downs, pool, outs)
    else:
        outs[0][...] = pool[pl.ds(0, blocks)]


def shards(
    residual, kin_inverse, cell_weight, upwind_frac, block_level, send_in, send_down, upwind_slot
):
    blocks, species, cells = residual.shape
    sections, groups = lax.axis_size("section"), lax.axis_size("blk")
    rows, columns = split_of(groups)
    rounds = send_in.shape[1]
    peers = send_in.transpose(1, 0, 2)
    downs = send_down.transpose(1, 0, 2)
    slots = upwind_slot.transpose(1, 0)
    kin_turned = kin_inverse.transpose(1, 2, 0)
    smem = pl.BlockSpec(memory_space=pltpu.SMEM)
    vmem = pl.BlockSpec(memory_space=pltpu.VMEM)
    hbm = pl.BlockSpec(memory_space=pltpu.HBM)
    params = pltpu.CompilerParams(vmem_limit_bytes=40 * 1024 * 1024)
    pool_shape = jax.ShapeDtypeStruct((blocks + 1 + 2 * rounds * groups, species, cells), jnp.float32)
    kin_shape = jax.ShapeDtypeStruct((blocks, species, species), jnp.float32)
    half = halves_of(rows)
    send_shapes = [jax.ShapeDtypeStruct((rows, species, cells), jnp.float32)] * columns
    send_shapes += [jax.ShapeDtypeStruct((half * columns, species, cells), jnp.float32)] * (rows // half)
    chosen = pltpu.SMEM((blocks + 1,), jnp.int32)
    to_first = (block_level, kin_turned, residual, cell_weight, peers, downs, slots, upwind_frac)
    held = (block_level, peers, downs, slots, residual, cell_weight, upwind_frac)
    held_shapes = [jax.ShapeDtypeStruct(x.shape, x.dtype) for x in held]
    pool, kin, *outs = pl.pallas_call(
        functools.partial(first_level, rows, columns),
        in_specs=[hbm] * len(to_first),
        out_specs=[vmem] * (2 + len(held) + len(send_shapes)),
        out_shape=[pool_shape, kin_shape] + held_shapes + send_shapes,
        scratch_shapes=[
            chosen,
            pltpu.SMEM(block_level.shape, jnp.int32),
            pltpu.VMEM(kin_turned.shape, jnp.float32),
            pltpu.SMEM(peers.shape, jnp.int32),
            pltpu.SMEM(downs.shape, jnp.int32),
            pltpu.SemaphoreType.DMA((11,)),
        ],
        compiler_params=params,
        name="first_level",
    )(*(pltpu.with_memory_space_constraint(x, pltpu.HBM) for x in to_first))
    held, outs = outs[: len(held)], outs[len(held) :]
    for level in range(1, rounds + 1):
        from_halves = outs[columns:]
        if half < rows:
            from_halves[1] = moved(from_halves[1], sections, rows, columns, (0, half, 0))
        from_above = [moved(outs[c], sections, rows, columns, (1, 0, c)) for c in range(columns)]
        arrived = []
        for row, column in last_steps(rows, columns):
            part = [] if column else [value[row] for value in from_above]
            if row < half:
                part += [value[row * columns + column] for value in from_halves]
            arrived.append(moved(jnp.stack(part), sections, rows, columns, (0, row, column)))
        if level < rounds:
            out_shapes = send_shapes
        else:
            out_shapes = [jax.ShapeDtypeStruct(residual.shape, residual.dtype)]
        operands = held + [kin] + arrived + from_above + from_halves + [pool]
        pool, *outs = pl.pallas_call(
            functools.partial(later_level, level, rows, columns),
            in_specs=[smem] * 4 + [vmem] * (len(operands) - 4),
            out_specs=[vmem] * (1 + len(out_shapes)),
            out_shape=[pool_shape] + out_shapes,
            scratch_shapes=[chosen],
            input_output_aliases={len(operands) - 1: 0},
            compiler_params=params,
            name="later_level",
        )(*operands)
    return outs[0]


def solution(mesh):
    return jax.shard_map(
        shards,
        mesh=mesh,
        in_specs=(
            P(("section", "blk"), None, None),
            P(("section", "blk"), None, None),
            P(("section", "blk"), None),
            P(("section", "blk"), None, None),
            P(("section", "blk")),
            P(("section", "blk"), None, None),
            P(("section", "blk"), None, None),
            P(("section", "blk"), None),
        ),
        out_specs=P(("section", "blk"), None, None),
        check_vma=False,
    )
```

```python
import functools

import jax
import jax.numpy as jnp
from jax import lax
from jax.experimental import pallas as pl
from jax.experimental.pallas import tpu as pltpu
from jax.sharding import PartitionSpec as P

GROUP = 8


def split_of(groups):
    columns = max(c for c in range(1, groups + 1) if groups % c == 0 and c * c <= groups)
    return groups // columns, columns


def stepped(row, step, rows, back=False):
    if rows & (rows - 1) == 0:
        return row ^ step
    return (row + (rows - step if back else step)) % rows


def moved(value, sections, rows, columns, steps):
    groups = rows * columns
    pairs = []
    for section in range(sections):
        for row in range(rows):
            for column in range(columns):
                target = stepped(row, steps[1], rows) * columns + (column + steps[2]) % columns
                below = (section + steps[0]) % sections
                pairs.append((section * groups + row * columns + column, below * groups + target))
    return lax.ppermute(value, ("section", "blk"), pairs)


def halves_of(rows):
    return rows // 2 if rows > 1 and rows & (rows - 1) == 0 else rows


def last_steps(rows, columns):
    half = halves_of(rows)
    across = [(row, 0) for row in range(rows - 1, half - 1, -1)]
    aside = [(row, column) for row in range(half - 1, -1, -1) for column in range(1, columns)]
    return across + aside + [(row, 0) for row in range(half - 1, 0, -1)]


def wrapped(value, count):
    return jnp.where(value >= count, value - count, value)


def list_level(level, blocks, levels, chosen):
    def listed(block, count):
        chosen[count] = block
        return count + jnp.where(levels[block] == level, 1, 0)

    return lax.fori_loop(0, blocks, listed, 0)


def solve_group(group, count, chosen, inflow_of, kin, weight, pool):
    ids = [chosen[jnp.minimum(group * GROUP + i, count - 1)] for i in range(GROUP)]
    solved = []
    for block in ids:
        mixed = jnp.dot(
            kin[block], inflow_of(block), precision=lax.Precision.HIGHEST, preferred_element_type=jnp.float32
        )
        solved.append(weight[pl.ds(block, 1), :] * mixed)
    for block, value in zip(ids, solved):
        pool[block] = value


def fill_sends(level, rows, columns, blocks, peers, downs, pool, outs):
    here = lax.axis_index("blk")
    row, column = here // columns, lax.rem(here, columns)
    ends = lax.axis_index("section") == lax.axis_size("section") - 1
    half = halves_of(rows)
    for row_step in range(rows):
        to_row = stepped(row, row_step, rows)
        for column_step in range(columns):
            target = to_row * columns + wrapped(column + column_step, columns)
            outs[column_step][row_step] = pool[jnp.where(ends, blocks, downs[level, 0, target])]
            part = outs[columns + row_step // half]
            part[row_step % half * columns + column_step] = pool[peers[level, 0, target]]


def first_level(rows, columns, *refs):
    refs = list(refs)
    levels_in, kin_in, residual_in, weight_in, peers_in, downs_in, slots_in, frac_in = (refs.pop(0) for _ in range(8))
    pool, kin, levels_out, peers_out, downs_out, slots_out, residual, weight, frac = (refs.pop(0) for _ in range(9))
    outs = [refs.pop(0) for _ in range(columns + rows // halves_of(rows))]
    chosen, levels, kin_here, peers, downs, sems = refs
    pairs = [(levels_in, levels), (kin_in, kin_here), (residual_in, residual), (weight_in, weight)]
    pairs += [(peers_in, peers), (downs_in, downs)]
    pairs += [(levels_in, levels_out), (peers_in, peers_out), (downs_in, downs_out)]
    pairs += [(slots_in, slots_out), (frac_in, frac)]
    copies = [pltpu.make_async_copy(source, target, sems.at[i]) for i, (source, target) in enumerate(pairs)]
    for copy in copies:
        copy.start()
    blocks = residual.shape[0]
    pool[blocks] = jnp.zeros(pool.shape[1:], pool.dtype)
    copies[0].wait()
    count = list_level(0, blocks, levels, chosen)
    copies[1].wait()
    for i in range(kin.shape[1]):
        kin[:, i, :] = jnp.transpose(kin_here[i])
    for copy in copies[2:6]:
        copy.wait()

    def group_body(group, carry):
        solve_group(group, count, chosen, lambda block: residual[block], kin, weight, pool)
        return carry

    lax.fori_loop(0, (count + GROUP - 1) // GROUP, group_body, 0)
    fill_sends(0, rows, columns, blocks, peers, downs, pool, outs)
    for copy in copies[6:]:
        copy.wait()


def later_level(level, rows, columns, levels, peers, downs, slots, residual, weight, frac, kin, *refs):
    refs = list(refs)
    half, steps = halves_of(rows), last_steps(rows, columns)
    from_halves = [refs.pop(0) for _ in range(rows // half)]
    from_above = [refs.pop(0) for _ in range(columns)]
    arrived = {step: refs.pop(0) for step in steps}
    refs.pop(0)
    pool = refs.pop(0)
    *outs, chosen = refs
    blocks, upw = residual.shape[0], slots.shape[0]
    rounds, groups = peers.shape[0], rows * columns
    here = lax.axis_index("blk")
    row, column = here // columns, lax.rem(here, columns)
    peers_first = blocks + 1 + (level - 1) * groups
    downs_first = peers_first + rounds * groups
    for row_step in range(rows):
        from_row = stepped(row, row_step, rows, back=True)
        for column_step in range(columns):
            source = from_row * columns + wrapped(column + columns - column_step, columns)
            down = arrived[row_step, 0].at[column_step] if row_step else from_above[column_step].at[0]
            at_half, rest = row_step // half, row_step % half
            if rest or column_step:
                peer = arrived[rest, column_step].at[at_half if column_step else columns + at_half]
            else:
                peer = from_halves[at_half].at[0]
            pool[downs_first + source] = down[...]
            pool[peers_first + source] = peer[...]
    count = list_level(level, blocks, levels, chosen)

    def inflow_of(block):
        inflow = residual[block]
        parts = frac[block]
        for k in range(upw):
            inflow = inflow + parts[k : k + 1, :] * pool[slots[k, block]]
        return inflow

    def group_body(group, carry):
        solve_group(group, count, chosen, inflow_of, kin, weight, pool)
        return carry

    lax.fori_loop(0, (count + GROUP - 1) // GROUP, group_body, 0)
    if level < rounds:
        fill_sends(level, rows, columns, blocks, peers, downs, pool, outs)
    else:
        outs[0][...] = pool[pl.ds(0, blocks)]


def shards(
    residual, kin_inverse, cell_weight, upwind_frac, block_level, send_in, send_down, upwind_slot
):
    blocks, species, cells = residual.shape
    sections, groups = lax.axis_size("section"), lax.axis_size("blk")
    rows, columns = split_of(groups)
    rounds = send_in.shape[1]
    peers = send_in.transpose(1, 0, 2)
    downs = send_down.transpose(1, 0, 2)
    slots = upwind_slot.transpose(1, 0)
    kin_turned = kin_inverse.transpose(1, 2, 0)
    smem = pl.BlockSpec(memory_space=pltpu.SMEM)
    vmem = pl.BlockSpec(memory_space=pltpu.VMEM)
    hbm = pl.BlockSpec(memory_space=pltpu.HBM)
    params = pltpu.CompilerParams(vmem_limit_bytes=40 * 1024 * 1024)
    pool_shape = jax.ShapeDtypeStruct((blocks + 1 + 2 * rounds * groups, species, cells), jnp.float32)
    kin_shape = jax.ShapeDtypeStruct((blocks, species, species), jnp.float32)
    half = halves_of(rows)
    send_shapes = [jax.ShapeDtypeStruct((rows, species, cells), jnp.float32)] * columns
    send_shapes += [jax.ShapeDtypeStruct((half * columns, species, cells), jnp.float32)] * (rows // half)
    chosen = pltpu.SMEM((blocks + 1,), jnp.int32)
    to_first = (block_level, kin_turned, residual, cell_weight, peers, downs, slots, upwind_frac)
    held = (block_level, peers, downs, slots, residual, cell_weight, upwind_frac)
    held_shapes = [jax.ShapeDtypeStruct(x.shape, x.dtype) for x in held]
    pool, kin, *outs = pl.pallas_call(
        functools.partial(first_level, rows, columns),
        in_specs=[hbm] * len(to_first),
        out_specs=[vmem] * (2 + len(held) + len(send_shapes)),
        out_shape=[pool_shape, kin_shape] + held_shapes + send_shapes,
        scratch_shapes=[
            chosen,
            pltpu.SMEM(block_level.shape, jnp.int32),
            pltpu.VMEM(kin_turned.shape, jnp.float32),
            pltpu.SMEM(peers.shape, jnp.int32),
            pltpu.SMEM(downs.shape, jnp.int32),
            pltpu.SemaphoreType.DMA((11,)),
        ],
        compiler_params=params,
        name="first_level",
    )(*(pltpu.with_memory_space_constraint(x, pltpu.HBM) for x in to_first))
    held, outs = outs[: len(held)], outs[len(held) :]
    for level in range(1, rounds + 1):
        from_halves = outs[columns:]
        if half < rows:
            from_halves[1] = moved(from_halves[1], sections, rows, columns, (0, half, 0))
        from_above = [moved(outs[c], sections, rows, columns, (1, 0, c)) for c in range(columns)]
        arrived = []
        for row, column in last_steps(rows, columns):
            part = [] if column else [value[row] for value in from_above]
            if row < half:
                part += [value[row * columns + column] for value in from_halves]
            arrived.append(moved(jnp.stack(part), sections, rows, columns, (0, row, column)))
        if level < rounds:
            out_shapes = send_shapes
        else:
            out_shapes = [jax.ShapeDtypeStruct(residual.shape, residual.dtype)]
        operands = held + [kin] + from_halves + from_above + arrived + [pool]
        pool, *outs = pl.pallas_call(
            functools.partial(later_level, level, rows, columns),
            in_specs=[smem] * 4 + [vmem] * (len(operands) - 4),
            out_specs=[vmem] * (1 + len(out_shapes)),
            out_shape=[pool_shape] + out_shapes,
            scratch_shapes=[chosen],
            input_output_aliases={len(operands) - 1: 0},
            compiler_params=params,
            name="later_level",
        )(*operands)
    return outs[0]


def solution(mesh):
    return jax.shard_map(
        shards,
        mesh=mesh,
        in_specs=(
            P(("section", "blk"), None, None),
            P(("section", "blk"), None, None),
            P(("section", "blk"), None),
            P(("section", "blk"), None, None),
            P(("section", "blk")),
            P(("section", "blk"), None, None),
            P(("section", "blk"), None, None),
            P(("section", "blk"), None),
        ),
        out_specs=P(("section", "blk"), None, None),
        check_vma=False,
    )
```

```python
import functools

import jax
import jax.numpy as jnp
from jax import lax
from jax.experimental import pallas as pl
from jax.experimental.pallas import tpu as pltpu
from jax.sharding import PartitionSpec as P

GROUP = 8


def split_of(groups):
    columns = max(c for c in range(1, groups + 1) if groups % c == 0 and c * c <= groups)
    return groups // columns, columns


def stepped(row, step, rows, back=False):
    if rows & (rows - 1) == 0:
        return row ^ step
    return (row + (rows - step if back else step)) % rows


def moved(value, sections, rows, columns, steps):
    groups = rows * columns
    pairs = []
    for section in range(sections):
        for row in range(rows):
            for column in range(columns):
                target = stepped(row, steps[1], rows) * columns + (column + steps[2]) % columns
                below = (section + steps[0]) % sections
                pairs.append((section * groups + row * columns + column, below * groups + target))
    return lax.ppermute(value, ("section", "blk"), pairs)


def row_order(rows):
    return sorted(range(rows), reverse=True)


def paired(value, rows, columns, step):
    if step:
        groups = [
            [row * columns + c, (row ^ step) * columns + c] for row in range(rows) if row < row ^ step for c in range(columns)
        ]
    else:
        groups = [[row * columns + c for c in range(columns)] for row in range(rows)]
    return lax.all_gather(value, "blk", axis_index_groups=groups, axis=0, tiled=False)


def wrapped(value, count):
    return jnp.where(value >= count, value - count, value)


def list_level(level, blocks, levels, chosen):
    def listed(block, count):
        chosen[count] = block
        return count + jnp.where(levels[block] == level, 1, 0)

    return lax.fori_loop(0, blocks, listed, 0)


def solve_group(group, count, chosen, inflow_of, kin, weight, pool):
    ids = [chosen[jnp.minimum(group * GROUP + i, count - 1)] for i in range(GROUP)]
    solved = []
    for block in ids:
        mixed = jnp.dot(
            kin[block], inflow_of(block), precision=lax.Precision.HIGHEST, preferred_element_type=jnp.float32
        )
        solved.append(weight[pl.ds(block, 1), :] * mixed)
    for block, value in zip(ids, solved):
        pool[block] = value


def fill_sends(level, rows, columns, blocks, peers, downs, pool, outs):
    here = lax.axis_index("blk")
    row, column = here // columns, lax.rem(here, columns)
    ends = lax.axis_index("section") == lax.axis_size("section") - 1
    for row_step in range(rows):
        to_row = stepped(row, row_step, rows)
        for column_step in range(columns):
            target = to_row * columns + wrapped(column + column_step, columns)
            outs[column_step][row_step] = pool[jnp.where(ends, blocks, downs[level, 0, target])]
            outs[columns + column_step][row_step] = pool[peers[level, 0, target]]


def first_level(rows, columns, *refs):
    refs = list(refs)
    levels_in, kin_in, residual_in, weight_in, peers_in, downs_in, slots_in, frac_in = (refs.pop(0) for _ in range(8))
    pool, kin, levels_out, peers_out, downs_out, slots_out, residual, weight, frac = (refs.pop(0) for _ in range(9))
    outs = [refs.pop(0) for _ in range(2 * columns)]
    chosen, levels, kin_here, peers, downs, sems = refs
    pairs = [(levels_in, levels), (kin_in, kin_here), (residual_in, residual), (weight_in, weight)]
    pairs += [(peers_in, peers), (downs_in, downs)]
    pairs += [(levels_in, levels_out), (peers_in, peers_out), (downs_in, downs_out)]
    pairs += [(slots_in, slots_out), (frac_in, frac)]
    copies = [pltpu.make_async_copy(source, target, sems.at[i]) for i, (source, target) in enumerate(pairs)]
    for copy in copies:
        copy.start()
    blocks = residual.shape[0]
    pool[blocks] = jnp.zeros(pool.shape[1:], pool.dtype)
    copies[0].wait()
    count = list_level(0, blocks, levels, chosen)
    copies[1].wait()
    for i in range(kin.shape[1]):
        kin[:, i, :] = jnp.transpose(kin_here[i])
    for copy in copies[2:6]:
        copy.wait()

    def group_body(group, carry):
        solve_group(group, count, chosen, lambda block: residual[block], kin, weight, pool)
        return carry

    lax.fori_loop(0, (count + GROUP - 1) // GROUP, group_body, 0)
    fill_sends(0, rows, columns, blocks, peers, downs, pool, outs)
    for copy in copies[6:]:
        copy.wait()


def later_level(level, rows, columns, levels, peers, downs, slots, residual, weight, frac, kin, *refs):
    refs = list(refs)
    arrived = [refs.pop(0) for _ in range(rows)]
    refs.pop(0)
    pool = refs.pop(0)
    *outs, chosen = refs
    blocks, upw = residual.shape[0], slots.shape[0]
    rounds, groups = peers.shape[0], rows * columns
    here = lax.axis_index("blk")
    row, column = here // columns, lax.rem(here, columns)
    peers_first = blocks + 1 + (level - 1) * groups
    downs_first = peers_first + rounds * groups
    for part, row_step in zip(arrived, row_order(rows)):
        from_row = stepped(row, row_step, rows, back=True)
        for column_step in range(columns):
            source = from_row * columns + wrapped(column + columns - column_step, columns)
            held = part.at[(from_row > row).astype(jnp.int32)] if row_step == 1 else part
            pool[downs_first + source] = held[column_step]
            pool[peers_first + source] = held[columns + column_step]
    count = list_level(level, blocks, levels, chosen)

    def inflow_of(block):
        inflow = residual[block]
        parts = frac[block]
        for k in range(upw):
            inflow = inflow + parts[k : k + 1, :] * pool[slots[k, block]]
        return inflow

    def group_body(group, carry):
        solve_group(group, count, chosen, inflow_of, kin, weight, pool)
        return carry

    lax.fori_loop(0, (count + GROUP - 1) // GROUP, group_body, 0)
    if level < rounds:
        fill_sends(level, rows, columns, blocks, peers, downs, pool, outs)
    else:
        outs[0][...] = pool[pl.ds(0, blocks)]


def shards(
    residual, kin_inverse, cell_weight, upwind_frac, block_level, send_in, send_down, upwind_slot
):
    blocks, species, cells = residual.shape
    sections, groups = lax.axis_size("section"), lax.axis_size("blk")
    rows, columns = split_of(groups)
    rounds = send_in.shape[1]
    peers = send_in.transpose(1, 0, 2)
    downs = send_down.transpose(1, 0, 2)
    slots = upwind_slot.transpose(1, 0)
    kin_turned = kin_inverse.transpose(1, 2, 0)
    smem = pl.BlockSpec(memory_space=pltpu.SMEM)
    vmem = pl.BlockSpec(memory_space=pltpu.VMEM)
    hbm = pl.BlockSpec(memory_space=pltpu.HBM)
    params = pltpu.CompilerParams(vmem_limit_bytes=40 * 1024 * 1024)
    pool_shape = jax.ShapeDtypeStruct((blocks + 1 + 2 * rounds * groups, species, cells), jnp.float32)
    kin_shape = jax.ShapeDtypeStruct((blocks, species, species), jnp.float32)
    send_shapes = [jax.ShapeDtypeStruct((rows, species, cells), jnp.float32)] * (2 * columns)
    chosen = pltpu.SMEM((blocks + 1,), jnp.int32)
    to_first = (block_level, kin_turned, residual, cell_weight, peers, downs, slots, upwind_frac)
    held = (block_level, peers, downs, slots, residual, cell_weight, upwind_frac)
    held_shapes = [jax.ShapeDtypeStruct(x.shape, x.dtype) for x in held]
    pool, kin, *outs = pl.pallas_call(
        functools.partial(first_level, rows, columns),
        in_specs=[hbm] * len(to_first),
        out_specs=[vmem] * (2 + len(held) + len(send_shapes)),
        out_shape=[pool_shape, kin_shape] + held_shapes + send_shapes,
        scratch_shapes=[
            chosen,
            pltpu.SMEM(block_level.shape, jnp.int32),
            pltpu.VMEM(kin_turned.shape, jnp.float32),
            pltpu.SMEM(peers.shape, jnp.int32),
            pltpu.SMEM(downs.shape, jnp.int32),
            pltpu.SemaphoreType.DMA((11,)),
        ],
        compiler_params=params,
        name="first_level",
    )(*(pltpu.with_memory_space_constraint(x, pltpu.HBM) for x in to_first))
    held, outs = outs[: len(held)], outs[len(held) :]
    for level in range(1, rounds + 1):
        turned = [moved(outs[c], sections, rows, columns, (1, 0, c)) for c in range(columns)]
        turned.append(outs[columns])
        turned += [moved(outs[columns + c], sections, rows, columns, (0, 0, c)) for c in range(1, columns)]
        arrived = []
        for step in row_order(rows):
            part = jnp.stack([value[step] for value in turned])
            if step == 1:
                part = paired(part, rows, columns, 1)
            elif step:
                part = moved(part, sections, rows, columns, (0, step, 0))
            arrived.append(part)
        if level < rounds:
            out_shapes = send_shapes
        else:
            out_shapes = [jax.ShapeDtypeStruct(residual.shape, residual.dtype)]
        operands = held + [kin] + arrived + [pool]
        pool, *outs = pl.pallas_call(
            functools.partial(later_level, level, rows, columns),
            in_specs=[smem] * 4 + [vmem] * (len(operands) - 4),
            out_specs=[vmem] * (1 + len(out_shapes)),
            out_shape=[pool_shape] + out_shapes,
            scratch_shapes=[chosen],
            input_output_aliases={len(operands) - 1: 0},
            compiler_params=params,
            name="later_level",
        )(*operands)
    return outs[0]


def solution(mesh):
    return jax.shard_map(
        shards,
        mesh=mesh,
        in_specs=(
            P(("section", "blk"), None, None),
            P(("section", "blk"), None, None),
            P(("section", "blk"), None),
            P(("section", "blk"), None, None),
            P(("section", "blk")),
            P(("section", "blk"), None, None),
            P(("section", "blk"), None, None),
            P(("section", "blk"), None),
        ),
        out_specs=P(("section", "blk"), None, None),
        check_vma=False,
    )
```

```python
import functools

import jax
import jax.numpy as jnp
from jax import lax
from jax.experimental import pallas as pl
from jax.experimental.pallas import tpu as pltpu
from jax.sharding import PartitionSpec as P

GROUP = 8


def split_of(groups):
    columns = max(c for c in range(1, groups + 1) if groups % c == 0 and c * c <= groups)
    return groups // columns, columns


def stepped(row, step, rows, back=False):
    if rows & (rows - 1) == 0:
        return row ^ step
    return (row + (rows - step if back else step)) % rows


def moved(value, sections, rows, columns, steps):
    groups = rows * columns
    pairs = []
    for section in range(sections):
        for row in range(rows):
            for column in range(columns):
                target = stepped(row, steps[1], rows) * columns + (column + steps[2]) % columns
                below = (section + steps[0]) % sections
                pairs.append((section * groups + row * columns + column, below * groups + target))
    return lax.ppermute(value, ("section", "blk"), pairs)


def halves_of(rows):
    return rows // 2 if rows > 1 and rows & (rows - 1) == 0 else rows


def last_steps(rows, columns):
    half = halves_of(rows)
    steps = [(row, column) for row in range(half) for column in range(columns)]
    return sorted(steps[1:], key=lambda step: (-(step[0] > 0) - (step[1] > 0), step))


def wrapped(value, count):
    return jnp.where(value >= count, value - count, value)


def list_level(level, blocks, levels, chosen):
    def listed(block, count):
        chosen[count] = block
        return count + jnp.where(levels[block] == level, 1, 0)

    return lax.fori_loop(0, blocks, listed, 0)


def solve_group(group, count, chosen, inflow_of, kin, weight, pool):
    ids = [chosen[jnp.minimum(group * GROUP + i, count - 1)] for i in range(GROUP)]
    solved = []
    for block in ids:
        mixed = jnp.dot(
            kin[block], inflow_of(block), precision=lax.Precision.HIGHEST, preferred_element_type=jnp.float32
        )
        solved.append(weight[pl.ds(block, 1), :] * mixed)
    for block, value in zip(ids, solved):
        pool[block] = value


def fill_sends(level, rows, columns, blocks, peers, downs, pool, outs):
    here = lax.axis_index("blk")
    row, column = here // columns, lax.rem(here, columns)
    ends = lax.axis_index("section") == lax.axis_size("section") - 1
    half = halves_of(rows)
    for row_step in range(rows):
        to_row = stepped(row, row_step, rows)
        for column_step in range(columns):
            target = to_row * columns + wrapped(column + column_step, columns)
            at, place = row_step // half, row_step % half * columns + column_step
            outs[at][place] = pool[jnp.where(ends, blocks, downs[level, 0, target])]
            outs[rows // half + at][place] = pool[peers[level, 0, target]]


def first_level(rows, columns, *refs):
    refs = list(refs)
    levels_in, kin_in, residual_in, weight_in, peers_in, downs_in, slots_in, frac_in = (refs.pop(0) for _ in range(8))
    pool, kin, levels_out, peers_out, downs_out, slots_out, residual, weight, frac = (refs.pop(0) for _ in range(9))
    outs = [refs.pop(0) for _ in range(2 * (rows // halves_of(rows)))]
    chosen, levels, kin_here, peers, downs, sems = refs
    pairs = [(levels_in, levels), (kin_in, kin_here), (residual_in, residual), (weight_in, weight)]
    pairs += [(peers_in, peers), (downs_in, downs)]
    pairs += [(levels_in, levels_out), (peers_in, peers_out), (downs_in, downs_out)]
    pairs += [(slots_in, slots_out), (frac_in, frac)]
    copies = [pltpu.make_async_copy(source, target, sems.at[i]) for i, (source, target) in enumerate(pairs)]
    for copy in copies:
        copy.start()
    blocks = residual.shape[0]
    pool[blocks] = jnp.zeros(pool.shape[1:], pool.dtype)
    copies[0].wait()
    count = list_level(0, blocks, levels, chosen)
    copies[1].wait()
    for i in range(kin.shape[1]):
        kin[:, i, :] = jnp.transpose(kin_here[i])
    for copy in copies[2:6]:
        copy.wait()

    def group_body(group, carry):
        solve_group(group, count, chosen, lambda block: residual[block], kin, weight, pool)
        return carry

    lax.fori_loop(0, (count + GROUP - 1) // GROUP, group_body, 0)
    fill_sends(0, rows, columns, blocks, peers, downs, pool, outs)
    for copy in copies[6:]:
        copy.wait()


def later_level(level, rows, columns, levels, peers, downs, slots, residual, weight, frac, kin, *refs):
    refs = list(refs)
    half, steps = halves_of(rows), last_steps(rows, columns)
    arrived = {step: refs.pop(0) for step in steps}
    from_above = [refs.pop(0) for _ in range(rows // half)]
    from_halves = [refs.pop(0) for _ in range(rows // half)]
    refs.pop(0)
    pool = refs.pop(0)
    *outs, chosen = refs
    blocks, upw = residual.shape[0], slots.shape[0]
    rounds, groups = peers.shape[0], rows * columns
    here = lax.axis_index("blk")
    row, column = here // columns, lax.rem(here, columns)
    peers_first = blocks + 1 + (level - 1) * groups
    downs_first = peers_first + rounds * groups
    for row_step in range(rows):
        from_row = stepped(row, row_step, rows, back=True)
        for column_step in range(columns):
            source = from_row * columns + wrapped(column + columns - column_step, columns)
            at, rest = row_step // half, row_step % half
            if rest or column_step:
                down = arrived[rest, column_step].at[at]
                peer = arrived[rest, column_step].at[rows // half + at]
            else:
                down, peer = from_above[at].at[0], from_halves[at].at[0]
            pool[downs_first + source] = down[...]
            pool[peers_first + source] = peer[...]
    count = list_level(level, blocks, levels, chosen)

    def inflow_of(block):
        inflow = residual[block]
        parts = frac[block]
        for k in range(upw):
            inflow = inflow + parts[k : k + 1, :] * pool[slots[k, block]]
        return inflow

    def group_body(group, carry):
        solve_group(group, count, chosen, inflow_of, kin, weight, pool)
        return carry

    lax.fori_loop(0, (count + GROUP - 1) // GROUP, group_body, 0)
    if level < rounds:
        fill_sends(level, rows, columns, blocks, peers, downs, pool, outs)
    else:
        outs[0][...] = pool[pl.ds(0, blocks)]


def shards(
    residual, kin_inverse, cell_weight, upwind_frac, block_level, send_in, send_down, upwind_slot
):
    blocks, species, cells = residual.shape
    sections, groups = lax.axis_size("section"), lax.axis_size("blk")
    rows, columns = split_of(groups)
    rounds = send_in.shape[1]
    peers = send_in.transpose(1, 0, 2)
    downs = send_down.transpose(1, 0, 2)
    slots = upwind_slot.transpose(1, 0)
    kin_turned = kin_inverse.transpose(1, 2, 0)
    smem = pl.BlockSpec(memory_space=pltpu.SMEM)
    vmem = pl.BlockSpec(memory_space=pltpu.VMEM)
    hbm = pl.BlockSpec(memory_space=pltpu.HBM)
    params = pltpu.CompilerParams(vmem_limit_bytes=40 * 1024 * 1024)
    pool_shape = jax.ShapeDtypeStruct((blocks + 1 + 2 * rounds * groups, species, cells), jnp.float32)
    kin_shape = jax.ShapeDtypeStruct((blocks, species, species), jnp.float32)
    half = halves_of(rows)
    send_shapes = [jax.ShapeDtypeStruct((half * columns, species, cells), jnp.float32)] * (2 * (rows // half))
    chosen = pltpu.SMEM((blocks + 1,), jnp.int32)
    to_first = (block_level, kin_turned, residual, cell_weight, peers, downs, slots, upwind_frac)
    held = (block_level, peers, downs, slots, residual, cell_weight, upwind_frac)
    held_shapes = [jax.ShapeDtypeStruct(x.shape, x.dtype) for x in held]
    pool, kin, *outs = pl.pallas_call(
        functools.partial(first_level, rows, columns),
        in_specs=[hbm] * len(to_first),
        out_specs=[vmem] * (2 + len(held) + len(send_shapes)),
        out_shape=[pool_shape, kin_shape] + held_shapes + send_shapes,
        scratch_shapes=[
            chosen,
            pltpu.SMEM(block_level.shape, jnp.int32),
            pltpu.VMEM(kin_turned.shape, jnp.float32),
            pltpu.SMEM(peers.shape, jnp.int32),
            pltpu.SMEM(downs.shape, jnp.int32),
            pltpu.SemaphoreType.DMA((11,)),
        ],
        compiler_params=params,
        name="first_level",
    )(*(pltpu.with_memory_space_constraint(x, pltpu.HBM) for x in to_first))
    held, outs = outs[: len(held)], outs[len(held) :]
    for level in range(1, rounds + 1):
        to_below, from_halves = outs[: rows // half], outs[rows // half :]
        from_above = [moved(x, sections, rows, columns, (1, at * half, 0)) for at, x in enumerate(to_below)]
        if half < rows:
            from_halves[1] = moved(from_halves[1], sections, rows, columns, (0, half, 0))
        arrived = []
        for row, column in last_steps(rows, columns):
            part = jnp.stack([value[row * columns + column] for value in from_above + from_halves])
            arrived.append(moved(part, sections, rows, columns, (0, row, column)))
        if level < rounds:
            out_shapes = send_shapes
        else:
            out_shapes = [jax.ShapeDtypeStruct(residual.shape, residual.dtype)]
        operands = held + [kin] + arrived + from_above + from_halves + [pool]
        pool, *outs = pl.pallas_call(
            functools.partial(later_level, level, rows, columns),
            in_specs=[smem] * 4 + [vmem] * (len(operands) - 4),
            out_specs=[vmem] * (1 + len(out_shapes)),
            out_shape=[pool_shape] + out_shapes,
            scratch_shapes=[chosen],
            input_output_aliases={len(operands) - 1: 0},
            compiler_params=params,
            name="later_level",
        )(*operands)
    return outs[0]


def solution(mesh):
    return jax.shard_map(
        shards,
        mesh=mesh,
        in_specs=(
            P(("section", "blk"), None, None),
            P(("section", "blk"), None, None),
            P(("section", "blk"), None),
            P(("section", "blk"), None, None),
            P(("section", "blk")),
            P(("section", "blk"), None, None),
            P(("section", "blk"), None, None),
            P(("section", "blk"), None),
        ),
        out_specs=P(("section", "blk"), None, None),
        check_vma=False,
    )
```

```python
import functools

import jax
import jax.numpy as jnp
from jax import lax
from jax.experimental import pallas as pl
from jax.experimental.pallas import tpu as pltpu
from jax.sharding import PartitionSpec as P

GROUP = 8


def split_of(groups):
    columns = max(c for c in range(1, groups + 1) if groups % c == 0 and c * c <= groups)
    return groups // columns, columns


def stepped(row, step, rows, back=False):
    if rows & (rows - 1) == 0:
        return row ^ step
    return (row + (rows - step if back else step)) % rows


def moved(value, sections, rows, columns, steps):
    groups = rows * columns
    pairs = []
    for section in range(sections):
        for row in range(rows):
            for column in range(columns):
                target = stepped(row, steps[1], rows) * columns + (column + steps[2]) % columns
                below = (section + steps[0]) % sections
                pairs.append((section * groups + row * columns + column, below * groups + target))
    return lax.ppermute(value, ("section", "blk"), pairs)


def halves_of(rows):
    return rows // 2 if rows > 1 and rows & (rows - 1) == 0 else rows


def wrapped(value, count):
    return jnp.where(value >= count, value - count, value)


def list_level(level, blocks, levels, chosen):
    def listed(block, count):
        chosen[count] = block
        return count + jnp.where(levels[block] == level, 1, 0)

    return lax.fori_loop(0, blocks, listed, 0)


def solve_group(group, count, chosen, inflow_of, kin, weight, pool):
    ids = [chosen[jnp.minimum(group * GROUP + i, count - 1)] for i in range(GROUP)]
    solved = []
    for block in ids:
        mixed = jnp.dot(
            kin[block], inflow_of(block), precision=lax.Precision.HIGHEST, preferred_element_type=jnp.float32
        )
        solved.append(weight[pl.ds(block, 1), :] * mixed)
    for block, value in zip(ids, solved):
        pool[block] = value


def fill_sends(level, rows, columns, blocks, peers, downs, pool, outs):
    here = lax.axis_index("blk")
    row, column = here // columns, lax.rem(here, columns)
    ends = lax.axis_index("section") == lax.axis_size("section") - 1
    half = halves_of(rows)
    for row_step in range(rows):
        to_row = stepped(row, row_step, rows)
        for column_step in range(columns):
            target = to_row * columns + wrapped(column + column_step, columns)
            outs[column_step][row_step] = pool[jnp.where(ends, blocks, downs[level, 0, target])]
            part = outs[columns + row_step // half]
            part[row_step % half * columns + column_step] = pool[peers[level, 0, target]]


def first_level(rows, columns, *refs):
    refs = list(refs)
    levels_in, kin_in, residual_in, weight_in, peers_in, downs_in, slots_in, frac_in = (refs.pop(0) for _ in range(8))
    pool, kin, levels_out, peers_out, downs_out, slots_out, residual, weight, frac = (refs.pop(0) for _ in range(9))
    outs = [refs.pop(0) for _ in range(columns + rows // halves_of(rows))]
    chosen, levels, kin_here, peers, downs, sems = refs
    pairs = [(levels_in, levels), (kin_in, kin_here), (residual_in, residual), (weight_in, weight)]
    pairs += [(peers_in, peers), (downs_in, downs)]
    pairs += [(levels_in, levels_out), (peers_in, peers_out), (downs_in, downs_out)]
    pairs += [(slots_in, slots_out), (frac_in, frac)]
    copies = [pltpu.make_async_copy(source, target, sems.at[i]) for i, (source, target) in enumerate(pairs)]
    for copy in copies:
        copy.start()
    blocks = residual.shape[0]
    pool[blocks] = jnp.zeros(pool.shape[1:], pool.dtype)
    copies[0].wait()
    count = list_level(0, blocks, levels, chosen)
    copies[1].wait()
    for i in range(kin.shape[1]):
        kin[:, i, :] = jnp.transpose(kin_here[i])
    for copy in copies[2:6]:
        copy.wait()

    def group_body(group, carry):
        solve_group(group, count, chosen, lambda block: residual[block], kin, weight, pool)
        return carry

    lax.fori_loop(0, (count + GROUP - 1) // GROUP, group_body, 0)
    fill_sends(0, rows, columns, blocks, peers, downs, pool, outs)
    for copy in copies[6:]:
        copy.wait()


def later_level(level, rows, columns, levels, peers, downs, slots, residual, weight, frac, kin, *refs):
    refs = list(refs)
    half = halves_of(rows)
    from_halves = [refs.pop(0) for _ in range(rows // half)]
    over_columns = [None] + [refs.pop(0) for _ in range(1, columns)]
    from_above = [refs.pop(0) for _ in range(columns)]
    arrived = {step: refs.pop(0) for step in range(rows - 1, 0, -1)}
    refs.pop(0)
    pool = refs.pop(0)
    *outs, chosen = refs
    blocks, upw = residual.shape[0], slots.shape[0]
    rounds, groups = peers.shape[0], rows * columns
    here = lax.axis_index("blk")
    row, column = here // columns, lax.rem(here, columns)
    peers_first = blocks + 1 + (level - 1) * groups
    downs_first = peers_first + rounds * groups
    for row_step in range(rows):
        from_row = stepped(row, row_step, rows, back=True)
        for column_step in range(columns):
            source = from_row * columns + wrapped(column + columns - column_step, columns)
            at, rest = row_step // half, row_step % half
            down = arrived[row_step].at[column_step] if row_step else from_above[column_step].at[0]
            if rest:
                peer = arrived[rest].at[columns + at * columns + column_step]
            else:
                peer = over_columns[column_step].at[row_step] if column_step else from_halves[at].at[0]
            pool[downs_first + source] = down[...]
            pool[peers_first + source] = peer[...]
    count = list_level(level, blocks, levels, chosen)

    def inflow_of(block):
        inflow = residual[block]
        parts = frac[block]
        for k in range(upw):
            inflow = inflow + parts[k : k + 1, :] * pool[slots[k, block]]
        return inflow

    def group_body(group, carry):
        solve_group(group, count, chosen, inflow_of, kin, weight, pool)
        return carry

    lax.fori_loop(0, (count + GROUP - 1) // GROUP, group_body, 0)
    if level < rounds:
        fill_sends(level, rows, columns, blocks, peers, downs, pool, outs)
    else:
        outs[0][...] = pool[pl.ds(0, blocks)]


def shards(
    residual, kin_inverse, cell_weight, upwind_frac, block_level, send_in, send_down, upwind_slot
):
    blocks, species, cells = residual.shape
    sections, groups = lax.axis_size("section"), lax.axis_size("blk")
    rows, columns = split_of(groups)
    rounds = send_in.shape[1]
    peers = send_in.transpose(1, 0, 2)
    downs = send_down.transpose(1, 0, 2)
    slots = upwind_slot.transpose(1, 0)
    kin_turned = kin_inverse.transpose(1, 2, 0)
    smem = pl.BlockSpec(memory_space=pltpu.SMEM)
    vmem = pl.BlockSpec(memory_space=pltpu.VMEM)
    hbm = pl.BlockSpec(memory_space=pltpu.HBM)
    params = pltpu.CompilerParams(vmem_limit_bytes=40 * 1024 * 1024)
    pool_shape = jax.ShapeDtypeStruct((blocks + 1 + 2 * rounds * groups, species, cells), jnp.float32)
    kin_shape = jax.ShapeDtypeStruct((blocks, species, species), jnp.float32)
    half = halves_of(rows)
    send_shapes = [jax.ShapeDtypeStruct((rows, species, cells), jnp.float32)] * columns
    send_shapes += [jax.ShapeDtypeStruct((half * columns, species, cells), jnp.float32)] * (rows // half)
    chosen = pltpu.SMEM((blocks + 1,), jnp.int32)
    to_first = (block_level, kin_turned, residual, cell_weight, peers, downs, slots, upwind_frac)
    held = (block_level, peers, downs, slots, residual, cell_weight, upwind_frac)
    held_shapes = [jax.ShapeDtypeStruct(x.shape, x.dtype) for x in held]
    pool, kin, *outs = pl.pallas_call(
        functools.partial(first_level, rows, columns),
        in_specs=[hbm] * len(to_first),
        out_specs=[vmem] * (2 + len(held) + len(send_shapes)),
        out_shape=[pool_shape, kin_shape] + held_shapes + send_shapes,
        scratch_shapes=[
            chosen,
            pltpu.SMEM(block_level.shape, jnp.int32),
            pltpu.VMEM(kin_turned.shape, jnp.float32),
            pltpu.SMEM(peers.shape, jnp.int32),
            pltpu.SMEM(downs.shape, jnp.int32),
            pltpu.SemaphoreType.DMA((11,)),
        ],
        compiler_params=params,
        name="first_level",
    )(*(pltpu.with_memory_space_constraint(x, pltpu.HBM) for x in to_first))
    held, outs = outs[: len(held)], outs[len(held) :]
    for level in range(1, rounds + 1):
        from_halves = outs[columns:]
        if half < rows:
            from_halves[1] = moved(from_halves[1], sections, rows, columns, (0, half, 0))
        from_above = [moved(outs[c], sections, rows, columns, (1, 0, c)) for c in range(columns)]
        over_columns = []
        for c in range(1, columns):
            part = jnp.stack([value[row * columns + c] for value in from_halves for row in range(half)])
            over_columns.append(moved(part, sections, rows, columns, (0, 0, c)))
        arrived = []
        for step in range(rows - 1, 0, -1):
            part = [value[step] for value in from_above]
            if step < half:
                for at, value in enumerate(from_halves):
                    part += [value[step * columns]] + [other[at * half + step] for other in over_columns]
            arrived.append(moved(jnp.stack(part), sections, rows, columns, (0, step, 0)))
        if level < rounds:
            out_shapes = send_shapes
        else:
            out_shapes = [jax.ShapeDtypeStruct(residual.shape, residual.dtype)]
        operands = held + [kin] + from_halves + over_columns + from_above + arrived + [pool]
        pool, *outs = pl.pallas_call(
            functools.partial(later_level, level, rows, columns),
            in_specs=[smem] * 4 + [vmem] * (len(operands) - 4),
            out_specs=[vmem] * (1 + len(out_shapes)),
            out_shape=[pool_shape] + out_shapes,
            scratch_shapes=[chosen],
            input_output_aliases={len(operands) - 1: 0},
            compiler_params=params,
            name="later_level",
        )(*operands)
    return outs[0]


def solution(mesh):
    return jax.shard_map(
        shards,
        mesh=mesh,
        in_specs=(
            P(("section", "blk"), None, None),
            P(("section", "blk"), None, None),
            P(("section", "blk"), None),
            P(("section", "blk"), None, None),
            P(("section", "blk")),
            P(("section", "blk"), None, None),
            P(("section", "blk"), None, None),
            P(("section", "blk"), None),
        ),
        out_specs=P(("section", "blk"), None, None),
        check_vma=False,
    )
```

```python
import functools

import jax
import jax.numpy as jnp
from jax import lax
from jax.experimental import pallas as pl
from jax.experimental.pallas import tpu as pltpu
from jax.sharding import PartitionSpec as P


def split_of(groups):
    columns = max(c for c in range(1, groups + 1) if groups % c == 0 and c * c <= groups)
    return groups // columns, columns


def stepped(row, step, rows, back=False):
    if rows & (rows - 1) == 0:
        return row ^ step
    return (row + (rows - step if back else step)) % rows


def moved(value, sections, rows, columns, steps):
    groups = rows * columns
    pairs = []
    for section in range(sections):
        for row in range(rows):
            for column in range(columns):
                target = stepped(row, steps[1], rows) * columns + (column + steps[2]) % columns
                below = (section + steps[0]) % sections
                pairs.append((section * groups + row * columns + column, below * groups + target))
    return lax.ppermute(value, ("section", "blk"), pairs)


def halves_of(rows):
    return rows // 2 if rows > 1 and rows & (rows - 1) == 0 else rows


def last_steps(rows, columns):
    half = halves_of(rows)
    across = [(row, 0) for row in range(rows - 1, half - 1, -1)]
    aside = [(row, column) for row in range(half - 1, -1, -1) for column in range(1, columns)]
    return across + aside + [(row, 0) for row in range(half - 1, 0, -1)]


def wrapped(value, count):
    return jnp.where(value >= count, value - count, value)


def sort_blocks(blocks, levels, plan):
    stride = blocks + 1
    for level in range(plan.shape[0] // stride):
        plan[level * stride + blocks] = 0

    def place(block, carry):
        first = levels[block] * stride
        count = plan[first + blocks]
        plan[first + count] = block
        plan[first + blocks] = count + 1
        return carry

    lax.fori_loop(0, blocks, place, 0)


def solve_blocks(level, blocks, plan, inflow_of, kin, weight, pool):
    first = level * (blocks + 1)
    count = plan[first + blocks]
    ids = [plan[first + jnp.minimum(i, count - 1)] for i in range(blocks * 8 // 24)]
    solved = []
    for block in ids:
        mixed = jnp.dot(
            kin[block], inflow_of(block), precision=lax.Precision.HIGHEST, preferred_element_type=jnp.float32
        )
        solved.append(weight[pl.ds(block, 1), :] * mixed)
    for block, value in zip(ids, solved):
        pool[block] = value


def fill_sends(level, rows, columns, blocks, peers, downs, pool, outs):
    here = lax.axis_index("blk")
    row, column = here // columns, lax.rem(here, columns)
    ends = lax.axis_index("section") == lax.axis_size("section") - 1
    half = halves_of(rows)
    for row_step in range(rows):
        to_row = stepped(row, row_step, rows)
        for column_step in range(columns):
            target = to_row * columns + wrapped(column + column_step, columns)
            outs[column_step][row_step] = pool[jnp.where(ends, blocks, downs[level, 0, target])]
            part = outs[columns + row_step // half]
            part[row_step % half * columns + column_step] = pool[peers[level, 0, target]]


def first_level(rows, columns, *refs):
    refs = list(refs)
    levels_in, kin_in, residual_in, weight_in, peers_in, downs_in, slots_in, frac_in = (refs.pop(0) for _ in range(8))
    pool, kin, plan, peers_out, downs_out, slots_out, residual, weight, frac = (refs.pop(0) for _ in range(9))
    outs = [refs.pop(0) for _ in range(columns + rows // halves_of(rows))]
    levels, kin_here, peers, downs, sems = refs
    pairs = [(levels_in, levels), (kin_in, kin_here), (residual_in, residual), (weight_in, weight)]
    pairs += [(peers_in, peers), (downs_in, downs)]
    pairs += [(peers_in, peers_out), (downs_in, downs_out), (slots_in, slots_out), (frac_in, frac)]
    copies = [pltpu.make_async_copy(source, target, sems.at[i]) for i, (source, target) in enumerate(pairs)]
    for copy in copies:
        copy.start()
    blocks = residual.shape[0]
    pool[blocks] = jnp.zeros(pool.shape[1:], pool.dtype)
    copies[0].wait()
    sort_blocks(blocks, levels, plan)
    copies[1].wait()
    for i in range(kin.shape[1]):
        kin[:, i, :] = jnp.transpose(kin_here[i])
    for copy in copies[2:6]:
        copy.wait()

    solve_blocks(0, blocks, plan, lambda block: residual[block], kin, weight, pool)
    fill_sends(0, rows, columns, blocks, peers, downs, pool, outs)
    for copy in copies[6:]:
        copy.wait()


def later_level(level, rows, columns, plan, peers, downs, slots, residual, weight, frac, kin, *refs):
    refs = list(refs)
    half, steps = halves_of(rows), last_steps(rows, columns)
    arrived = {step: refs.pop(0) for step in steps}
    from_above = [refs.pop(0) for _ in range(columns)]
    from_halves = [refs.pop(0) for _ in range(rows // half)]
    refs.pop(0)
    pool = refs.pop(0)
    outs = refs
    blocks, upw = residual.shape[0], slots.shape[0]
    rounds, groups = peers.shape[0], rows * columns
    here = lax.axis_index("blk")
    row, column = here // columns, lax.rem(here, columns)
    peers_first = blocks + 1 + (level - 1) * groups
    downs_first = peers_first + rounds * groups
    for row_step in range(rows):
        from_row = stepped(row, row_step, rows, back=True)
        for column_step in range(columns):
            source = from_row * columns + wrapped(column + columns - column_step, columns)
            down = arrived[row_step, 0].at[column_step] if row_step else from_above[column_step].at[0]
            at_half, rest = row_step // half, row_step % half
            if rest or column_step:
                peer = arrived[rest, column_step].at[at_half if column_step else columns + at_half]
            else:
                peer = from_halves[at_half].at[0]
            pool[downs_first + source] = down[...]
            pool[peers_first + source] = peer[...]

    def inflow_of(block):
        inflow = residual[block]
        parts = frac[block]
        for k in range(upw):
            inflow = inflow + parts[k : k + 1, :] * pool[slots[k, block]]
        return inflow

    solve_blocks(level, blocks, plan, inflow_of, kin, weight, pool)
    if level < rounds:
        fill_sends(level, rows, columns, blocks, peers, downs, pool, outs)
    else:
        outs[0][...] = pool[pl.ds(0, blocks)]


def shards(
    residual, kin_inverse, cell_weight, upwind_frac, block_level, send_in, send_down, upwind_slot
):
    blocks, species, cells = residual.shape
    sections, groups = lax.axis_size("section"), lax.axis_size("blk")
    rows, columns = split_of(groups)
    rounds = send_in.shape[1]
    peers = send_in.transpose(1, 0, 2)
    downs = send_down.transpose(1, 0, 2)
    slots = upwind_slot.transpose(1, 0)
    kin_turned = kin_inverse.transpose(1, 2, 0)
    smem = pl.BlockSpec(memory_space=pltpu.SMEM)
    vmem = pl.BlockSpec(memory_space=pltpu.VMEM)
    hbm = pl.BlockSpec(memory_space=pltpu.HBM)
    params = pltpu.CompilerParams(vmem_limit_bytes=40 * 1024 * 1024)
    pool_shape = jax.ShapeDtypeStruct((blocks + 1 + 2 * rounds * groups, species, cells), jnp.float32)
    kin_shape = jax.ShapeDtypeStruct((blocks, species, species), jnp.float32)
    half = halves_of(rows)
    send_shapes = [jax.ShapeDtypeStruct((rows, species, cells), jnp.float32)] * columns
    send_shapes += [jax.ShapeDtypeStruct((half * columns, species, cells), jnp.float32)] * (rows // half)
    to_first = (block_level, kin_turned, residual, cell_weight, peers, downs, slots, upwind_frac)
    held = (peers, downs, slots, residual, cell_weight, upwind_frac)
    held_shapes = [jax.ShapeDtypeStruct(((rounds + 1) * (blocks + 1),), jnp.int32)]
    held_shapes += [jax.ShapeDtypeStruct(x.shape, x.dtype) for x in held]
    pool, kin, *outs = pl.pallas_call(
        functools.partial(first_level, rows, columns),
        in_specs=[hbm] * len(to_first),
        out_specs=[vmem, vmem, smem] + [vmem] * (len(held) + len(send_shapes)),
        out_shape=[pool_shape, kin_shape] + held_shapes + send_shapes,
        scratch_shapes=[
            pltpu.SMEM(block_level.shape, jnp.int32),
            pltpu.VMEM(kin_turned.shape, jnp.float32),
            pltpu.SMEM(peers.shape, jnp.int32),
            pltpu.SMEM(downs.shape, jnp.int32),
            pltpu.SemaphoreType.DMA((10,)),
        ],
        compiler_params=params,
        name="first_level",
    )(*(pltpu.with_memory_space_constraint(x, pltpu.HBM) for x in to_first))
    held, outs = outs[: len(held_shapes)], outs[len(held_shapes) :]
    for level in range(1, rounds + 1):
        from_halves = outs[columns:]
        if half < rows:
            from_halves[1] = moved(from_halves[1], sections, rows, columns, (0, half, 0))
        from_above = [moved(outs[c], sections, rows, columns, (1, 0, c)) for c in range(columns)]
        arrived = []
        for row, column in last_steps(rows, columns):
            part = [] if column else [value[row] for value in from_above]
            if row < half:
                part += [value[row * columns + column] for value in from_halves]
            arrived.append(moved(jnp.stack(part), sections, rows, columns, (0, row, column)))
        if level < rounds:
            out_shapes = send_shapes
        else:
            out_shapes = [jax.ShapeDtypeStruct(residual.shape, residual.dtype)]
        operands = held + [kin] + arrived + from_above + from_halves + [pool]
        pool, *outs = pl.pallas_call(
            functools.partial(later_level, level, rows, columns),
            in_specs=[smem] * 4 + [vmem] * (len(operands) - 4),
            out_specs=[vmem] * (1 + len(out_shapes)),
            out_shape=[pool_shape] + out_shapes,
            input_output_aliases={len(operands) - 1: 0},
            compiler_params=params,
            name="later_level",
        )(*operands)
    return outs[0]


def solution(mesh):
    return jax.shard_map(
        shards,
        mesh=mesh,
        in_specs=(
            P(("section", "blk"), None, None),
            P(("section", "blk"), None, None),
            P(("section", "blk"), None),
            P(("section", "blk"), None, None),
            P(("section", "blk")),
            P(("section", "blk"), None, None),
            P(("section", "blk"), None, None),
            P(("section", "blk"), None),
        ),
        out_specs=P(("section", "blk"), None, None),
        check_vma=False,
    )
```

```python
import functools

import jax
import jax.numpy as jnp
from jax import lax
from jax.experimental import pallas as pl
from jax.experimental.pallas import tpu as pltpu
from jax.sharding import PartitionSpec as P


def split_of(groups):
    columns = max(c for c in range(1, groups + 1) if groups % c == 0 and c * c <= groups)
    return groups // columns, columns


def stepped(row, step, rows, back=False):
    if rows & (rows - 1) == 0:
        return row ^ step
    return (row + (rows - step if back else step)) % rows


def moved(value, sections, rows, columns, steps):
    groups = rows * columns
    pairs = []
    for section in range(sections):
        for row in range(rows):
            for column in range(columns):
                target = stepped(row, steps[1], rows) * columns + (column + steps[2]) % columns
                below = (section + steps[0]) % sections
                pairs.append((section * groups + row * columns + column, below * groups + target))
    return lax.ppermute(value, ("section", "blk"), pairs)


def halves_of(rows):
    return rows // 2 if rows > 1 and rows & (rows - 1) == 0 else rows


def last_steps(rows, columns):
    half = halves_of(rows)
    across = [(row, 0) for row in range(rows - 1, half - 1, -1)]
    aside = [(row, column) for row in range(half - 1, -1, -1) for column in range(1, columns)]
    return across + aside + [(row, 0) for row in range(half - 1, 0, -1)]


def wrapped(value, count):
    return jnp.where(value >= count, value - count, value)


def sort_blocks(blocks, levels, plan):
    stride = blocks + 1
    count = plan.shape[0] // stride
    together = 4 if blocks % 4 == 0 else 1

    def place(step, ends):
        for i in range(together):
            block = step * together + i
            level = levels[block]
            for end in ends:
                plan[end] = block
            ends = tuple(end + jnp.where(level == own, 1, 0) for own, end in enumerate(ends))
        return ends

    ends = lax.fori_loop(0, blocks // together, place, tuple(jnp.int32(own * stride) for own in range(count)))
    for own, end in enumerate(ends):
        plan[own * stride + blocks] = end - own * stride


def solve_blocks(level, blocks, plan, inflow_of, kin, weight, pool):
    first = level * (blocks + 1)
    count = plan[first + blocks]
    ids = [plan[first + jnp.minimum(i, count - 1)] for i in range(blocks * 8 // 24)]
    solved = []
    for block in ids:
        mixed = jnp.dot(
            kin[block], inflow_of(block), precision=lax.Precision.HIGHEST, preferred_element_type=jnp.float32
        )
        solved.append(weight[pl.ds(block, 1), :] * mixed)
    for block, value in zip(ids, solved):
        pool[block] = value


def fill_sends(level, rows, columns, blocks, peers, downs, pool, outs):
    here = lax.axis_index("blk")
    row, column = here // columns, lax.rem(here, columns)
    ends = lax.axis_index("section") == lax.axis_size("section") - 1
    half = halves_of(rows)
    for row_step in range(rows):
        to_row = stepped(row, row_step, rows)
        for column_step in range(columns):
            target = to_row * columns + wrapped(column + column_step, columns)
            outs[column_step][row_step] = pool[jnp.where(ends, blocks, downs[level, 0, target])]
            part = outs[columns + row_step // half]
            part[row_step % half * columns + column_step] = pool[peers[level, 0, target]]


def first_level(rows, columns, *refs):
    refs = list(refs)
    levels_in, kin_in, residual_in, weight_in, peers_in, downs_in, slots_in, frac_in = (refs.pop(0) for _ in range(8))
    pool, kin, plan, peers_out, downs_out, slots_out, residual, weight, frac = (refs.pop(0) for _ in range(9))
    outs = [refs.pop(0) for _ in range(columns + rows // halves_of(rows))]
    levels, kin_here, peers, downs, sems = refs
    pairs = [(levels_in, levels), (kin_in, kin_here), (residual_in, residual), (weight_in, weight)]
    pairs += [(peers_in, peers), (downs_in, downs)]
    pairs += [(peers_in, peers_out), (downs_in, downs_out), (slots_in, slots_out), (frac_in, frac)]
    copies = [pltpu.make_async_copy(source, target, sems.at[i]) for i, (source, target) in enumerate(pairs)]
    for copy in copies:
        copy.start()
    blocks = residual.shape[0]
    pool[blocks] = jnp.zeros(pool.shape[1:], pool.dtype)
    copies[0].wait()
    sort_blocks(blocks, levels, plan)
    copies[1].wait()
    for i in range(kin.shape[1]):
        kin[:, i, :] = jnp.transpose(kin_here[i])
    for copy in copies[2:6]:
        copy.wait()

    solve_blocks(0, blocks, plan, lambda block: residual[block], kin, weight, pool)
    fill_sends(0, rows, columns, blocks, peers, downs, pool, outs)
    for copy in copies[6:]:
        copy.wait()


def later_level(level, rows, columns, plan, peers, downs, slots, residual, weight, frac, kin, *refs):
    refs = list(refs)
    half, steps = halves_of(rows), last_steps(rows, columns)
    arrived = {step: refs.pop(0) for step in steps}
    from_above = [refs.pop(0) for _ in range(columns)]
    from_halves = [refs.pop(0) for _ in range(rows // half)]
    refs.pop(0)
    pool = refs.pop(0)
    outs = refs
    blocks, upw = residual.shape[0], slots.shape[0]
    rounds, groups = peers.shape[0], rows * columns
    here = lax.axis_index("blk")
    row, column = here // columns, lax.rem(here, columns)
    peers_first = blocks + 1 + (level - 1) * groups
    downs_first = peers_first + rounds * groups
    for row_step in range(rows):
        from_row = stepped(row, row_step, rows, back=True)
        for column_step in range(columns):
            source = from_row * columns + wrapped(column + columns - column_step, columns)
            down = arrived[row_step, 0].at[column_step] if row_step else from_above[column_step].at[0]
            at_half, rest = row_step // half, row_step % half
            if rest or column_step:
                peer = arrived[rest, column_step].at[at_half if column_step else columns + at_half]
            else:
                peer = from_halves[at_half].at[0]
            pool[downs_first + source] = down[...]
            pool[peers_first + source] = peer[...]

    def inflow_of(block):
        inflow = residual[block]
        parts = frac[block]
        for k in range(upw):
            inflow = inflow + parts[k : k + 1, :] * pool[slots[k, block]]
        return inflow

    solve_blocks(level, blocks, plan, inflow_of, kin, weight, pool)
    if level < rounds:
        fill_sends(level, rows, columns, blocks, peers, downs, pool, outs)
    else:
        outs[0][...] = pool[pl.ds(0, blocks)]


def shards(
    residual, kin_inverse, cell_weight, upwind_frac, block_level, send_in, send_down, upwind_slot
):
    blocks, species, cells = residual.shape
    sections, groups = lax.axis_size("section"), lax.axis_size("blk")
    rows, columns = split_of(groups)
    rounds = send_in.shape[1]
    peers = send_in.transpose(1, 0, 2)
    downs = send_down.transpose(1, 0, 2)
    slots = upwind_slot.transpose(1, 0)
    kin_turned = kin_inverse.transpose(1, 2, 0)
    smem = pl.BlockSpec(memory_space=pltpu.SMEM)
    vmem = pl.BlockSpec(memory_space=pltpu.VMEM)
    hbm = pl.BlockSpec(memory_space=pltpu.HBM)
    params = pltpu.CompilerParams(vmem_limit_bytes=40 * 1024 * 1024)
    pool_shape = jax.ShapeDtypeStruct((blocks + 1 + 2 * rounds * groups, species, cells), jnp.float32)
    kin_shape = jax.ShapeDtypeStruct((blocks, species, species), jnp.float32)
    half = halves_of(rows)
    send_shapes = [jax.ShapeDtypeStruct((rows, species, cells), jnp.float32)] * columns
    send_shapes += [jax.ShapeDtypeStruct((half * columns, species, cells), jnp.float32)] * (rows // half)
    to_first = (block_level, kin_turned, residual, cell_weight, peers, downs, slots, upwind_frac)
    held = (peers, downs, slots, residual, cell_weight, upwind_frac)
    held_shapes = [jax.ShapeDtypeStruct(((rounds + 1) * (blocks + 1),), jnp.int32)]
    held_shapes += [jax.ShapeDtypeStruct(x.shape, x.dtype) for x in held]
    pool, kin, *outs = pl.pallas_call(
        functools.partial(first_level, rows, columns),
        in_specs=[hbm] * len(to_first),
        out_specs=[vmem, vmem, smem] + [vmem] * (len(held) + len(send_shapes)),
        out_shape=[pool_shape, kin_shape] + held_shapes + send_shapes,
        scratch_shapes=[
            pltpu.SMEM(block_level.shape, jnp.int32),
            pltpu.VMEM(kin_turned.shape, jnp.float32),
            pltpu.SMEM(peers.shape, jnp.int32),
            pltpu.SMEM(downs.shape, jnp.int32),
            pltpu.SemaphoreType.DMA((10,)),
        ],
        compiler_params=params,
        name="first_level",
    )(*(pltpu.with_memory_space_constraint(x, pltpu.HBM) for x in to_first))
    held, outs = outs[: len(held_shapes)], outs[len(held_shapes) :]
    for level in range(1, rounds + 1):
        from_halves = outs[columns:]
        if half < rows:
            from_halves[1] = moved(from_halves[1], sections, rows, columns, (0, half, 0))
        from_above = [moved(outs[c], sections, rows, columns, (1, 0, c)) for c in range(columns)]
        arrived = []
        for row, column in last_steps(rows, columns):
            part = [] if column else [value[row] for value in from_above]
            if row < half:
                part += [value[row * columns + column] for value in from_halves]
            arrived.append(moved(jnp.stack(part), sections, rows, columns, (0, row, column)))
        if level < rounds:
            out_shapes = send_shapes
        else:
            out_shapes = [jax.ShapeDtypeStruct(residual.shape, residual.dtype)]
        operands = held + [kin] + arrived + from_above + from_halves + [pool]
        pool, *outs = pl.pallas_call(
            functools.partial(later_level, level, rows, columns),
            in_specs=[smem] * 4 + [vmem] * (len(operands) - 4),
            out_specs=[vmem] * (1 + len(out_shapes)),
            out_shape=[pool_shape] + out_shapes,
            input_output_aliases={len(operands) - 1: 0},
            compiler_params=params,
            name="later_level",
        )(*operands)
    return outs[0]


def solution(mesh):
    return jax.shard_map(
        shards,
        mesh=mesh,
        in_specs=(
            P(("section", "blk"), None, None),
            P(("section", "blk"), None, None),
            P(("section", "blk"), None),
            P(("section", "blk"), None, None),
            P(("section", "blk")),
            P(("section", "blk"), None, None),
            P(("section", "blk"), None, None),
            P(("section", "blk"), None),
        ),
        out_specs=P(("section", "blk"), None, None),
        check_vma=False,
    )
```

```python
import functools

import jax
import jax.numpy as jnp
from jax import lax
from jax.experimental import pallas as pl
from jax.experimental.pallas import tpu as pltpu
from jax.sharding import PartitionSpec as P


def split_of(groups):
    columns = max(c for c in range(1, groups + 1) if groups % c == 0 and c * c <= groups)
    return groups // columns, columns


def stepped(row, step, rows, back=False):
    if rows & (rows - 1) == 0:
        return row ^ step
    return (row + (rows - step if back else step)) % rows


def moved(value, sections, rows, columns, steps):
    groups = rows * columns
    pairs = []
    for section in range(sections):
        for row in range(rows):
            for column in range(columns):
                target = stepped(row, steps[1], rows) * columns + (column + steps[2]) % columns
                below = (section + steps[0]) % sections
                pairs.append((section * groups + row * columns + column, below * groups + target))
    return lax.ppermute(value, ("section", "blk"), pairs)


def halves_of(rows):
    return rows // 2 if rows > 1 and rows & (rows - 1) == 0 else rows


def last_steps(rows, columns):
    half = halves_of(rows)
    across = [(row, 0) for row in range(rows - 1, half - 1, -1)]
    aside = [(row, column) for row in range(half - 1, -1, -1) for column in range(1, columns)]
    return across + aside + [(row, 0) for row in range(half - 1, 0, -1)]


def wrapped(value, count):
    return jnp.where(value >= count, value - count, value)


def sort_blocks(blocks, levels, plan):
    stride = blocks + 1
    count = plan.shape[0] // stride
    together = 4 if blocks % 4 == 0 else 1

    def place(step, ends):
        for i in range(together):
            block = step * together + i
            level = levels[block]
            for end in ends:
                plan[end] = block
            ends = tuple(end + jnp.where(level == own, 1, 0) for own, end in enumerate(ends))
        return ends

    ends = lax.fori_loop(0, blocks // together, place, tuple(jnp.int32(own * stride) for own in range(count)))
    for own, end in enumerate(ends):
        plan[own * stride + blocks] = end - own * stride


def solve_blocks(level, blocks, plan, inflow_of, kin, weight, pool):
    first = level * (blocks + 1)
    count = plan[first + blocks]
    ids = [plan[first + jnp.minimum(i, count - 1)] for i in range(blocks * 8 // 24)]
    solved = []
    for block in ids:
        mixed = jnp.dot(
            kin[block], inflow_of(block), precision=lax.Precision.HIGHEST, preferred_element_type=jnp.float32
        )
        solved.append(weight[pl.ds(block, 1), :] * mixed)
    for block, value in zip(ids, solved):
        pool[block] = value


def fill_sends(level, rows, columns, blocks, peers, downs, pool, outs):
    here = lax.axis_index("blk")
    row, column = here // columns, lax.rem(here, columns)
    ends = lax.axis_index("section") == lax.axis_size("section") - 1
    half = halves_of(rows)
    for row_step in range(rows):
        to_row = stepped(row, row_step, rows)
        for column_step in range(columns):
            target = to_row * columns + wrapped(column + column_step, columns)
            outs[column_step][row_step] = pool[jnp.where(ends, blocks, downs[level, 0, target])]
            part = outs[columns + row_step // half]
            part[row_step % half * columns + column_step] = pool[peers[level, 0, target]]


def first_level(rows, columns, *refs):
    refs = list(refs)
    levels_in, kin_in, residual_in, weight_in, peers_in, downs_in, slots_in, frac_in = (refs.pop(0) for _ in range(8))
    pool, kin, plan_out, peers_out, downs_out, slots_out, residual, weight, frac = (refs.pop(0) for _ in range(9))
    outs = [refs.pop(0) for _ in range(columns + rows // halves_of(rows))]
    plan, levels, kin_here, peers, downs, sems = refs
    pairs = [(levels_in, levels), (kin_in, kin_here), (residual_in, residual), (weight_in, weight)]
    pairs += [(peers_in, peers), (downs_in, downs)]
    pairs += [(peers_in, peers_out), (downs_in, downs_out), (slots_in, slots_out), (frac_in, frac)]
    pairs += [(plan, plan_out)]
    copies = [pltpu.make_async_copy(source, target, sems.at[i]) for i, (source, target) in enumerate(pairs)]
    for copy in copies[:-1]:
        copy.start()
    blocks = residual.shape[0]
    pool[blocks] = jnp.zeros(pool.shape[1:], pool.dtype)
    copies[0].wait()
    sort_blocks(blocks, levels, plan)
    copies[-1].start()
    copies[1].wait()
    for i in range(kin.shape[1]):
        kin[:, i, :] = jnp.transpose(kin_here[i])
    for copy in copies[2:6]:
        copy.wait()

    solve_blocks(0, blocks, plan, lambda block: residual[block], kin, weight, pool)
    fill_sends(0, rows, columns, blocks, peers, downs, pool, outs)
    for copy in copies[6:]:
        copy.wait()


def later_level(level, rows, columns, plan, peers, downs, slots, residual, weight, frac, kin, *refs):
    refs = list(refs)
    half, steps = halves_of(rows), last_steps(rows, columns)
    arrived = {step: refs.pop(0) for step in steps}
    from_above = [refs.pop(0) for _ in range(columns)]
    from_halves = [refs.pop(0) for _ in range(rows // half)]
    refs.pop(0)
    pool = refs.pop(0)
    outs = refs
    blocks, upw = residual.shape[0], slots.shape[0]
    rounds, groups = peers.shape[0], rows * columns
    here = lax.axis_index("blk")
    row, column = here // columns, lax.rem(here, columns)
    peers_first = blocks + 1 + (level - 1) * groups
    downs_first = peers_first + rounds * groups
    for row_step in range(rows):
        from_row = stepped(row, row_step, rows, back=True)
        for column_step in range(columns):
            source = from_row * columns + wrapped(column + columns - column_step, columns)
            down = arrived[row_step, 0].at[column_step] if row_step else from_above[column_step].at[0]
            at_half, rest = row_step // half, row_step % half
            if rest or column_step:
                peer = arrived[rest, column_step].at[at_half if column_step else columns + at_half]
            else:
                peer = from_halves[at_half].at[0]
            pool[downs_first + source] = down[...]
            pool[peers_first + source] = peer[...]

    def inflow_of(block):
        inflow = residual[block]
        parts = frac[block]
        for k in range(upw):
            inflow = inflow + parts[k : k + 1, :] * pool[slots[k, block]]
        return inflow

    solve_blocks(level, blocks, plan, inflow_of, kin, weight, pool)
    if level < rounds:
        fill_sends(level, rows, columns, blocks, peers, downs, pool, outs)
    else:
        outs[0][...] = pool[pl.ds(0, blocks)]


def shards(
    residual, kin_inverse, cell_weight, upwind_frac, block_level, send_in, send_down, upwind_slot
):
    blocks, species, cells = residual.shape
    sections, groups = lax.axis_size("section"), lax.axis_size("blk")
    rows, columns = split_of(groups)
    rounds = send_in.shape[1]
    peers = send_in.transpose(1, 0, 2)
    downs = send_down.transpose(1, 0, 2)
    slots = upwind_slot.transpose(1, 0)
    kin_turned = kin_inverse.transpose(1, 2, 0)
    smem = pl.BlockSpec(memory_space=pltpu.SMEM)
    vmem = pl.BlockSpec(memory_space=pltpu.VMEM)
    hbm = pl.BlockSpec(memory_space=pltpu.HBM)
    params = pltpu.CompilerParams(vmem_limit_bytes=40 * 1024 * 1024)
    pool_shape = jax.ShapeDtypeStruct((blocks + 1 + 2 * rounds * groups, species, cells), jnp.float32)
    kin_shape = jax.ShapeDtypeStruct((blocks, species, species), jnp.float32)
    half = halves_of(rows)
    send_shapes = [jax.ShapeDtypeStruct((rows, species, cells), jnp.float32)] * columns
    send_shapes += [jax.ShapeDtypeStruct((half * columns, species, cells), jnp.float32)] * (rows // half)
    to_first = (block_level, kin_turned, residual, cell_weight, peers, downs, slots, upwind_frac)
    held = (peers, downs, slots, residual, cell_weight, upwind_frac)
    held_shapes = [jax.ShapeDtypeStruct(((rounds + 1) * (blocks + 1),), jnp.int32)]
    held_shapes += [jax.ShapeDtypeStruct(x.shape, x.dtype) for x in held]
    pool, kin, *outs = pl.pallas_call(
        functools.partial(first_level, rows, columns),
        in_specs=[hbm] * len(to_first),
        out_specs=[vmem] * (2 + len(held_shapes) + len(send_shapes)),
        out_shape=[pool_shape, kin_shape] + held_shapes + send_shapes,
        scratch_shapes=[
            pltpu.SMEM(held_shapes[0].shape, jnp.int32),
            pltpu.SMEM(block_level.shape, jnp.int32),
            pltpu.VMEM(kin_turned.shape, jnp.float32),
            pltpu.SMEM(peers.shape, jnp.int32),
            pltpu.SMEM(downs.shape, jnp.int32),
            pltpu.SemaphoreType.DMA((11,)),
        ],
        compiler_params=params,
        name="first_level",
    )(*(pltpu.with_memory_space_constraint(x, pltpu.HBM) for x in to_first))
    held, outs = outs[: len(held_shapes)], outs[len(held_shapes) :]
    for level in range(1, rounds + 1):
        from_halves = outs[columns:]
        if half < rows:
            from_halves[1] = moved(from_halves[1], sections, rows, columns, (0, half, 0))
        from_above = [moved(outs[c], sections, rows, columns, (1, 0, c)) for c in range(columns)]
        arrived = []
        for row, column in last_steps(rows, columns):
            part = [] if column else [value[row] for value in from_above]
            if row < half:
                part += [value[row * columns + column] for value in from_halves]
            arrived.append(moved(jnp.stack(part), sections, rows, columns, (0, row, column)))
        if level < rounds:
            out_shapes = send_shapes
        else:
            out_shapes = [jax.ShapeDtypeStruct(residual.shape, residual.dtype)]
        operands = held + [kin] + arrived + from_above + from_halves + [pool]
        pool, *outs = pl.pallas_call(
            functools.partial(later_level, level, rows, columns),
            in_specs=[smem] * 4 + [vmem] * (len(operands) - 4),
            out_specs=[vmem] * (1 + len(out_shapes)),
            out_shape=[pool_shape] + out_shapes,
            input_output_aliases={len(operands) - 1: 0},
            compiler_params=params,
            name="later_level",
        )(*operands)
    return outs[0]


def solution(mesh):
    return jax.shard_map(
        shards,
        mesh=mesh,
        in_specs=(
            P(("section", "blk"), None, None),
            P(("section", "blk"), None, None),
            P(("section", "blk"), None),
            P(("section", "blk"), None, None),
            P(("section", "blk")),
            P(("section", "blk"), None, None),
            P(("section", "blk"), None, None),
            P(("section", "blk"), None),
        ),
        out_specs=P(("section", "blk"), None, None),
        check_vma=False,
    )
```

```python
import functools

import jax
import jax.numpy as jnp
from jax import lax
from jax.experimental import pallas as pl
from jax.experimental.pallas import tpu as pltpu
from jax.sharding import PartitionSpec as P


def split_of(groups):
    columns = max(c for c in range(1, groups + 1) if groups % c == 0 and c * c <= groups)
    return groups // columns, columns


def stepped(row, step, rows, back=False):
    if rows & (rows - 1) == 0:
        return row ^ step
    return (row + (rows - step if back else step)) % rows


def moved(value, sections, rows, columns, steps):
    groups = rows * columns
    pairs = []
    for section in range(sections):
        for row in range(rows):
            for column in range(columns):
                target = stepped(row, steps[1], rows) * columns + (column + steps[2]) % columns
                below = (section + steps[0]) % sections
                pairs.append((section * groups + row * columns + column, below * groups + target))
    return lax.ppermute(value, ("section", "blk"), pairs)


def halves_of(rows):
    return rows // 2 if rows > 1 and rows & (rows - 1) == 0 else rows


def wrapped(value, count):
    return jnp.where(value >= count, value - count, value)


def sort_blocks(blocks, levels, plan):
    stride = blocks + 1
    count = plan.shape[0] // stride
    together = 4 if blocks % 4 == 0 else 1

    def place(step, ends):
        for i in range(together):
            block = step * together + i
            level = levels[block]
            for end in ends:
                plan[end] = block
            ends = tuple(end + jnp.where(level == own, 1, 0) for own, end in enumerate(ends))
        return ends

    ends = lax.fori_loop(0, blocks // together, place, tuple(jnp.int32(own * stride) for own in range(count)))
    for own, end in enumerate(ends):
        plan[own * stride + blocks] = end - own * stride


def solve_blocks(level, blocks, plan, inflow_of, kin, weight, pool):
    first = level * (blocks + 1)
    count = plan[first + blocks]
    ids = [plan[first + jnp.minimum(i, count - 1)] for i in range(blocks * 8 // 24)]
    solved = []
    for block in ids:
        mixed = jnp.dot(
            kin[block], inflow_of(block), precision=lax.Precision.HIGHEST, preferred_element_type=jnp.float32
        )
        solved.append(weight[pl.ds(block, 1), :] * mixed)
    for block, value in zip(ids, solved):
        pool[block] = value


def fill_sends(level, rows, columns, blocks, peers, downs, pool, outs):
    here = lax.axis_index("blk")
    row, column = here // columns, lax.rem(here, columns)
    ends = lax.axis_index("section") == lax.axis_size("section") - 1
    half = halves_of(rows)
    for row_step in range(rows):
        to_row = stepped(row, row_step, rows)
        for column_step in range(columns):
            target = to_row * columns + wrapped(column + column_step, columns)
            outs[column_step][row_step] = pool[jnp.where(ends, blocks, downs[level, 0, target])]
            peer = pool[peers[level, 0, target]]
            if column_step:
                outs[columns - 1 + column_step][row_step] = peer
            else:
                outs[2 * columns - 1 + row_step // half][row_step % half] = peer


def first_level(rows, columns, *refs):
    refs = list(refs)
    levels_in, kin_in, residual_in, weight_in, peers_in, downs_in, slots_in, frac_in = (refs.pop(0) for _ in range(8))
    pool, kin, plan_out, peers_out, downs_out, slots_out, residual, weight, frac = (refs.pop(0) for _ in range(9))
    outs = [refs.pop(0) for _ in range(2 * columns - 1 + rows // halves_of(rows))]
    plan, levels, kin_here, peers, downs, sems = refs
    pairs = [(levels_in, levels), (kin_in, kin_here), (residual_in, residual), (weight_in, weight)]
    pairs += [(peers_in, peers), (downs_in, downs)]
    pairs += [(peers_in, peers_out), (downs_in, downs_out), (slots_in, slots_out), (frac_in, frac)]
    pairs += [(plan, plan_out)]
    copies = [pltpu.make_async_copy(source, target, sems.at[i]) for i, (source, target) in enumerate(pairs)]
    for copy in copies[:-1]:
        copy.start()
    blocks = residual.shape[0]
    pool[blocks] = jnp.zeros(pool.shape[1:], pool.dtype)
    copies[0].wait()
    sort_blocks(blocks, levels, plan)
    copies[-1].start()
    copies[1].wait()
    for i in range(kin.shape[1]):
        kin[:, i, :] = jnp.transpose(kin_here[i])
    for copy in copies[2:6]:
        copy.wait()

    solve_blocks(0, blocks, plan, lambda block: residual[block], kin, weight, pool)
    fill_sends(0, rows, columns, blocks, peers, downs, pool, outs)
    for copy in copies[6:]:
        copy.wait()


def later_level(level, rows, columns, plan, peers, downs, slots, residual, weight, frac, kin, *refs):
    refs = list(refs)
    half = halves_of(rows)
    from_above = [refs.pop(0) for _ in range(columns)]
    over_columns = [None] + [refs.pop(0) for _ in range(1, columns)]
    own_column = [refs.pop(0) for _ in range(rows // half)]
    arrived = {step: refs.pop(0) for step in range(rows - 1, 0, -1)}
    refs.pop(0)
    pool = refs.pop(0)
    outs = refs
    blocks, upw = residual.shape[0], slots.shape[0]
    rounds, groups = peers.shape[0], rows * columns
    here = lax.axis_index("blk")
    row, column = here // columns, lax.rem(here, columns)
    peers_first = blocks + 1 + (level - 1) * groups
    downs_first = peers_first + rounds * groups
    for row_step in range(rows):
        from_row = stepped(row, row_step, rows, back=True)
        for column_step in range(columns):
            source = from_row * columns + wrapped(column + columns - column_step, columns)
            down = arrived[row_step].at[column_step] if row_step else from_above[column_step].at[0]
            if column_step:
                peer = arrived[row_step].at[columns - 1 + column_step] if row_step else over_columns[column_step].at[0]
            else:
                at, rest = row_step // half, row_step % half
                peer = arrived[rest].at[2 * columns - 1 + at] if rest else own_column[at].at[0]
            pool[downs_first + source] = down[...]
            pool[peers_first + source] = peer[...]

    def inflow_of(block):
        inflow = residual[block]
        parts = frac[block]
        for k in range(upw):
            inflow = inflow + parts[k : k + 1, :] * pool[slots[k, block]]
        return inflow

    solve_blocks(level, blocks, plan, inflow_of, kin, weight, pool)
    if level < rounds:
        fill_sends(level, rows, columns, blocks, peers, downs, pool, outs)
    else:
        outs[0][...] = pool[pl.ds(0, blocks)]


def shards(
    residual, kin_inverse, cell_weight, upwind_frac, block_level, send_in, send_down, upwind_slot
):
    blocks, species, cells = residual.shape
    sections, groups = lax.axis_size("section"), lax.axis_size("blk")
    rows, columns = split_of(groups)
    rounds = send_in.shape[1]
    peers = send_in.transpose(1, 0, 2)
    downs = send_down.transpose(1, 0, 2)
    slots = upwind_slot.transpose(1, 0)
    kin_turned = kin_inverse.transpose(1, 2, 0)
    smem = pl.BlockSpec(memory_space=pltpu.SMEM)
    vmem = pl.BlockSpec(memory_space=pltpu.VMEM)
    hbm = pl.BlockSpec(memory_space=pltpu.HBM)
    params = pltpu.CompilerParams(vmem_limit_bytes=40 * 1024 * 1024)
    pool_shape = jax.ShapeDtypeStruct((blocks + 1 + 2 * rounds * groups, species, cells), jnp.float32)
    kin_shape = jax.ShapeDtypeStruct((blocks, species, species), jnp.float32)
    half = halves_of(rows)
    send_shapes = [jax.ShapeDtypeStruct((rows, species, cells), jnp.float32)] * (2 * columns - 1)
    send_shapes += [jax.ShapeDtypeStruct((half, species, cells), jnp.float32)] * (rows // half)
    to_first = (block_level, kin_turned, residual, cell_weight, peers, downs, slots, upwind_frac)
    held = (peers, downs, slots, residual, cell_weight, upwind_frac)
    held_shapes = [jax.ShapeDtypeStruct(((rounds + 1) * (blocks + 1),), jnp.int32)]
    held_shapes += [jax.ShapeDtypeStruct(x.shape, x.dtype) for x in held]
    pool, kin, *outs = pl.pallas_call(
        functools.partial(first_level, rows, columns),
        in_specs=[hbm] * len(to_first),
        out_specs=[vmem] * (2 + len(held_shapes) + len(send_shapes)),
        out_shape=[pool_shape, kin_shape] + held_shapes + send_shapes,
        scratch_shapes=[
            pltpu.SMEM(held_shapes[0].shape, jnp.int32),
            pltpu.SMEM(block_level.shape, jnp.int32),
            pltpu.VMEM(kin_turned.shape, jnp.float32),
            pltpu.SMEM(peers.shape, jnp.int32),
            pltpu.SMEM(downs.shape, jnp.int32),
            pltpu.SemaphoreType.DMA((11,)),
        ],
        compiler_params=params,
        name="first_level",
    )(*(pltpu.with_memory_space_constraint(x, pltpu.HBM) for x in to_first))
    held, outs = outs[: len(held_shapes)], outs[len(held_shapes) :]
    for level in range(1, rounds + 1):
        from_above = [moved(outs[c], sections, rows, columns, (1, 0, c)) for c in range(columns)]
        over_columns = [moved(outs[columns - 1 + c], sections, rows, columns, (0, 0, c)) for c in range(1, columns)]
        own_column = outs[2 * columns - 1 :]
        if half < rows:
            own_column[1] = moved(own_column[1], sections, rows, columns, (0, half, 0))
        arrived = []
        for step in range(rows - 1, 0, -1):
            part = [value[step] for value in from_above + over_columns]
            if step < half:
                part += [value[step] for value in own_column]
            arrived.append(moved(jnp.stack(part), sections, rows, columns, (0, step, 0)))
        if level < rounds:
            out_shapes = send_shapes
        else:
            out_shapes = [jax.ShapeDtypeStruct(residual.shape, residual.dtype)]
        operands = held + [kin] + from_above + over_columns + own_column + arrived + [pool]
        pool, *outs = pl.pallas_call(
            functools.partial(later_level, level, rows, columns),
            in_specs=[smem] * 4 + [vmem] * (len(operands) - 4),
            out_specs=[vmem] * (1 + len(out_shapes)),
            out_shape=[pool_shape] + out_shapes,
            input_output_aliases={len(operands) - 1: 0},
            compiler_params=params,
            name="later_level",
        )(*operands)
    return outs[0]


def solution(mesh):
    return jax.shard_map(
        shards,
        mesh=mesh,
        in_specs=(
            P(("section", "blk"), None, None),
            P(("section", "blk"), None, None),
            P(("section", "blk"), None),
            P(("section", "blk"), None, None),
            P(("section", "blk")),
            P(("section", "blk"), None, None),
            P(("section", "blk"), None, None),
            P(("section", "blk"), None),
        ),
        out_specs=P(("section", "blk"), None, None),
        check_vma=False,
    )
```

```python
import functools

import jax
import jax.numpy as jnp
from jax import lax
from jax.experimental import pallas as pl
from jax.experimental.pallas import tpu as pltpu
from jax.sharding import PartitionSpec as P


def split_of(groups):
    columns = max(c for c in range(1, groups + 1) if groups % c == 0 and c * c <= groups)
    return groups // columns, columns


def stepped(row, step, rows, back=False):
    if rows & (rows - 1) == 0:
        return row ^ step
    return (row + (rows - step if back else step)) % rows


def moved(value, sections, rows, columns, steps):
    groups = rows * columns
    pairs = []
    for section in range(sections):
        for row in range(rows):
            for column in range(columns):
                target = stepped(row, steps[1], rows) * columns + (column + steps[2]) % columns
                below = (section + steps[0]) % sections
                pairs.append((section * groups + row * columns + column, below * groups + target))
    return lax.ppermute(value, ("section", "blk"), pairs)


def halves_of(rows):
    return rows // 2 if rows > 1 and rows & (rows - 1) == 0 else rows


def last_steps(rows, columns):
    half = halves_of(rows)
    across = [(row, 0) for row in range(rows - 1, half - 1, -1)]
    aside = [(row, column) for row in range(half - 1, -1, -1) for column in range(1, columns)]
    return across + aside + [(row, 0) for row in range(half - 1, 0, -1)]


def wrapped(value, count):
    return jnp.where(value >= count, value - count, value)


def plan_places(blocks, rounds, groups):
    sends_at = (rounds + 1) * (blocks + 1)
    return sends_at, sends_at + 2 * rounds * groups


def plan_levels(levels, peers, downs, slots, plan):
    blocks, rounds, groups = levels.shape[0], peers.shape[0], peers.shape[2]
    sends_at, slots_at = plan_places(blocks, rounds, groups)
    stride = blocks + 1
    ends = lax.axis_index("section") == lax.axis_size("section") - 1
    for round_ in range(rounds):
        for j in range(groups):
            place = sends_at + 2 * groups * round_ + j
            plan[place] = jnp.where(ends, blocks, downs[round_, 0, j])
            plan[place + groups] = peers[round_, 0, j]
    together = 4 if blocks % 4 == 0 else 1

    def place_block(step, lasts):
        for i in range(together):
            block = step * together + i
            level = levels[block]
            for last in lasts:
                plan[last] = block
            lasts = tuple(last + jnp.where(level == own, 1, 0) for own, last in enumerate(lasts))
            for k in range(slots.shape[0]):
                plan[slots_at + k * blocks + block] = slots[k, block]
        return lasts

    lasts = tuple(jnp.int32(own * stride) for own in range(rounds + 1))
    lasts = lax.fori_loop(0, blocks // together, place_block, lasts)
    for own, last in enumerate(lasts):
        plan[own * stride + blocks] = last - own * stride


def solve_blocks(ids, inflow_of, kin, weight, pool):
    solved = []
    for block in ids:
        mixed = jnp.dot(
            kin[block], inflow_of(block), precision=lax.Precision.HIGHEST, preferred_element_type=jnp.float32
        )
        solved.append(weight[pl.ds(block, 1), :] * mixed)
    for block, value in zip(ids, solved):
        pool[block] = value


def first_places(count, blocks):
    return [jnp.minimum(i, count - 1) for i in range(blocks * 8 // 24)]


def fill_sends(rows, columns, down_of, peer_of, pool, outs):
    here = lax.axis_index("blk")
    row, column = here // columns, lax.rem(here, columns)
    half = halves_of(rows)
    for row_step in range(rows):
        to_row = stepped(row, row_step, rows)
        for column_step in range(columns):
            target = to_row * columns + wrapped(column + column_step, columns)
            outs[column_step][row_step] = pool[down_of(target)]
            part = outs[columns + row_step // half]
            part[row_step % half * columns + column_step] = pool[peer_of(target)]


def first_level(rows, columns, *refs):
    refs = list(refs)
    levels_in, kin_in, residual_in, weight_in, peers_in, downs_in, slots_in, frac_in = (refs.pop(0) for _ in range(8))
    pool, kin, levels_out, peers_out, downs_out, slots_out, residual, weight, frac = (refs.pop(0) for _ in range(9))
    outs = [refs.pop(0) for _ in range(columns + rows // halves_of(rows))]
    chosen, levels, kin_here, peers, downs, sems = refs
    pairs = [(levels_in, levels), (kin_in, kin_here), (residual_in, residual), (weight_in, weight)]
    pairs += [(peers_in, peers), (downs_in, downs)]
    pairs += [(levels_in, levels_out), (peers_in, peers_out), (downs_in, downs_out)]
    pairs += [(slots_in, slots_out), (frac_in, frac)]
    copies = [pltpu.make_async_copy(source, target, sems.at[i]) for i, (source, target) in enumerate(pairs)]
    for copy in copies:
        copy.start()
    blocks = residual.shape[0]
    pool[blocks] = jnp.zeros(pool.shape[1:], pool.dtype)
    copies[0].wait()

    def listed(block, count):
        chosen[count] = block
        return count + jnp.where(levels[block] == 0, 1, 0)

    count = lax.fori_loop(0, blocks, listed, 0)
    copies[1].wait()
    for i in range(kin.shape[1]):
        kin[:, i, :] = jnp.transpose(kin_here[i])
    for copy in copies[2:6]:
        copy.wait()
    ids = [chosen[place] for place in first_places(count, blocks)]
    solve_blocks(ids, lambda block: residual[block], kin, weight, pool)
    ends = lax.axis_index("section") == lax.axis_size("section") - 1
    fill_sends(
        rows, columns, lambda j: jnp.where(ends, blocks, downs[0, 0, j]), lambda j: peers[0, 0, j], pool, outs
    )
    for copy in copies[6:]:
        copy.wait()


def later_level(level, rounds, rows, columns, plan, residual, weight, frac, kin, *refs):
    refs = list(refs)
    half, steps = halves_of(rows), last_steps(rows, columns)
    arrived = {step: refs.pop(0) for step in steps}
    from_above = [refs.pop(0) for _ in range(columns)]
    from_halves = [refs.pop(0) for _ in range(rows // half)]
    refs.pop(0)
    pool = refs.pop(0)
    outs = refs
    blocks, upw = frac.shape[:2]
    groups = rows * columns
    sends_at, slots_at = plan_places(blocks, rounds, groups)
    here = lax.axis_index("blk")
    row, column = here // columns, lax.rem(here, columns)
    peers_first = blocks + 1 + (level - 1) * groups
    downs_first = peers_first + rounds * groups
    for row_step in range(rows):
        from_row = stepped(row, row_step, rows, back=True)
        for column_step in range(columns):
            source = from_row * columns + wrapped(column + columns - column_step, columns)
            down = arrived[row_step, 0].at[column_step] if row_step else from_above[column_step].at[0]
            at_half, rest = row_step // half, row_step % half
            if rest or column_step:
                peer = arrived[rest, column_step].at[at_half if column_step else columns + at_half]
            else:
                peer = from_halves[at_half].at[0]
            pool[downs_first + source] = down[...]
            pool[peers_first + source] = peer[...]

    def inflow_of(block):
        inflow = residual[block]
        parts = frac[block]
        for k in range(upw):
            inflow = inflow + parts[k : k + 1, :] * pool[plan[slots_at + k * blocks + block]]
        return inflow

    first = level * (blocks + 1)
    ids = [plan[first + place] for place in first_places(plan[first + blocks], blocks)]
    solve_blocks(ids, inflow_of, kin, weight, pool)
    if level < rounds:
        downs_at = sends_at + 2 * groups * level
        fill_sends(
            rows, columns, lambda j: plan[downs_at + j], lambda j: plan[downs_at + groups + j], pool, outs
        )
    else:
        outs[0][...] = pool[pl.ds(0, blocks)]


def shards(
    residual, kin_inverse, cell_weight, upwind_frac, block_level, send_in, send_down, upwind_slot
):
    blocks, species, cells = residual.shape
    sections, groups = lax.axis_size("section"), lax.axis_size("blk")
    rows, columns = split_of(groups)
    rounds = send_in.shape[1]
    peers = send_in.transpose(1, 0, 2)
    downs = send_down.transpose(1, 0, 2)
    slots = upwind_slot.transpose(1, 0)
    kin_turned = kin_inverse.transpose(1, 2, 0)
    smem = pl.BlockSpec(memory_space=pltpu.SMEM)
    vmem = pl.BlockSpec(memory_space=pltpu.VMEM)
    hbm = pl.BlockSpec(memory_space=pltpu.HBM)
    params = pltpu.CompilerParams(vmem_limit_bytes=40 * 1024 * 1024)
    pool_shape = jax.ShapeDtypeStruct((blocks + 1 + 2 * rounds * groups, species, cells), jnp.float32)
    kin_shape = jax.ShapeDtypeStruct((blocks, species, species), jnp.float32)
    half = halves_of(rows)
    send_shapes = [jax.ShapeDtypeStruct((rows, species, cells), jnp.float32)] * columns
    send_shapes += [jax.ShapeDtypeStruct((half * columns, species, cells), jnp.float32)] * (rows // half)
    to_first = (block_level, kin_turned, residual, cell_weight, peers, downs, slots, upwind_frac)
    held = (block_level, peers, downs, slots, residual, cell_weight, upwind_frac)
    held_shapes = [jax.ShapeDtypeStruct(x.shape, x.dtype) for x in held]
    pool, kin, *outs = pl.pallas_call(
        functools.partial(first_level, rows, columns),
        in_specs=[hbm] * len(to_first),
        out_specs=[vmem] * (2 + len(held_shapes) + len(send_shapes)),
        out_shape=[pool_shape, kin_shape] + held_shapes + send_shapes,
        scratch_shapes=[
            pltpu.SMEM((blocks + 1,), jnp.int32),
            pltpu.SMEM(block_level.shape, jnp.int32),
            pltpu.VMEM(kin_turned.shape, jnp.float32),
            pltpu.SMEM(peers.shape, jnp.int32),
            pltpu.SMEM(downs.shape, jnp.int32),
            pltpu.SemaphoreType.DMA((11,)),
        ],
        compiler_params=params,
        name="first_level",
    )(*(pltpu.with_memory_space_constraint(x, pltpu.HBM) for x in to_first))
    held, outs = outs[: len(held_shapes)], outs[len(held_shapes) :]
    plan = pl.pallas_call(
        plan_levels,
        in_specs=[smem] * 4,
        out_specs=smem,
        out_shape=jax.ShapeDtypeStruct((plan_places(blocks, rounds, groups)[1] + upwind_slot.size,), jnp.int32),
        name="plan_levels",
    )(*held[:4])
    held = [plan] + held[4:]
    for level in range(1, rounds + 1):
        from_halves = outs[columns:]
        if half < rows:
            from_halves[1] = moved(from_halves[1], sections, rows, columns, (0, half, 0))
        from_above = [moved(outs[c], sections, rows, columns, (1, 0, c)) for c in range(columns)]
        arrived = []
        for row, column in last_steps(rows, columns):
            part = [] if column else [value[row] for value in from_above]
            if row < half:
                part += [value[row * columns + column] for value in from_halves]
            arrived.append(moved(jnp.stack(part), sections, rows, columns, (0, row, column)))
        if level < rounds:
            out_shapes = send_shapes
        else:
            out_shapes = [jax.ShapeDtypeStruct(residual.shape, residual.dtype)]
        operands = held + [kin] + arrived + from_above + from_halves + [pool]
        pool, *outs = pl.pallas_call(
            functools.partial(later_level, level, rounds, rows, columns),
            in_specs=[smem] + [vmem] * (len(operands) - 1),
            out_specs=[vmem] * (1 + len(out_shapes)),
            out_shape=[pool_shape] + out_shapes,
            input_output_aliases={len(operands) - 1: 0},
            compiler_params=params,
            name="later_level",
        )(*operands)
    return outs[0]


def solution(mesh):
    return jax.shard_map(
        shards,
        mesh=mesh,
        in_specs=(
            P(("section", "blk"), None, None),
            P(("section", "blk"), None, None),
            P(("section", "blk"), None),
            P(("section", "blk"), None, None),
            P(("section", "blk")),
            P(("section", "blk"), None, None),
            P(("section", "blk"), None, None),
            P(("section", "blk"), None),
        ),
        out_specs=P(("section", "blk"), None, None),
        check_vma=False,
    )
```

```python
import functools

import jax
import jax.numpy as jnp
from jax import lax
from jax.experimental import pallas as pl
from jax.experimental.pallas import tpu as pltpu
from jax.sharding import PartitionSpec as P


def split_of(groups):
    columns = max(c for c in range(1, groups + 1) if groups % c == 0 and c * c <= groups)
    return groups // columns, columns


def stepped(row, step, rows, back=False):
    if rows & (rows - 1) == 0:
        return row ^ step
    return (row + (rows - step if back else step)) % rows


def moved(value, sections, rows, columns, steps):
    groups = rows * columns
    pairs = []
    for section in range(sections):
        for row in range(rows):
            for column in range(columns):
                target = stepped(row, steps[1], rows) * columns + (column + steps[2]) % columns
                below = (section + steps[0]) % sections
                pairs.append((section * groups + row * columns + column, below * groups + target))
    return lax.ppermute(value, ("section", "blk"), pairs)


def halves_of(rows):
    return rows // 2 if rows > 1 and rows & (rows - 1) == 0 else rows


def wrapped(value, count):
    return jnp.where(value >= count, value - count, value)


def sort_blocks(blocks, levels, plan):
    stride = blocks + 1
    count = plan.shape[0] // stride
    together = 4 if blocks % 4 == 0 else 1

    def place(step, ends):
        for i in range(together):
            block = step * together + i
            level = levels[block]
            for end in ends:
                plan[end] = block
            ends = tuple(end + jnp.where(level == own, 1, 0) for own, end in enumerate(ends))
        return ends

    ends = lax.fori_loop(0, blocks // together, place, tuple(jnp.int32(own * stride) for own in range(count)))
    for own, end in enumerate(ends):
        plan[own * stride + blocks] = end - own * stride


def solve_blocks(level, blocks, plan, inflow_of, kin, weight, pool):
    first = level * (blocks + 1)
    count = plan[first + blocks]
    ids = [plan[first + jnp.minimum(i, count - 1)] for i in range(blocks * 8 // 24)]
    solved = []
    for block in ids:
        mixed = jnp.dot(
            kin[block], inflow_of(block), precision=lax.Precision.HIGHEST, preferred_element_type=jnp.float32
        )
        solved.append(weight[pl.ds(block, 1), :] * mixed)
    for block, value in zip(ids, solved):
        pool[block] = value


def fill_sends(level, rows, columns, blocks, peers, downs, pool, outs):
    here = lax.axis_index("blk")
    row, column = here // columns, lax.rem(here, columns)
    ends = lax.axis_index("section") == lax.axis_size("section") - 1
    half = halves_of(rows)
    for row_step in range(rows):
        to_row = stepped(row, row_step, rows)
        for column_step in range(columns):
            target = to_row * columns + wrapped(column + column_step, columns)
            outs[column_step][row_step] = pool[jnp.where(ends, blocks, downs[level, 0, target])]
            part = outs[columns + row_step // half]
            part[row_step % half * columns + column_step] = pool[peers[level, 0, target]]


def first_level(rows, columns, *refs):
    refs = list(refs)
    levels_in, kin_in, residual_in, weight_in, peers_in, downs_in, slots_in, frac_in = (refs.pop(0) for _ in range(8))
    pool, kin, plan_out, peers_out, downs_out, slots_out, residual, weight, frac = (refs.pop(0) for _ in range(9))
    outs = [refs.pop(0) for _ in range(columns + rows // halves_of(rows))]
    plan, levels, kin_here, peers, downs, sems = refs
    pairs = [(levels_in, levels), (kin_in, kin_here), (residual_in, residual), (weight_in, weight)]
    pairs += [(peers_in, peers), (downs_in, downs)]
    pairs += [(peers_in, peers_out), (downs_in, downs_out), (slots_in, slots_out), (frac_in, frac)]
    pairs += [(plan, plan_out)]
    copies = [pltpu.make_async_copy(source, target, sems.at[i]) for i, (source, target) in enumerate(pairs)]
    for copy in copies[:-1]:
        copy.start()
    blocks = residual.shape[0]
    pool[blocks] = jnp.zeros(pool.shape[1:], pool.dtype)
    copies[0].wait()
    sort_blocks(blocks, levels, plan)
    copies[-1].start()
    copies[1].wait()
    for i in range(kin.shape[1]):
        kin[:, i, :] = jnp.transpose(kin_here[i])
    for copy in copies[2:6]:
        copy.wait()

    solve_blocks(0, blocks, plan, lambda block: residual[block], kin, weight, pool)
    fill_sends(0, rows, columns, blocks, peers, downs, pool, outs)
    for copy in copies[6:]:
        copy.wait()


def later_level(level, rows, columns, plan, peers, downs, slots, residual, weight, frac, kin, *refs):
    refs = list(refs)
    half = halves_of(rows)
    from_above = [refs.pop(0) for _ in range(columns)]
    from_halves = [refs.pop(0) for _ in range(rows // half)]
    crossed = refs.pop(0) if half < rows else None
    peer_rows = [from_halves] + [refs.pop(0) for _ in range(1, half)]
    down_rows = [None] + [refs.pop(0) for _ in range(1, half)]
    peer_columns = [None] + [refs.pop(0) for _ in range(1, columns)]
    refs.pop(0)
    pool = refs.pop(0)
    outs = refs
    blocks, upw = residual.shape[0], slots.shape[0]
    rounds, groups = peers.shape[0], rows * columns
    here = lax.axis_index("blk")
    row, column = here // columns, lax.rem(here, columns)
    peers_first = blocks + 1 + (level - 1) * groups
    downs_first = peers_first + rounds * groups
    for row_step in range(rows):
        from_row = stepped(row, row_step, rows, back=True)
        for column_step in range(columns):
            source = from_row * columns + wrapped(column + columns - column_step, columns)
            at, rest = row_step // half, row_step % half
            if rest:
                down = down_rows[rest].at[at * columns + column_step]
            else:
                down = crossed.at[column_step * half] if at else from_above[column_step].at[0]
            if column_step:
                peer = peer_columns[column_step].at[row_step]
            else:
                peer = peer_rows[rest].at[at * columns] if rest else from_halves[at].at[0]
            pool[downs_first + source] = down[...]
            pool[peers_first + source] = peer[...]

    def inflow_of(block):
        inflow = residual[block]
        parts = frac[block]
        for k in range(upw):
            inflow = inflow + parts[k : k + 1, :] * pool[slots[k, block]]
        return inflow

    solve_blocks(level, blocks, plan, inflow_of, kin, weight, pool)
    if level < rounds:
        fill_sends(level, rows, columns, blocks, peers, downs, pool, outs)
    else:
        outs[0][...] = pool[pl.ds(0, blocks)]


def shards(
    residual, kin_inverse, cell_weight, upwind_frac, block_level, send_in, send_down, upwind_slot
):
    blocks, species, cells = residual.shape
    sections, groups = lax.axis_size("section"), lax.axis_size("blk")
    rows, columns = split_of(groups)
    rounds = send_in.shape[1]
    peers = send_in.transpose(1, 0, 2)
    downs = send_down.transpose(1, 0, 2)
    slots = upwind_slot.transpose(1, 0)
    kin_turned = kin_inverse.transpose(1, 2, 0)
    smem = pl.BlockSpec(memory_space=pltpu.SMEM)
    vmem = pl.BlockSpec(memory_space=pltpu.VMEM)
    hbm = pl.BlockSpec(memory_space=pltpu.HBM)
    params = pltpu.CompilerParams(vmem_limit_bytes=40 * 1024 * 1024)
    pool_shape = jax.ShapeDtypeStruct((blocks + 1 + 2 * rounds * groups, species, cells), jnp.float32)
    kin_shape = jax.ShapeDtypeStruct((blocks, species, species), jnp.float32)
    half = halves_of(rows)
    send_shapes = [jax.ShapeDtypeStruct((rows, species, cells), jnp.float32)] * columns
    send_shapes += [jax.ShapeDtypeStruct((half * columns, species, cells), jnp.float32)] * (rows // half)
    to_first = (block_level, kin_turned, residual, cell_weight, peers, downs, slots, upwind_frac)
    held = (peers, downs, slots, residual, cell_weight, upwind_frac)
    held_shapes = [jax.ShapeDtypeStruct(((rounds + 1) * (blocks + 1),), jnp.int32)]
    held_shapes += [jax.ShapeDtypeStruct(x.shape, x.dtype) for x in held]
    pool, kin, *outs = pl.pallas_call(
        functools.partial(first_level, rows, columns),
        in_specs=[hbm] * len(to_first),
        out_specs=[vmem] * (2 + len(held_shapes) + len(send_shapes)),
        out_shape=[pool_shape, kin_shape] + held_shapes + send_shapes,
        scratch_shapes=[
            pltpu.SMEM(held_shapes[0].shape, jnp.int32),
            pltpu.SMEM(block_level.shape, jnp.int32),
            pltpu.VMEM(kin_turned.shape, jnp.float32),
            pltpu.SMEM(peers.shape, jnp.int32),
            pltpu.SMEM(downs.shape, jnp.int32),
            pltpu.SemaphoreType.DMA((11,)),
        ],
        compiler_params=params,
        name="first_level",
    )(*(pltpu.with_memory_space_constraint(x, pltpu.HBM) for x in to_first))
    held, outs = outs[: len(held_shapes)], outs[len(held_shapes) :]
    for level in range(1, rounds + 1):
        from_halves = outs[columns:]
        if half < rows:
            from_halves[1] = moved(from_halves[1], sections, rows, columns, (0, half, 0))
        from_above = [moved(outs[c], sections, rows, columns, (1, 0, c)) for c in range(columns)]
        crossed = []
        if half < rows:
            part = jnp.stack([value[half + row] for value in from_above for row in range(half)])
            crossed.append(moved(part, sections, rows, columns, (0, half, 0)))
        peer_rows, down_rows, peer_columns = [], [], []
        for row in range(1, half):
            part = jnp.stack([value[row * columns + c] for value in from_halves for c in range(columns)])
            peer_rows.append(moved(part, sections, rows, columns, (0, row, 0)))
        for row in range(1, half):
            far = [value[c * half + row] for value in crossed for c in range(columns)]
            part = jnp.stack([value[row] for value in from_above] + far)
            down_rows.append(moved(part, sections, rows, columns, (0, row, 0)))
        for c in range(1, columns):
            part = []
            for at, value in enumerate(from_halves):
                part += [value[c]] + [other[at * columns + c] for other in peer_rows]
            peer_columns.append(moved(jnp.stack(part), sections, rows, columns, (0, 0, c)))
        arrived = from_above + from_halves + crossed + peer_rows + down_rows + peer_columns
        if level < rounds:
            out_shapes = send_shapes
        else:
            out_shapes = [jax.ShapeDtypeStruct(residual.shape, residual.dtype)]
        operands = held + [kin] + arrived + [pool]
        pool, *outs = pl.pallas_call(
            functools.partial(later_level, level, rows, columns),
            in_specs=[smem] * 4 + [vmem] * (len(operands) - 4),
            out_specs=[vmem] * (1 + len(out_shapes)),
            out_shape=[pool_shape] + out_shapes,
            input_output_aliases={len(operands) - 1: 0},
            compiler_params=params,
            name="later_level",
        )(*operands)
    return outs[0]


def solution(mesh):
    return jax.shard_map(
        shards,
        mesh=mesh,
        in_specs=(
            P(("section", "blk"), None, None),
            P(("section", "blk"), None, None),
            P(("section", "blk"), None),
            P(("section", "blk"), None, None),
            P(("section", "blk")),
            P(("section", "blk"), None, None),
            P(("section", "blk"), None, None),
            P(("section", "blk"), None),
        ),
        out_specs=P(("section", "blk"), None, None),
        check_vma=False,
    )
```

```python
import functools

import jax
import jax.numpy as jnp
from jax import lax
from jax.experimental import pallas as pl
from jax.experimental.pallas import tpu as pltpu
from jax.sharding import PartitionSpec as P


def split_of(groups):
    columns = max(c for c in range(1, groups + 1) if groups % c == 0 and c * c <= groups)
    return groups // columns, columns


def stepped(row, step, rows, back=False):
    if rows & (rows - 1) == 0:
        return row ^ step
    return (row + (rows - step if back else step)) % rows


def moved(value, sections, rows, columns, steps):
    groups = rows * columns
    pairs = []
    for section in range(sections):
        for row in range(rows):
            for column in range(columns):
                target = stepped(row, steps[1], rows) * columns + (column + steps[2]) % columns
                below = (section + steps[0]) % sections
                pairs.append((section * groups + row * columns + column, below * groups + target))
    return lax.ppermute(value, ("section", "blk"), pairs)


def halves_of(rows):
    return rows // 2 if rows > 1 and rows & (rows - 1) == 0 else rows


def wrapped(value, count):
    return jnp.where(value >= count, value - count, value)


def sort_blocks(blocks, levels, plan):
    stride = blocks + 1
    count = plan.shape[0] // stride
    together = 4 if blocks % 4 == 0 else 1

    def place(step, ends):
        for i in range(together):
            block = step * together + i
            level = levels[block]
            for end in ends:
                plan[end] = block
            ends = tuple(end + jnp.where(level == own, 1, 0) for own, end in enumerate(ends))
        return ends

    ends = lax.fori_loop(0, blocks // together, place, tuple(jnp.int32(own * stride) for own in range(count)))
    for own, end in enumerate(ends):
        plan[own * stride + blocks] = end - own * stride


def solve_blocks(level, blocks, plan, inflow_of, kin, weight, pool):
    first = level * (blocks + 1)
    count = plan[first + blocks]
    ids = [plan[first + jnp.minimum(i, count - 1)] for i in range(blocks * 8 // 24)]
    solved = []
    for block in ids:
        mixed = jnp.dot(
            kin[block], inflow_of(block), precision=lax.Precision.HIGHEST, preferred_element_type=jnp.float32
        )
        solved.append(weight[pl.ds(block, 1), :] * mixed)
    for block, value in zip(ids, solved):
        pool[block] = value


def fill_sends(level, rows, columns, blocks, peers, downs, pool, outs):
    here = lax.axis_index("blk")
    row, column = here // columns, lax.rem(here, columns)
    ends = lax.axis_index("section") == lax.axis_size("section") - 1
    half = halves_of(rows)
    for row_step in range(rows):
        to_row = stepped(row, row_step, rows)
        for column_step in range(columns):
            target = to_row * columns + wrapped(column + column_step, columns)
            outs[column_step][row_step] = pool[jnp.where(ends, blocks, downs[level, 0, target])]
            part = outs[columns + row_step // half * columns + column_step]
            part[row_step % half] = pool[peers[level, 0, target]]


def first_level(rows, columns, *refs):
    refs = list(refs)
    levels_in, kin_in, residual_in, weight_in, peers_in, downs_in, slots_in, frac_in = (refs.pop(0) for _ in range(8))
    pool, kin, plan_out, peers_out, downs_out, slots_out, residual, weight, frac = (refs.pop(0) for _ in range(9))
    outs = [refs.pop(0) for _ in range(columns + rows // halves_of(rows) * columns)]
    plan, levels, kin_here, peers, downs, sems = refs
    pairs = [(levels_in, levels), (kin_in, kin_here), (residual_in, residual), (weight_in, weight)]
    pairs += [(peers_in, peers), (downs_in, downs)]
    pairs += [(peers_in, peers_out), (downs_in, downs_out), (slots_in, slots_out), (frac_in, frac)]
    pairs += [(plan, plan_out)]
    copies = [pltpu.make_async_copy(source, target, sems.at[i]) for i, (source, target) in enumerate(pairs)]
    for copy in copies[:-1]:
        copy.start()
    blocks = residual.shape[0]
    pool[blocks] = jnp.zeros(pool.shape[1:], pool.dtype)
    copies[0].wait()
    sort_blocks(blocks, levels, plan)
    copies[-1].start()
    copies[1].wait()
    for i in range(kin.shape[1]):
        kin[:, i, :] = jnp.transpose(kin_here[i])
    for copy in copies[2:6]:
        copy.wait()

    solve_blocks(0, blocks, plan, lambda block: residual[block], kin, weight, pool)
    fill_sends(0, rows, columns, blocks, peers, downs, pool, outs)
    for copy in copies[6:]:
        copy.wait()


def later_level(level, rows, columns, plan, peers, downs, slots, residual, weight, frac, kin, *refs):
    refs = list(refs)
    half = halves_of(rows)
    arrived = {step: refs.pop(0) for step in range(rows - 1, 0, -1)}
    from_above = [refs.pop(0) for _ in range(columns)]
    from_peers = [refs.pop(0) for _ in range(rows // half * columns)]
    refs.pop(0)
    pool = refs.pop(0)
    outs = refs
    blocks, upw = residual.shape[0], slots.shape[0]
    rounds, groups = peers.shape[0], rows * columns
    here = lax.axis_index("blk")
    row, column = here // columns, lax.rem(here, columns)
    peers_first = blocks + 1 + (level - 1) * groups
    downs_first = peers_first + rounds * groups
    for row_step in range(rows):
        from_row = stepped(row, row_step, rows, back=True)
        for column_step in range(columns):
            source = from_row * columns + wrapped(column + columns - column_step, columns)
            down = arrived[row_step].at[column_step] if row_step else from_above[column_step].at[0]
            at, rest = row_step // half * columns + column_step, row_step % half
            peer = arrived[rest].at[columns + at] if rest else from_peers[at].at[0]
            pool[downs_first + source] = down[...]
            pool[peers_first + source] = peer[...]

    def inflow_of(block):
        inflow = residual[block]
        parts = frac[block]
        for k in range(upw):
            inflow = inflow + parts[k : k + 1, :] * pool[slots[k, block]]
        return inflow

    solve_blocks(level, blocks, plan, inflow_of, kin, weight, pool)
    if level < rounds:
        fill_sends(level, rows, columns, blocks, peers, downs, pool, outs)
    else:
        outs[0][...] = pool[pl.ds(0, blocks)]


def shards(
    residual, kin_inverse, cell_weight, upwind_frac, block_level, send_in, send_down, upwind_slot
):
    blocks, species, cells = residual.shape
    sections, groups = lax.axis_size("section"), lax.axis_size("blk")
    rows, columns = split_of(groups)
    rounds = send_in.shape[1]
    peers = send_in.transpose(1, 0, 2)
    downs = send_down.transpose(1, 0, 2)
    slots = upwind_slot.transpose(1, 0)
    kin_turned = kin_inverse.transpose(1, 2, 0)
    smem = pl.BlockSpec(memory_space=pltpu.SMEM)
    vmem = pl.BlockSpec(memory_space=pltpu.VMEM)
    hbm = pl.BlockSpec(memory_space=pltpu.HBM)
    params = pltpu.CompilerParams(vmem_limit_bytes=40 * 1024 * 1024)
    pool_shape = jax.ShapeDtypeStruct((blocks + 1 + 2 * rounds * groups, species, cells), jnp.float32)
    kin_shape = jax.ShapeDtypeStruct((blocks, species, species), jnp.float32)
    half = halves_of(rows)
    send_shapes = [jax.ShapeDtypeStruct((rows, species, cells), jnp.float32)] * columns
    send_shapes += [jax.ShapeDtypeStruct((half, species, cells), jnp.float32)] * (rows // half * columns)
    to_first = (block_level, kin_turned, residual, cell_weight, peers, downs, slots, upwind_frac)
    held = (peers, downs, slots, residual, cell_weight, upwind_frac)
    held_shapes = [jax.ShapeDtypeStruct(((rounds + 1) * (blocks + 1),), jnp.int32)]
    held_shapes += [jax.ShapeDtypeStruct(x.shape, x.dtype) for x in held]
    pool, kin, *outs = pl.pallas_call(
        functools.partial(first_level, rows, columns),
        in_specs=[hbm] * len(to_first),
        out_specs=[vmem] * (2 + len(held_shapes) + len(send_shapes)),
        out_shape=[pool_shape, kin_shape] + held_shapes + send_shapes,
        scratch_shapes=[
            pltpu.SMEM(held_shapes[0].shape, jnp.int32),
            pltpu.SMEM(block_level.shape, jnp.int32),
            pltpu.VMEM(kin_turned.shape, jnp.float32),
            pltpu.SMEM(peers.shape, jnp.int32),
            pltpu.SMEM(downs.shape, jnp.int32),
            pltpu.SemaphoreType.DMA((11,)),
        ],
        compiler_params=params,
        name="first_level",
    )(*(pltpu.with_memory_space_constraint(x, pltpu.HBM) for x in to_first))
    held, outs = outs[: len(held_shapes)], outs[len(held_shapes) :]
    for level in range(1, rounds + 1):
        from_above = [moved(outs[c], sections, rows, columns, (1, 0, c)) for c in range(columns)]
        from_peers = outs[columns:]
        for at in range(1, len(from_peers)):
            steps = (0, at // columns * half, at % columns)
            from_peers[at] = moved(from_peers[at], sections, rows, columns, steps)
        arrived = []
        from_above = list(lax.optimization_barrier(tuple(from_above)))
        for step in range(rows - 1, 0, -1):
            part = [value[step] for value in from_above]
            if step < half:
                part += [value[step] for value in from_peers]
            arrived.append(moved(jnp.stack(part), sections, rows, columns, (0, step, 0)))
        if level < rounds:
            out_shapes = send_shapes
        else:
            out_shapes = [jax.ShapeDtypeStruct(residual.shape, residual.dtype)]
        operands = held + [kin] + arrived + from_above + from_peers + [pool]
        pool, *outs = pl.pallas_call(
            functools.partial(later_level, level, rows, columns),
            in_specs=[smem] * 4 + [vmem] * (len(operands) - 4),
            out_specs=[vmem] * (1 + len(out_shapes)),
            out_shape=[pool_shape] + out_shapes,
            input_output_aliases={len(operands) - 1: 0},
            compiler_params=params,
            name="later_level",
        )(*operands)
    return outs[0]


def solution(mesh):
    return jax.shard_map(
        shards,
        mesh=mesh,
        in_specs=(
            P(("section", "blk"), None, None),
            P(("section", "blk"), None, None),
            P(("section", "blk"), None),
            P(("section", "blk"), None, None),
            P(("section", "blk")),
            P(("section", "blk"), None, None),
            P(("section", "blk"), None, None),
            P(("section", "blk"), None),
        ),
        out_specs=P(("section", "blk"), None, None),
        check_vma=False,
    )
```

```python
import functools

import jax
import jax.numpy as jnp
from jax import lax
from jax.experimental import pallas as pl
from jax.experimental.pallas import tpu as pltpu
from jax.sharding import PartitionSpec as P


def split_of(groups):
    columns = max(c for c in range(1, groups + 1) if groups % c == 0 and c * c <= groups)
    return groups // columns, columns


def stepped(row, step, rows, back=False):
    if rows & (rows - 1) == 0:
        return row ^ step
    return (row + (rows - step if back else step)) % rows


def moved(value, sections, rows, columns, steps):
    groups = rows * columns
    pairs = []
    for section in range(sections):
        for row in range(rows):
            for column in range(columns):
                target = stepped(row, steps[1], rows) * columns + (column + steps[2]) % columns
                below = (section + steps[0]) % sections
                pairs.append((section * groups + row * columns + column, below * groups + target))
    return lax.ppermute(value, ("section", "blk"), pairs)


def halves_of(rows):
    return rows // 2 if rows > 1 and rows & (rows - 1) == 0 else rows


def last_steps(rows, columns):
    half = halves_of(rows)
    across = [(row, 0) for row in range(rows - 1, half - 1, -1)]
    aside = [(row, column) for row in range(half - 1, -1, -1) for column in range(1, columns)]
    return across + aside + [(row, 0) for row in range(half - 1, 0, -1)]


def wrapped(value, count):
    return jnp.where(value >= count, value - count, value)


def sort_blocks(blocks, levels, plan):
    stride = blocks + 1
    count = plan.shape[0] // stride
    ends = [jnp.int32(own * stride) for own in range(count)]
    for block in range(blocks):
        level = levels[block]
        for end in ends:
            plan[end] = block
        ends = [end + jnp.where(level == own, 1, 0) for own, end in enumerate(ends)]
    for own, end in enumerate(ends):
        plan[own * stride + blocks] = end - own * stride


def solve_blocks(level, blocks, plan, inflow_of, kin, weight, pool):
    first = level * (blocks + 1)
    count = plan[first + blocks]
    ids = [plan[first + jnp.minimum(i, count - 1)] for i in range(blocks * 8 // 24)]
    solved = []
    for block in ids:
        mixed = jnp.dot(
            kin[block], inflow_of(block), precision=lax.Precision.HIGHEST, preferred_element_type=jnp.float32
        )
        solved.append(weight[pl.ds(block, 1), :] * mixed)
    if pool is not None:
        for block, value in zip(ids, solved):
            pool[block] = value
    return count, ids, solved


def fill_sends(level, rows, columns, blocks, peers, downs, pool, outs):
    here = lax.axis_index("blk")
    row, column = here // columns, lax.rem(here, columns)
    ends = lax.axis_index("section") == lax.axis_size("section") - 1
    half = halves_of(rows)
    for row_step in range(rows):
        to_row = stepped(row, row_step, rows)
        for column_step in range(columns):
            target = to_row * columns + wrapped(column + column_step, columns)
            outs[column_step][row_step] = pool[jnp.where(ends, blocks, downs[level, 0, target])]
            part = outs[columns + row_step // half]
            part[row_step % half * columns + column_step] = pool[peers[level, 0, target]]


def first_level(rows, columns, *refs):
    refs = list(refs)
    levels_in, kin_in, residual_in, weight_in, peers_in, downs_in, slots_in, frac_in = (refs.pop(0) for _ in range(8))
    pool, kin, plan_out, peers_out, downs_out, slots_out, residual, weight, frac = (refs.pop(0) for _ in range(9))
    outs = [refs.pop(0) for _ in range(columns + rows // halves_of(rows))]
    plan, levels, kin_here, peers, downs, sems = refs
    pairs = [(levels_in, levels), (kin_in, kin_here), (residual_in, residual), (weight_in, weight)]
    pairs += [(peers_in, peers), (downs_in, downs)]
    pairs += [(peers_in, peers_out), (downs_in, downs_out), (slots_in, slots_out), (frac_in, frac)]
    pairs += [(plan, plan_out)]
    copies = [pltpu.make_async_copy(source, target, sems.at[i]) for i, (source, target) in enumerate(pairs)]
    for copy in copies[:-1]:
        copy.start()
    blocks = residual.shape[0]
    pool[blocks] = jnp.zeros(pool.shape[1:], pool.dtype)
    for copy in copies[:6]:
        copy.wait()
    sort_blocks(blocks, levels, plan)
    for i in range(kin.shape[1]):
        kin[:, i, :] = jnp.transpose(kin_here[i])
    copies[-1].start()
    solve_blocks(0, blocks, plan, lambda block: residual[block], kin, weight, pool)
    fill_sends(0, rows, columns, blocks, peers, downs, pool, outs)
    for copy in copies[6:]:
        copy.wait()


def later_level(level, rows, columns, plan, peers, downs, slots, residual, weight, frac, kin, *refs):
    refs = list(refs)
    half, steps = halves_of(rows), last_steps(rows, columns)
    arrived = {step: refs.pop(0) for step in steps}
    from_above = [refs.pop(0) for _ in range(columns)]
    from_halves = [refs.pop(0) for _ in range(rows // half)]
    refs.pop(0)
    pool = refs.pop(0)
    outs = refs
    blocks, upw = residual.shape[0], slots.shape[0]
    rounds, groups = peers.shape[0], rows * columns
    if level == rounds:
        out, last, sems = refs
        earlier = pltpu.make_async_copy(pool.at[pl.ds(0, blocks)], out, sems.at[last.shape[0]])
        earlier.start()
    here = lax.axis_index("blk")
    row, column = here // columns, lax.rem(here, columns)
    peers_first = blocks + 1 + (level - 1) * groups
    downs_first = peers_first + rounds * groups
    for row_step in range(rows):
        from_row = stepped(row, row_step, rows, back=True)
        for column_step in range(columns):
            source = from_row * columns + wrapped(column + columns - column_step, columns)
            down = arrived[row_step, 0].at[column_step] if row_step else from_above[column_step].at[0]
            at_half, rest = row_step // half, row_step % half
            if rest or column_step:
                peer = arrived[rest, column_step].at[at_half if column_step else columns + at_half]
            else:
                peer = from_halves[at_half].at[0]
            pool[downs_first + source] = down[...]
            pool[peers_first + source] = peer[...]

    def inflow_of(block):
        inflow = residual[block]
        parts = frac[block]
        for k in range(upw):
            inflow = inflow + parts[k : k + 1, :] * pool[slots[k, block]]
        return inflow

    if level < rounds:
        solve_blocks(level, blocks, plan, inflow_of, kin, weight, pool)
        fill_sends(level, rows, columns, blocks, peers, downs, pool, outs)
        return
    count, ids, solved = solve_blocks(level, blocks, plan, inflow_of, kin, weight, None)
    for i, value in enumerate(solved):
        last[i] = value
    copies = [pltpu.make_async_copy(last.at[i], out.at[block], sems.at[i]) for i, block in enumerate(ids)]
    earlier.wait()
    for i, copy in enumerate(copies):
        pl.when(i < count)(copy.start)
    for i, copy in enumerate(copies):
        pl.when(i < count)(copy.wait)


def shards(
    residual, kin_inverse, cell_weight, upwind_frac, block_level, send_in, send_down, upwind_slot
):
    blocks, species, cells = residual.shape
    sections, groups = lax.axis_size("section"), lax.axis_size("blk")
    rows, columns = split_of(groups)
    rounds = send_in.shape[1]
    peers = send_in.transpose(1, 0, 2)
    downs = send_down.transpose(1, 0, 2)
    slots = upwind_slot.transpose(1, 0)
    kin_turned = kin_inverse.transpose(1, 2, 0)
    smem = pl.BlockSpec(memory_space=pltpu.SMEM)
    vmem = pl.BlockSpec(memory_space=pltpu.VMEM)
    hbm = pl.BlockSpec(memory_space=pltpu.HBM)
    params = pltpu.CompilerParams(vmem_limit_bytes=40 * 1024 * 1024)
    pool_shape = jax.ShapeDtypeStruct((blocks + 1 + 2 * rounds * groups, species, cells), jnp.float32)
    kin_shape = jax.ShapeDtypeStruct((blocks, species, species), jnp.float32)
    half = halves_of(rows)
    send_shapes = [jax.ShapeDtypeStruct((rows, species, cells), jnp.float32)] * columns
    send_shapes += [jax.ShapeDtypeStruct((half * columns, species, cells), jnp.float32)] * (rows // half)
    to_first = (block_level, kin_turned, residual, cell_weight, peers, downs, slots, upwind_frac)
    held = (peers, downs, slots, residual, cell_weight, upwind_frac)
    held_shapes = [jax.ShapeDtypeStruct(((rounds + 1) * (blocks + 1),), jnp.int32)]
    held_shapes += [jax.ShapeDtypeStruct(x.shape, x.dtype) for x in held]
    pool, kin, *outs = pl.pallas_call(
        functools.partial(first_level, rows, columns),
        in_specs=[hbm] * len(to_first),
        out_specs=[vmem] * (2 + len(held_shapes) + len(send_shapes)),
        out_shape=[pool_shape, kin_shape] + held_shapes + send_shapes,
        scratch_shapes=[
            pltpu.SMEM(held_shapes[0].shape, jnp.int32),
            pltpu.SMEM(block_level.shape, jnp.int32),
            pltpu.VMEM(kin_turned.shape, jnp.float32),
            pltpu.SMEM(peers.shape, jnp.int32),
            pltpu.SMEM(downs.shape, jnp.int32),
            pltpu.SemaphoreType.DMA((11,)),
        ],
        compiler_params=params,
        name="first_level",
    )(*(pltpu.with_memory_space_constraint(x, pltpu.HBM) for x in to_first))
    held, outs = outs[: len(held_shapes)], outs[len(held_shapes) :]
    for level in range(1, rounds + 1):
        from_halves = outs[columns:]
        if half < rows:
            from_halves[1] = moved(from_halves[1], sections, rows, columns, (0, half, 0))
        from_above = [moved(outs[c], sections, rows, columns, (1, 0, c)) for c in range(columns)]
        arrived = []
        for row, column in last_steps(rows, columns):
            part = [] if column else [value[row] for value in from_above]
            if row < half:
                part += [value[row * columns + column] for value in from_halves]
            arrived.append(moved(jnp.stack(part), sections, rows, columns, (0, row, column)))
        if level < rounds:
            out_shapes = send_shapes
        else:
            out_shapes = [jax.ShapeDtypeStruct(residual.shape, residual.dtype)]
        operands = held + [kin] + arrived + from_above + from_halves + [pool]
        own = blocks * 8 // 24
        pool, *outs = pl.pallas_call(
            functools.partial(later_level, level, rows, columns),
            in_specs=[smem] * 4 + [vmem] * (len(operands) - 4),
            out_specs=[vmem] + [vmem if level < rounds else hbm] * len(out_shapes),
            out_shape=[pool_shape] + out_shapes,
            scratch_shapes=[]
            if level < rounds
            else [pltpu.VMEM((own, species, cells), jnp.float32), pltpu.SemaphoreType.DMA((own + 1,))],
            input_output_aliases={len(operands) - 1: 0},
            compiler_params=params,
            name="later_level",
        )(*operands)
    return outs[0]


def solution(mesh):
    return jax.shard_map(
        shards,
        mesh=mesh,
        in_specs=(
            P(("section", "blk"), None, None),
            P(("section", "blk"), None, None),
            P(("section", "blk"), None),
            P(("section", "blk"), None, None),
            P(("section", "blk")),
            P(("section", "blk"), None, None),
            P(("section", "blk"), None, None),
            P(("section", "blk"), None),
        ),
        out_specs=P(("section", "blk"), None, None),
        check_vma=False,
    )
```

```python
import functools

import jax
import jax.numpy as jnp
from jax import lax
from jax.experimental import pallas as pl
from jax.experimental.pallas import tpu as pltpu
from jax.sharding import PartitionSpec as P


def split_of(groups):
    columns = max(c for c in range(1, groups + 1) if groups % c == 0 and c * c <= groups)
    return groups // columns, columns


def stepped(row, step, rows, back=False):
    if rows & (rows - 1) == 0:
        return row ^ step
    return (row + (rows - step if back else step)) % rows


def moved(value, sections, rows, columns, steps):
    groups = rows * columns
    pairs = []
    for section in range(sections):
        for row in range(rows):
            for column in range(columns):
                target = stepped(row, steps[1], rows) * columns + (column + steps[2]) % columns
                below = (section + steps[0]) % sections
                pairs.append((section * groups + row * columns + column, below * groups + target))
    return lax.ppermute(value, ("section", "blk"), pairs)


def halves_of(rows):
    return rows // 2 if rows > 1 and rows & (rows - 1) == 0 else rows


def last_steps(rows, columns):
    half = halves_of(rows)
    across = [(row, 0) for row in range(rows - 1, half - 1, -1)]
    aside = [(row, column) for row in range(half - 1, -1, -1) for column in range(1, columns)]
    return across + aside + [(row, 0) for row in range(half - 1, 0, -1)]


def wrapped(value, count):
    return jnp.where(value >= count, value - count, value)


def sort_blocks(blocks, levels, plan):
    stride = blocks + 1
    count = plan.shape[0] // stride
    together = 4 if blocks % 4 == 0 else 1

    def place(step, ends):
        for i in range(together):
            block = step * together + i
            level = levels[block]
            for end in ends:
                plan[end] = block
            ends = tuple(end + jnp.where(level == own, 1, 0) for own, end in enumerate(ends))
        return ends

    ends = lax.fori_loop(0, blocks // together, place, tuple(jnp.int32(own * stride) for own in range(count)))
    for own, end in enumerate(ends):
        plan[own * stride + blocks] = end - own * stride


def solve_blocks(level, blocks, plan, inflow_of, kin, weight, pool):
    first = level * (blocks + 1)
    count = plan[first + blocks]
    ids = [plan[first + jnp.minimum(i, count - 1)] for i in range(blocks * 8 // 24)]
    solved = []
    for block in ids:
        mixed = jnp.dot(
            kin[block], inflow_of(block), precision=lax.Precision.HIGH, preferred_element_type=jnp.float32
        )
        solved.append(weight[pl.ds(block, 1), :] * mixed)
    for block, value in zip(ids, solved):
        pool[block] = value


def fill_sends(level, rows, columns, blocks, peers, downs, pool, outs):
    here = lax.axis_index("blk")
    row, column = here // columns, lax.rem(here, columns)
    ends = lax.axis_index("section") == lax.axis_size("section") - 1
    half = halves_of(rows)
    for row_step in range(rows):
        to_row = stepped(row, row_step, rows)
        for column_step in range(columns):
            target = to_row * columns + wrapped(column + column_step, columns)
            outs[column_step][row_step] = pool[jnp.where(ends, blocks, downs[level, 0, target])]
            part = outs[columns + row_step // half]
            part[row_step % half * columns + column_step] = pool[peers[level, 0, target]]


def first_level(rows, columns, *refs):
    refs = list(refs)
    levels_in, kin_in, residual_in, weight_in, peers_in, downs_in, slots_in, frac_in = (refs.pop(0) for _ in range(8))
    pool, kin, plan_out, peers_out, downs_out, slots_out, residual, weight, frac = (refs.pop(0) for _ in range(9))
    outs = [refs.pop(0) for _ in range(columns + rows // halves_of(rows))]
    plan, levels, kin_here, peers, downs, sems = refs
    pairs = [(levels_in, levels), (kin_in, kin_here), (residual_in, residual), (weight_in, weight)]
    pairs += [(peers_in, peers), (downs_in, downs)]
    pairs += [(peers_in, peers_out), (downs_in, downs_out), (slots_in, slots_out), (frac_in, frac)]
    pairs += [(plan, plan_out)]
    copies = [pltpu.make_async_copy(source, target, sems.at[i]) for i, (source, target) in enumerate(pairs)]
    for copy in copies[:-1]:
        copy.start()
    blocks = residual.shape[0]
    pool[blocks] = jnp.zeros(pool.shape[1:], pool.dtype)
    copies[0].wait()
    sort_blocks(blocks, levels, plan)
    copies[-1].start()
    copies[1].wait()
    for i in range(kin.shape[1]):
        kin[:, i, :] = jnp.transpose(kin_here[i])
    for copy in copies[2:6]:
        copy.wait()

    solve_blocks(0, blocks, plan, lambda block: residual[block], kin, weight, pool)
    fill_sends(0, rows, columns, blocks, peers, downs, pool, outs)
    for copy in copies[6:]:
        copy.wait()


def later_level(level, rows, columns, plan, peers, downs, slots, residual, weight, frac, kin, *refs):
    refs = list(refs)
    half, steps = halves_of(rows), last_steps(rows, columns)
    arrived = {step: refs.pop(0) for step in steps}
    from_above = [refs.pop(0) for _ in range(columns)]
    from_halves = [refs.pop(0) for _ in range(rows // half)]
    refs.pop(0)
    pool = refs.pop(0)
    outs = refs
    blocks, upw = residual.shape[0], slots.shape[0]
    rounds, groups = peers.shape[0], rows * columns
    here = lax.axis_index("blk")
    row, column = here // columns, lax.rem(here, columns)
    peers_first = blocks + 1 + (level - 1) * groups
    downs_first = peers_first + rounds * groups
    for row_step in range(rows):
        from_row = stepped(row, row_step, rows, back=True)
        for column_step in range(columns):
            source = from_row * columns + wrapped(column + columns - column_step, columns)
            down = arrived[row_step, 0].at[column_step] if row_step else from_above[column_step].at[0]
            at_half, rest = row_step // half, row_step % half
            if rest or column_step:
                peer = arrived[rest, column_step].at[at_half if column_step else columns + at_half]
            else:
                peer = from_halves[at_half].at[0]
            pool[downs_first + source] = down[...]
            pool[peers_first + source] = peer[...]

    def inflow_of(block):
        inflow = residual[block]
        parts = frac[block]
        for k in range(upw):
            inflow = inflow + parts[k : k + 1, :] * pool[slots[k, block]]
        return inflow

    solve_blocks(level, blocks, plan, inflow_of, kin, weight, pool)
    if level < rounds:
        fill_sends(level, rows, columns, blocks, peers, downs, pool, outs)
    else:
        outs[0][...] = pool[pl.ds(0, blocks)]


def shards(
    residual, kin_inverse, cell_weight, upwind_frac, block_level, send_in, send_down, upwind_slot
):
    blocks, species, cells = residual.shape
    sections, groups = lax.axis_size("section"), lax.axis_size("blk")
    rows, columns = split_of(groups)
    rounds = send_in.shape[1]
    peers = send_in.transpose(1, 0, 2)
    downs = send_down.transpose(1, 0, 2)
    slots = upwind_slot.transpose(1, 0)
    kin_turned = kin_inverse.transpose(1, 2, 0)
    smem = pl.BlockSpec(memory_space=pltpu.SMEM)
    vmem = pl.BlockSpec(memory_space=pltpu.VMEM)
    hbm = pl.BlockSpec(memory_space=pltpu.HBM)
    params = pltpu.CompilerParams(vmem_limit_bytes=40 * 1024 * 1024)
    pool_shape = jax.ShapeDtypeStruct((blocks + 1 + 2 * rounds * groups, species, cells), jnp.float32)
    kin_shape = jax.ShapeDtypeStruct((blocks, species, species), jnp.float32)
    half = halves_of(rows)
    send_shapes = [jax.ShapeDtypeStruct((rows, species, cells), jnp.float32)] * columns
    send_shapes += [jax.ShapeDtypeStruct((half * columns, species, cells), jnp.float32)] * (rows // half)
    to_first = (block_level, kin_turned, residual, cell_weight, peers, downs, slots, upwind_frac)
    held = (peers, downs, slots, residual, cell_weight, upwind_frac)
    held_shapes = [jax.ShapeDtypeStruct(((rounds + 1) * (blocks + 1),), jnp.int32)]
    held_shapes += [jax.ShapeDtypeStruct(x.shape, x.dtype) for x in held]
    pool, kin, *outs = pl.pallas_call(
        functools.partial(first_level, rows, columns),
        in_specs=[hbm] * len(to_first),
        out_specs=[vmem] * (2 + len(held_shapes) + len(send_shapes)),
        out_shape=[pool_shape, kin_shape] + held_shapes + send_shapes,
        scratch_shapes=[
            pltpu.SMEM(held_shapes[0].shape, jnp.int32),
            pltpu.SMEM(block_level.shape, jnp.int32),
            pltpu.VMEM(kin_turned.shape, jnp.float32),
            pltpu.SMEM(peers.shape, jnp.int32),
            pltpu.SMEM(downs.shape, jnp.int32),
            pltpu.SemaphoreType.DMA((11,)),
        ],
        compiler_params=params,
        name="first_level",
    )(*(pltpu.with_memory_space_constraint(x, pltpu.HBM) for x in to_first))
    held, outs = outs[: len(held_shapes)], outs[len(held_shapes) :]
    for level in range(1, rounds + 1):
        from_halves = outs[columns:]
        if half < rows:
            from_halves[1] = moved(from_halves[1], sections, rows, columns, (0, half, 0))
        from_above = [moved(outs[c], sections, rows, columns, (1, 0, c)) for c in range(columns)]
        arrived = []
        for row, column in last_steps(rows, columns):
            part = [] if column else [value[row] for value in from_above]
            if row < half:
                part += [value[row * columns + column] for value in from_halves]
            arrived.append(moved(jnp.stack(part), sections, rows, columns, (0, row, column)))
        if level < rounds:
            out_shapes = send_shapes
        else:
            out_shapes = [jax.ShapeDtypeStruct(residual.shape, residual.dtype)]
        operands = held + [kin] + arrived + from_above + from_halves + [pool]
        pool, *outs = pl.pallas_call(
            functools.partial(later_level, level, rows, columns),
            in_specs=[smem] * 4 + [vmem] * (len(operands) - 4),
            out_specs=[vmem] * (1 + len(out_shapes)),
            out_shape=[pool_shape] + out_shapes,
            input_output_aliases={len(operands) - 1: 0},
            compiler_params=params,
            name="later_level",
        )(*operands)
    return outs[0]


def solution(mesh):
    return jax.shard_map(
        shards,
        mesh=mesh,
        in_specs=(
            P(("section", "blk"), None, None),
            P(("section", "blk"), None, None),
            P(("section", "blk"), None),
            P(("section", "blk"), None, None),
            P(("section", "blk")),
            P(("section", "blk"), None, None),
            P(("section", "blk"), None, None),
            P(("section", "blk"), None),
        ),
        out_specs=P(("section", "blk"), None, None),
        check_vma=False,
    )
```

```python
import functools

import jax
import jax.numpy as jnp
from jax import lax
from jax.experimental import pallas as pl
from jax.experimental.pallas import tpu as pltpu
from jax.sharding import PartitionSpec as P


def split_of(groups):
    columns = max(c for c in range(1, groups + 1) if groups % c == 0 and c * c <= groups)
    return groups // columns, columns


def stepped(row, step, rows, back=False):
    if rows & (rows - 1) == 0:
        return row ^ step
    return (row + (rows - step if back else step)) % rows


def moved(value, sections, rows, columns, steps):
    groups = rows * columns
    pairs = []
    for section in range(sections):
        for row in range(rows):
            for column in range(columns):
                target = stepped(row, steps[1], rows) * columns + (column + steps[2]) % columns
                below = (section + steps[0]) % sections
                pairs.append((section * groups + row * columns + column, below * groups + target))
    return lax.ppermute(value, ("section", "blk"), pairs)


def halves_of(rows):
    return rows // 2 if rows > 1 and rows & (rows - 1) == 0 else rows


def last_steps(rows, columns):
    half = halves_of(rows)
    across = [(row, 0) for row in range(rows - 1, half - 1, -1)]
    aside = [(row, column) for row in range(half - 1, -1, -1) for column in range(1, columns)]
    return across + aside + [(row, 0) for row in range(half - 1, 0, -1)]


def wrapped(value, count):
    return jnp.where(value >= count, value - count, value)


def sort_blocks(blocks, levels, plan):
    stride = blocks + 1
    count = plan.shape[0] // stride
    together = 4 if blocks % 4 == 0 else 1

    def place(step, ends):
        for i in range(together):
            block = step * together + i
            level = levels[block]
            for end in ends:
                plan[end] = block
            ends = tuple(end + jnp.where(level == own, 1, 0) for own, end in enumerate(ends))
        return ends

    ends = lax.fori_loop(0, blocks // together, place, tuple(jnp.int32(own * stride) for own in range(count)))
    for own, end in enumerate(ends):
        plan[own * stride + blocks] = end - own * stride


def solve_blocks(level, blocks, plan, inflow_of, kin, weight, pool):
    first = level * (blocks + 1)
    count = plan[first + blocks]
    ids = [plan[first + jnp.minimum(i, count - 1)] for i in range(blocks * 8 // 24)]
    solved = []
    for block in ids:
        mixed = jnp.dot(
            kin[block], inflow_of(block), precision=lax.Precision.HIGH, preferred_element_type=jnp.float32
        )
        solved.append(weight[pl.ds(block, 1), :] * mixed)
    for block, value in zip(ids, solved):
        pool[block] = value


def fill_sends(level, rows, columns, blocks, peers, downs, pool, outs):
    here = lax.axis_index("blk")
    row, column = here // columns, lax.rem(here, columns)
    ends = lax.axis_index("section") == lax.axis_size("section") - 1
    half = halves_of(rows)
    for row_step in range(rows):
        to_row = stepped(row, row_step, rows)
        for column_step in range(columns):
            target = to_row * columns + wrapped(column + column_step, columns)
            outs[columns - 1 - column_step][row_step] = pool[jnp.where(ends, blocks, downs[level, 0, target])]
            part = outs[columns + row_step // half]
            part[row_step % half * columns + column_step] = pool[peers[level, 0, target]]


def first_level(rows, columns, *refs):
    refs = list(refs)
    levels_in, kin_in, residual_in, weight_in, peers_in, downs_in, slots_in, frac_in = (refs.pop(0) for _ in range(8))
    pool, kin, plan_out, peers_out, downs_out, slots_out, residual, weight, frac = (refs.pop(0) for _ in range(9))
    outs = [refs.pop(0) for _ in range(columns + rows // halves_of(rows))]
    plan, levels, kin_here, peers, downs, sems = refs
    pairs = [(levels_in, levels), (kin_in, kin_here), (residual_in, residual), (weight_in, weight)]
    pairs += [(peers_in, peers), (downs_in, downs)]
    pairs += [(peers_in, peers_out), (downs_in, downs_out), (slots_in, slots_out), (frac_in, frac)]
    pairs += [(plan, plan_out)]
    copies = [pltpu.make_async_copy(source, target, sems.at[i]) for i, (source, target) in enumerate(pairs)]
    for copy in copies[:-1]:
        copy.start()
    blocks = residual.shape[0]
    pool[blocks] = jnp.zeros(pool.shape[1:], pool.dtype)
    copies[0].wait()
    sort_blocks(blocks, levels, plan)
    copies[-1].start()
    copies[1].wait()
    for i in range(kin.shape[1]):
        kin[:, i, :] = jnp.transpose(kin_here[i])
    for copy in copies[2:6]:
        copy.wait()

    solve_blocks(0, blocks, plan, lambda block: residual[block], kin, weight, pool)
    fill_sends(0, rows, columns, blocks, peers, downs, pool, outs)
    for copy in copies[6:]:
        copy.wait()


def later_level(level, rows, columns, plan, peers, downs, slots, residual, weight, frac, kin, *refs):
    refs = list(refs)
    half, steps = halves_of(rows), last_steps(rows, columns)
    arrived = {step: refs.pop(0) for step in steps}
    from_above = [refs.pop(0) for _ in range(columns)]
    from_halves = [refs.pop(0) for _ in range(rows // half)]
    refs.pop(0)
    pool = refs.pop(0)
    outs = refs
    blocks, upw = residual.shape[0], slots.shape[0]
    rounds, groups = peers.shape[0], rows * columns
    here = lax.axis_index("blk")
    row, column = here // columns, lax.rem(here, columns)
    peers_first = blocks + 1 + (level - 1) * groups
    downs_first = peers_first + rounds * groups
    for row_step in range(rows):
        from_row = stepped(row, row_step, rows, back=True)
        for column_step in range(columns):
            source = from_row * columns + wrapped(column + columns - column_step, columns)
            at_column = columns - 1 - column_step
            down = arrived[row_step, 0].at[at_column] if row_step else from_above[at_column].at[0]
            at_half, rest = row_step // half, row_step % half
            if rest or column_step:
                peer = arrived[rest, column_step].at[at_half if column_step else columns + at_half]
            else:
                peer = from_halves[at_half].at[0]
            pool[downs_first + source] = down[...]
            pool[peers_first + source] = peer[...]

    def inflow_of(block):
        inflow = residual[block]
        parts = frac[block]
        for k in range(upw):
            inflow = inflow + parts[k : k + 1, :] * pool[slots[k, block]]
        return inflow

    solve_blocks(level, blocks, plan, inflow_of, kin, weight, pool)
    if level < rounds:
        fill_sends(level, rows, columns, blocks, peers, downs, pool, outs)
    else:
        outs[0][...] = pool[pl.ds(0, blocks)]


def shards(
    residual, kin_inverse, cell_weight, upwind_frac, block_level, send_in, send_down, upwind_slot
):
    blocks, species, cells = residual.shape
    sections, groups = lax.axis_size("section"), lax.axis_size("blk")
    rows, columns = split_of(groups)
    rounds = send_in.shape[1]
    peers = send_in.transpose(1, 0, 2)
    downs = send_down.transpose(1, 0, 2)
    slots = upwind_slot.transpose(1, 0)
    kin_turned = kin_inverse.transpose(1, 2, 0)
    smem = pl.BlockSpec(memory_space=pltpu.SMEM)
    vmem = pl.BlockSpec(memory_space=pltpu.VMEM)
    hbm = pl.BlockSpec(memory_space=pltpu.HBM)
    params = pltpu.CompilerParams(vmem_limit_bytes=40 * 1024 * 1024)
    pool_shape = jax.ShapeDtypeStruct((blocks + 1 + 2 * rounds * groups, species, cells), jnp.float32)
    kin_shape = jax.ShapeDtypeStruct((blocks, species, species), jnp.float32)
    half = halves_of(rows)
    send_shapes = [jax.ShapeDtypeStruct((rows, species, cells), jnp.float32)] * columns
    send_shapes += [jax.ShapeDtypeStruct((half * columns, species, cells), jnp.float32)] * (rows // half)
    to_first = (block_level, kin_turned, residual, cell_weight, peers, downs, slots, upwind_frac)
    held = (peers, downs, slots, residual, cell_weight, upwind_frac)
    held_shapes = [jax.ShapeDtypeStruct(((rounds + 1) * (blocks + 1),), jnp.int32)]
    held_shapes += [jax.ShapeDtypeStruct(x.shape, x.dtype) for x in held]
    pool, kin, *outs = pl.pallas_call(
        functools.partial(first_level, rows, columns),
        in_specs=[hbm] * len(to_first),
        out_specs=[vmem] * (2 + len(held_shapes) + len(send_shapes)),
        out_shape=[pool_shape, kin_shape] + held_shapes + send_shapes,
        scratch_shapes=[
            pltpu.SMEM(held_shapes[0].shape, jnp.int32),
            pltpu.SMEM(block_level.shape, jnp.int32),
            pltpu.VMEM(kin_turned.shape, jnp.float32),
            pltpu.SMEM(peers.shape, jnp.int32),
            pltpu.SMEM(downs.shape, jnp.int32),
            pltpu.SemaphoreType.DMA((11,)),
        ],
        compiler_params=params,
        name="first_level",
    )(*(pltpu.with_memory_space_constraint(x, pltpu.HBM) for x in to_first))
    held, outs = outs[: len(held_shapes)], outs[len(held_shapes) :]
    for level in range(1, rounds + 1):
        from_halves = outs[columns:]
        if half < rows:
            from_halves[1] = moved(from_halves[1], sections, rows, columns, (0, half, 0))
        from_above = [moved(outs[c], sections, rows, columns, (1, 0, columns - 1 - c)) for c in range(columns)]
        arrived = []
        for row, column in last_steps(rows, columns):
            part = [] if column else [value[row] for value in from_above]
            if row < half:
                part += [value[row * columns + column] for value in from_halves]
            arrived.append(moved(jnp.stack(part), sections, rows, columns, (0, row, column)))
        if level < rounds:
            out_shapes = send_shapes
        else:
            out_shapes = [jax.ShapeDtypeStruct(residual.shape, residual.dtype)]
        operands = held + [kin] + arrived + from_above + from_halves + [pool]
        pool, *outs = pl.pallas_call(
            functools.partial(later_level, level, rows, columns),
            in_specs=[smem] * 4 + [vmem] * (len(operands) - 4),
            out_specs=[vmem] * (1 + len(out_shapes)),
            out_shape=[pool_shape] + out_shapes,
            input_output_aliases={len(operands) - 1: 0},
            compiler_params=params,
            name="later_level",
        )(*operands)
    return outs[0]


def solution(mesh):
    return jax.shard_map(
        shards,
        mesh=mesh,
        in_specs=(
            P(("section", "blk"), None, None),
            P(("section", "blk"), None, None),
            P(("section", "blk"), None),
            P(("section", "blk"), None, None),
            P(("section", "blk")),
            P(("section", "blk"), None, None),
            P(("section", "blk"), None, None),
            P(("section", "blk"), None),
        ),
        out_specs=P(("section", "blk"), None, None),
        check_vma=False,
    )
```

```python
import functools

import jax
import jax.numpy as jnp
from jax import lax
from jax.experimental import pallas as pl
from jax.experimental.pallas import tpu as pltpu
from jax.sharding import PartitionSpec as P


def split_of(groups):
    rows = 2 if groups % 2 == 0 else 1
    return rows, groups // rows


def stepped(row, step, rows, back=False):
    if rows & (rows - 1) == 0:
        return row ^ step
    return (row + (rows - step if back else step)) % rows


def moved(value, sections, rows, columns, steps):
    groups = rows * columns
    pairs = []
    for section in range(sections):
        for row in range(rows):
            for column in range(columns):
                target = stepped(row, steps[1], rows) * columns + stepped(column, steps[2], columns)
                below = (section + steps[0]) % sections
                pairs.append((section * groups + row * columns + column, below * groups + target))
    return lax.ppermute(value, ("section", "blk"), pairs)


def halves_of(rows):
    return rows // 2 if rows > 1 and rows & (rows - 1) == 0 else rows


def last_steps(rows, columns):
    half = halves_of(rows)
    across = [(row, 0) for row in range(rows - 1, half - 1, -1)]
    aside = [(row, column) for row in range(half - 1, -1, -1) for column in range(1, columns)]
    return across + aside + [(row, 0) for row in range(half - 1, 0, -1)]


def sort_blocks(blocks, levels, plan):
    stride = blocks + 1
    count = plan.shape[0] // stride
    together = 4 if blocks % 4 == 0 else 1

    def place(step, ends):
        for i in range(together):
            block = step * together + i
            level = levels[block]
            for end in ends:
                plan[end] = block
            ends = tuple(end + jnp.where(level == own, 1, 0) for own, end in enumerate(ends))
        return ends

    ends = lax.fori_loop(0, blocks // together, place, tuple(jnp.int32(own * stride) for own in range(count)))
    for own, end in enumerate(ends):
        plan[own * stride + blocks] = end - own * stride


def solve_blocks(level, blocks, plan, inflow_of, kin, weight, pool):
    first = level * (blocks + 1)
    count = plan[first + blocks]
    ids = [plan[first + jnp.minimum(i, count - 1)] for i in range(blocks * 8 // 24)]
    solved = []
    for block in ids:
        mixed = jnp.dot(
            kin[block], inflow_of(block), precision=lax.Precision.HIGH, preferred_element_type=jnp.float32
        )
        solved.append(weight[pl.ds(block, 1), :] * mixed)
    for block, value in zip(ids, solved):
        pool[block] = value


def fill_sends(level, rows, columns, blocks, peers, downs, pool, outs):
    here = lax.axis_index("blk")
    row, column = here // columns, lax.rem(here, columns)
    ends = lax.axis_index("section") == lax.axis_size("section") - 1
    half = halves_of(rows)
    for row_step in range(rows):
        to_row = stepped(row, row_step, rows)
        for column_step in range(columns):
            target = to_row * columns + stepped(column, column_step, columns)
            outs[column_step][row_step] = pool[jnp.where(ends, blocks, downs[level, 0, target])]
            part = outs[columns + row_step // half]
            part[row_step % half * columns + column_step] = pool[peers[level, 0, target]]


def first_level(rows, columns, *refs):
    refs = list(refs)
    levels_in, kin_in, residual_in, weight_in, peers_in, downs_in, slots_in, frac_in = (refs.pop(0) for _ in range(8))
    pool, kin, plan_out, peers_out, downs_out, slots_out, residual, weight, frac = (refs.pop(0) for _ in range(9))
    outs = [refs.pop(0) for _ in range(columns + rows // halves_of(rows))]
    plan, levels, kin_here, peers, downs, sems = refs
    pairs = [(levels_in, levels), (kin_in, kin_here), (residual_in, residual), (weight_in, weight)]
    pairs += [(peers_in, peers), (downs_in, downs)]
    pairs += [(peers_in, peers_out), (downs_in, downs_out), (slots_in, slots_out), (frac_in, frac)]
    pairs += [(plan, plan_out)]
    copies = [pltpu.make_async_copy(source, target, sems.at[i]) for i, (source, target) in enumerate(pairs)]
    for copy in copies[:-1]:
        copy.start()
    blocks = residual.shape[0]
    pool[blocks] = jnp.zeros(pool.shape[1:], pool.dtype)
    copies[0].wait()
    sort_blocks(blocks, levels, plan)
    copies[-1].start()
    copies[1].wait()
    for i in range(kin.shape[1]):
        kin[:, i, :] = jnp.transpose(kin_here[i])
    for copy in copies[2:6]:
        copy.wait()

    solve_blocks(0, blocks, plan, lambda block: residual[block], kin, weight, pool)
    fill_sends(0, rows, columns, blocks, peers, downs, pool, outs)
    for copy in copies[6:]:
        copy.wait()


def later_level(level, rows, columns, plan, peers, downs, slots, residual, weight, frac, kin, *refs):
    refs = list(refs)
    half, steps = halves_of(rows), last_steps(rows, columns)
    arrived = {step: refs.pop(0) for step in steps}
    from_above = [refs.pop(0) for _ in range(columns)]
    from_halves = [refs.pop(0) for _ in range(rows // half)]
    refs.pop(0)
    pool = refs.pop(0)
    outs = refs
    blocks, upw = residual.shape[0], slots.shape[0]
    rounds, groups = peers.shape[0], rows * columns
    here = lax.axis_index("blk")
    row, column = here // columns, lax.rem(here, columns)
    peers_first = blocks + 1 + (level - 1) * groups
    downs_first = peers_first + rounds * groups
    for row_step in range(rows):
        from_row = stepped(row, row_step, rows, back=True)
        for column_step in range(columns):
            source = from_row * columns + stepped(column, column_step, columns, back=True)
            down = arrived[row_step, 0].at[column_step] if row_step else from_above[column_step].at[0]
            at_half, rest = row_step // half, row_step % half
            if rest or column_step:
                peer = arrived[rest, column_step].at[at_half if column_step else columns + at_half]
            else:
                peer = from_halves[at_half].at[0]
            pool[downs_first + source] = down[...]
            pool[peers_first + source] = peer[...]

    def inflow_of(block):
        inflow = residual[block]
        parts = frac[block]
        for k in range(upw):
            inflow = inflow + parts[k : k + 1, :] * pool[slots[k, block]]
        return inflow

    solve_blocks(level, blocks, plan, inflow_of, kin, weight, pool)
    if level < rounds:
        fill_sends(level, rows, columns, blocks, peers, downs, pool, outs)
    else:
        outs[0][...] = pool[pl.ds(0, blocks)]


def shards(
    residual, kin_inverse, cell_weight, upwind_frac, block_level, send_in, send_down, upwind_slot
):
    blocks, species, cells = residual.shape
    sections, groups = lax.axis_size("section"), lax.axis_size("blk")
    rows, columns = split_of(groups)
    rounds = send_in.shape[1]
    peers = send_in.transpose(1, 0, 2)
    downs = send_down.transpose(1, 0, 2)
    slots = upwind_slot.transpose(1, 0)
    kin_turned = kin_inverse.transpose(1, 2, 0)
    smem = pl.BlockSpec(memory_space=pltpu.SMEM)
    vmem = pl.BlockSpec(memory_space=pltpu.VMEM)
    hbm = pl.BlockSpec(memory_space=pltpu.HBM)
    params = pltpu.CompilerParams(vmem_limit_bytes=40 * 1024 * 1024)
    pool_shape = jax.ShapeDtypeStruct((blocks + 1 + 2 * rounds * groups, species, cells), jnp.float32)
    kin_shape = jax.ShapeDtypeStruct((blocks, species, species), jnp.float32)
    half = halves_of(rows)
    send_shapes = [jax.ShapeDtypeStruct((rows, species, cells), jnp.float32)] * columns
    send_shapes += [jax.ShapeDtypeStruct((half * columns, species, cells), jnp.float32)] * (rows // half)
    to_first = (block_level, kin_turned, residual, cell_weight, peers, downs, slots, upwind_frac)
    held = (peers, downs, slots, residual, cell_weight, upwind_frac)
    held_shapes = [jax.ShapeDtypeStruct(((rounds + 1) * (blocks + 1),), jnp.int32)]
    held_shapes += [jax.ShapeDtypeStruct(x.shape, x.dtype) for x in held]
    pool, kin, *outs = pl.pallas_call(
        functools.partial(first_level, rows, columns),
        in_specs=[hbm] * len(to_first),
        out_specs=[vmem] * (2 + len(held_shapes) + len(send_shapes)),
        out_shape=[pool_shape, kin_shape] + held_shapes + send_shapes,
        scratch_shapes=[
            pltpu.SMEM(held_shapes[0].shape, jnp.int32),
            pltpu.SMEM(block_level.shape, jnp.int32),
            pltpu.VMEM(kin_turned.shape, jnp.float32),
            pltpu.SMEM(peers.shape, jnp.int32),
            pltpu.SMEM(downs.shape, jnp.int32),
            pltpu.SemaphoreType.DMA((11,)),
        ],
        compiler_params=params,
        name="first_level",
    )(*(pltpu.with_memory_space_constraint(x, pltpu.HBM) for x in to_first))
    held, outs = outs[: len(held_shapes)], outs[len(held_shapes) :]
    for level in range(1, rounds + 1):
        from_halves = outs[columns:]
        if half < rows:
            from_halves[1] = moved(from_halves[1], sections, rows, columns, (0, half, 0))
        from_above = [moved(outs[c], sections, rows, columns, (1, 0, c)) for c in range(columns)]
        arrived = []
        for row, column in last_steps(rows, columns):
            part = [] if column else [value[row] for value in from_above]
            if row < half:
                part += [value[row * columns + column] for value in from_halves]
            arrived.append(moved(jnp.stack(part), sections, rows, columns, (0, row, column)))
        if level < rounds:
            out_shapes = send_shapes
        else:
            out_shapes = [jax.ShapeDtypeStruct(residual.shape, residual.dtype)]
        operands = held + [kin] + arrived + from_above + from_halves + [pool]
        pool, *outs = pl.pallas_call(
            functools.partial(later_level, level, rows, columns),
            in_specs=[smem] * 4 + [vmem] * (len(operands) - 4),
            out_specs=[vmem] * (1 + len(out_shapes)),
            out_shape=[pool_shape] + out_shapes,
            input_output_aliases={len(operands) - 1: 0},
            compiler_params=params,
            name="later_level",
        )(*operands)
    return outs[0]


def solution(mesh):
    return jax.shard_map(
        shards,
        mesh=mesh,
        in_specs=(
            P(("section", "blk"), None, None),
            P(("section", "blk"), None, None),
            P(("section", "blk"), None),
            P(("section", "blk"), None, None),
            P(("section", "blk")),
            P(("section", "blk"), None, None),
            P(("section", "blk"), None, None),
            P(("section", "blk"), None),
        ),
        out_specs=P(("section", "blk"), None, None),
        check_vma=False,
    )
```

```python
import functools

import jax
import jax.numpy as jnp
from jax import lax
from jax.experimental import pallas as pl
from jax.experimental.pallas import tpu as pltpu
from jax.sharding import PartitionSpec as P


def split_of(groups):
    columns = max(c for c in range(1, groups + 1) if groups % c == 0 and c * c <= groups)
    return groups // columns, columns


def stepped(row, step, rows, back=False):
    if rows & (rows - 1) == 0:
        return row ^ step
    return (row + (rows - step if back else step)) % rows


def moved(value, sections, rows, columns, steps):
    groups = rows * columns
    pairs = []
    for section in range(sections):
        for row in range(rows):
            for column in range(columns):
                target = stepped(row, steps[1], rows) * columns + (column + steps[2]) % columns
                below = (section + steps[0]) % sections
                pairs.append((section * groups + row * columns + column, below * groups + target))
    return lax.ppermute(value, ("section", "blk"), pairs)


def row_order(rows):
    return sorted(range(rows), reverse=True)


def wrapped(value, count):
    return jnp.where(value >= count, value - count, value)


def sort_blocks(blocks, levels, plan):
    stride = blocks + 1
    count = plan.shape[0] // stride
    together = 4 if blocks % 4 == 0 else 1

    def place(step, ends):
        for i in range(together):
            block = step * together + i
            level = levels[block]
            for end in ends:
                plan[end] = block
            ends = tuple(end + jnp.where(level == own, 1, 0) for own, end in enumerate(ends))
        return ends

    ends = lax.fori_loop(0, blocks // together, place, tuple(jnp.int32(own * stride) for own in range(count)))
    for own, end in enumerate(ends):
        plan[own * stride + blocks] = end - own * stride


def solve_blocks(level, blocks, plan, inflow_of, kin, weight, pool):
    first = level * (blocks + 1)
    count = plan[first + blocks]
    ids = [plan[first + jnp.minimum(i, count - 1)] for i in range(blocks * 8 // 24)]
    solved = []
    for block in ids:
        mixed = jnp.dot(
            kin[block], inflow_of(block), precision=lax.Precision.HIGH, preferred_element_type=jnp.float32
        )
        solved.append(weight[pl.ds(block, 1), :] * mixed)
    for block, value in zip(ids, solved):
        pool[block] = value


def fill_sends(level, rows, columns, blocks, peers, downs, pool, outs):
    here = lax.axis_index("blk")
    row, column = here // columns, lax.rem(here, columns)
    ends = lax.axis_index("section") == lax.axis_size("section") - 1
    for row_step in range(rows):
        to_row = stepped(row, row_step, rows)
        for column_step in range(columns):
            target = to_row * columns + wrapped(column + column_step, columns)
            outs[column_step][row_step] = pool[peers[level, 0, target]]
            outs[columns + column_step][row_step] = pool[jnp.where(ends, blocks, downs[level, 0, target])]


def first_level(rows, columns, *refs):
    refs = list(refs)
    levels_in, kin_in, residual_in, weight_in, peers_in, downs_in, slots_in, frac_in = (refs.pop(0) for _ in range(8))
    pool, kin, plan_out, peers_out, downs_out, slots_out, residual, weight, frac = (refs.pop(0) for _ in range(9))
    outs = [refs.pop(0) for _ in range(2 * columns)]
    plan, levels, kin_here, peers, downs, sems = refs
    pairs = [(levels_in, levels), (kin_in, kin_here), (residual_in, residual), (weight_in, weight)]
    pairs += [(peers_in, peers), (downs_in, downs)]
    pairs += [(peers_in, peers_out), (downs_in, downs_out), (slots_in, slots_out), (frac_in, frac)]
    pairs += [(plan, plan_out)]
    copies = [pltpu.make_async_copy(source, target, sems.at[i]) for i, (source, target) in enumerate(pairs)]
    for copy in copies[:-1]:
        copy.start()
    blocks = residual.shape[0]
    pool[blocks] = jnp.zeros(pool.shape[1:], pool.dtype)
    copies[0].wait()
    sort_blocks(blocks, levels, plan)
    copies[-1].start()
    copies[1].wait()
    for i in range(kin.shape[1]):
        kin[:, i, :] = jnp.transpose(kin_here[i])
    for copy in copies[2:6]:
        copy.wait()

    solve_blocks(0, blocks, plan, lambda block: residual[block], kin, weight, pool)
    fill_sends(0, rows, columns, blocks, peers, downs, pool, outs)
    for copy in copies[6:]:
        copy.wait()


def later_level(level, rows, columns, plan, peers, downs, slots, residual, weight, frac, kin, *refs):
    refs = list(refs)
    arrived = [refs.pop(0) for _ in range(rows)]
    refs.pop(0)
    pool = refs.pop(0)
    outs = refs
    blocks, upw = residual.shape[0], slots.shape[0]
    rounds, groups = peers.shape[0], rows * columns
    here = lax.axis_index("blk")
    row, column = here // columns, lax.rem(here, columns)
    peers_first = blocks + 1 + (level - 1) * groups
    downs_first = peers_first + rounds * groups
    for part, row_step in zip(arrived, row_order(rows)):
        from_row = stepped(row, row_step, rows, back=True)
        for column_step in range(columns):
            source = from_row * columns + wrapped(column + columns - column_step, columns)
            pool[peers_first + source] = part[column_step]
            pool[downs_first + source] = part[columns + column_step]

    def inflow_of(block):
        inflow = residual[block]
        parts = frac[block]
        for k in range(upw):
            inflow = inflow + parts[k : k + 1, :] * pool[slots[k, block]]
        return inflow

    solve_blocks(level, blocks, plan, inflow_of, kin, weight, pool)
    if level < rounds:
        fill_sends(level, rows, columns, blocks, peers, downs, pool, outs)
    else:
        outs[0][...] = pool[pl.ds(0, blocks)]


def shards(
    residual, kin_inverse, cell_weight, upwind_frac, block_level, send_in, send_down, upwind_slot
):
    blocks, species, cells = residual.shape
    sections, groups = lax.axis_size("section"), lax.axis_size("blk")
    rows, columns = split_of(groups)
    rounds = send_in.shape[1]
    peers = send_in.transpose(1, 0, 2)
    downs = send_down.transpose(1, 0, 2)
    slots = upwind_slot.transpose(1, 0)
    kin_turned = kin_inverse.transpose(1, 2, 0)
    smem = pl.BlockSpec(memory_space=pltpu.SMEM)
    vmem = pl.BlockSpec(memory_space=pltpu.VMEM)
    hbm = pl.BlockSpec(memory_space=pltpu.HBM)
    params = pltpu.CompilerParams(vmem_limit_bytes=40 * 1024 * 1024)
    pool_shape = jax.ShapeDtypeStruct((blocks + 1 + 2 * rounds * groups, species, cells), jnp.float32)
    kin_shape = jax.ShapeDtypeStruct((blocks, species, species), jnp.float32)
    send_shapes = [jax.ShapeDtypeStruct((rows, species, cells), jnp.float32)] * (2 * columns)
    to_first = (block_level, kin_turned, residual, cell_weight, peers, downs, slots, upwind_frac)
    held = (peers, downs, slots, residual, cell_weight, upwind_frac)
    held_shapes = [jax.ShapeDtypeStruct(((rounds + 1) * (blocks + 1),), jnp.int32)]
    held_shapes += [jax.ShapeDtypeStruct(x.shape, x.dtype) for x in held]
    pool, kin, *outs = pl.pallas_call(
        functools.partial(first_level, rows, columns),
        in_specs=[hbm] * len(to_first),
        out_specs=[vmem] * (2 + len(held_shapes) + len(send_shapes)),
        out_shape=[pool_shape, kin_shape] + held_shapes + send_shapes,
        scratch_shapes=[
            pltpu.SMEM(held_shapes[0].shape, jnp.int32),
            pltpu.SMEM(block_level.shape, jnp.int32),
            pltpu.VMEM(kin_turned.shape, jnp.float32),
            pltpu.SMEM(peers.shape, jnp.int32),
            pltpu.SMEM(downs.shape, jnp.int32),
            pltpu.SemaphoreType.DMA((11,)),
        ],
        compiler_params=params,
        name="first_level",
    )(*(pltpu.with_memory_space_constraint(x, pltpu.HBM) for x in to_first))
    held, outs = outs[: len(held_shapes)], outs[len(held_shapes) :]
    for level in range(1, rounds + 1):
        turned = [outs[0]]
        turned += [moved(outs[c], sections, rows, columns, (0, 0, c)) for c in range(1, columns)]
        turned += [moved(outs[columns + c], sections, rows, columns, (1, 0, c)) for c in range(columns)]
        arrived = []
        for step in row_order(rows):
            part = jnp.stack([value[step] for value in turned])
            arrived.append(moved(part, sections, rows, columns, (0, step, 0)) if step else part)
        if level < rounds:
            out_shapes = send_shapes
        else:
            out_shapes = [jax.ShapeDtypeStruct(residual.shape, residual.dtype)]
        operands = held + [kin] + arrived + [pool]
        pool, *outs = pl.pallas_call(
            functools.partial(later_level, level, rows, columns),
            in_specs=[smem] * 4 + [vmem] * (len(operands) - 4),
            out_specs=[vmem] * (1 + len(out_shapes)),
            out_shape=[pool_shape] + out_shapes,
            input_output_aliases={len(operands) - 1: 0},
            compiler_params=params,
            name="later_level",
        )(*operands)
    return outs[0]


def solution(mesh):
    return jax.shard_map(
        shards,
        mesh=mesh,
        in_specs=(
            P(("section", "blk"), None, None),
            P(("section", "blk"), None, None),
            P(("section", "blk"), None),
            P(("section", "blk"), None, None),
            P(("section", "blk")),
            P(("section", "blk"), None, None),
            P(("section", "blk"), None, None),
            P(("section", "blk"), None),
        ),
        out_specs=P(("section", "blk"), None, None),
        check_vma=False,
    )
```

```python
import functools

import jax
import jax.numpy as jnp
from jax import lax
from jax.experimental import pallas as pl
from jax.experimental.pallas import tpu as pltpu
from jax.sharding import PartitionSpec as P


def split_of(groups):
    columns = max(c for c in range(1, groups + 1) if groups % c == 0 and c * c <= groups)
    return groups // columns, columns


def stepped(row, step, rows, back=False):
    if rows & (rows - 1) == 0:
        return row ^ step
    return (row + (rows - step if back else step)) % rows


def moved(value, sections, rows, columns, steps):
    groups = rows * columns
    pairs = []
    for section in range(sections):
        for row in range(rows):
            for column in range(columns):
                target = stepped(row, steps[1], rows) * columns + (column + steps[2]) % columns
                below = (section + steps[0]) % sections
                pairs.append((section * groups + row * columns + column, below * groups + target))
    return lax.ppermute(value, ("section", "blk"), pairs)


def halves_of(rows):
    return rows // 2 if rows > 1 and rows & (rows - 1) == 0 else rows


def wrapped(value, count):
    return jnp.where(value >= count, value - count, value)


def sort_blocks(blocks, levels, plan):
    stride = blocks + 1
    count = plan.shape[0] // stride
    together = 4 if blocks % 4 == 0 else 1

    def place(step, ends):
        for i in range(together):
            block = step * together + i
            level = levels[block]
            for end in ends:
                plan[end] = block
            ends = tuple(end + jnp.where(level == own, 1, 0) for own, end in enumerate(ends))
        return ends

    ends = lax.fori_loop(0, blocks // together, place, tuple(jnp.int32(own * stride) for own in range(count)))
    for own, end in enumerate(ends):
        plan[own * stride + blocks] = end - own * stride


def solve_blocks(level, blocks, plan, inflow_of, kin, weight, pool):
    first = level * (blocks + 1)
    count = plan[first + blocks]
    ids = [plan[first + jnp.minimum(i, count - 1)] for i in range(blocks * 8 // 24)]
    solved = []
    for block in ids:
        mixed = jnp.dot(
            kin[block], inflow_of(block), precision=lax.Precision.HIGH, preferred_element_type=jnp.float32
        )
        solved.append(weight[pl.ds(block, 1), :] * mixed)
    for block, value in zip(ids, solved):
        pool[block] = value


def fill_sends(level, rows, columns, blocks, peers, downs, pool, outs):
    here = lax.axis_index("blk")
    row, column = here // columns, lax.rem(here, columns)
    ends = lax.axis_index("section") == lax.axis_size("section") - 1
    half = halves_of(rows)
    for row_step in range(rows):
        to_row = stepped(row, row_step, rows)
        for column_step in range(columns):
            target = to_row * columns + wrapped(column + column_step, columns)
            outs[columns - 1 + column_step][row_step] = pool[jnp.where(ends, blocks, downs[level, 0, target])]
            peer = pool[peers[level, 0, target]]
            if column_step:
                outs[column_step - 1][row_step] = peer
            else:
                outs[2 * columns - 1 + row_step // half][row_step % half] = peer


def first_level(rows, columns, *refs):
    refs = list(refs)
    levels_in, kin_in, residual_in, weight_in, peers_in, downs_in, slots_in, frac_in = (refs.pop(0) for _ in range(8))
    pool, kin, plan_out, peers_out, downs_out, slots_out, residual, weight, frac = (refs.pop(0) for _ in range(9))
    outs = [refs.pop(0) for _ in range(2 * columns - 1 + rows // halves_of(rows))]
    plan, levels, kin_here, peers, downs, sems = refs
    pairs = [(levels_in, levels), (kin_in, kin_here), (residual_in, residual), (weight_in, weight)]
    pairs += [(peers_in, peers), (downs_in, downs)]
    pairs += [(peers_in, peers_out), (downs_in, downs_out), (slots_in, slots_out), (frac_in, frac)]
    pairs += [(plan, plan_out)]
    copies = [pltpu.make_async_copy(source, target, sems.at[i]) for i, (source, target) in enumerate(pairs)]
    for copy in copies[:-1]:
        copy.start()
    blocks = residual.shape[0]
    pool[blocks] = jnp.zeros(pool.shape[1:], pool.dtype)
    copies[0].wait()
    sort_blocks(blocks, levels, plan)
    copies[-1].start()
    copies[1].wait()
    for i in range(kin.shape[1]):
        kin[:, i, :] = jnp.transpose(kin_here[i])
    for copy in copies[2:6]:
        copy.wait()

    solve_blocks(0, blocks, plan, lambda block: residual[block], kin, weight, pool)
    fill_sends(0, rows, columns, blocks, peers, downs, pool, outs)
    for copy in copies[6:]:
        copy.wait()


def later_level(level, rows, columns, plan, peers, downs, slots, residual, weight, frac, kin, *refs):
    refs = list(refs)
    half = halves_of(rows)
    from_above = [refs.pop(0) for _ in range(columns)]
    over_columns = [None] + [refs.pop(0) for _ in range(1, columns)]
    own_column = [refs.pop(0) for _ in range(rows // half)]
    arrived = {step: refs.pop(0) for step in range(rows - 1, 0, -1)}
    refs.pop(0)
    pool = refs.pop(0)
    outs = refs
    blocks, upw = residual.shape[0], slots.shape[0]
    rounds, groups = peers.shape[0], rows * columns
    here = lax.axis_index("blk")
    row, column = here // columns, lax.rem(here, columns)
    peers_first = blocks + 1 + (level - 1) * groups
    downs_first = peers_first + rounds * groups
    for row_step in range(rows):
        from_row = stepped(row, row_step, rows, back=True)
        for column_step in range(columns):
            source = from_row * columns + wrapped(column + columns - column_step, columns)
            down = arrived[row_step].at[columns - 1 + column_step] if row_step else from_above[column_step].at[0]
            if column_step:
                peer = arrived[row_step].at[column_step - 1] if row_step else over_columns[column_step].at[0]
            else:
                at, rest = row_step // half, row_step % half
                peer = arrived[rest].at[2 * columns - 1 + at] if rest else own_column[at].at[0]
            pool[downs_first + source] = down[...]
            pool[peers_first + source] = peer[...]

    def inflow_of(block):
        inflow = residual[block]
        parts = frac[block]
        for k in range(upw):
            inflow = inflow + parts[k : k + 1, :] * pool[slots[k, block]]
        return inflow

    solve_blocks(level, blocks, plan, inflow_of, kin, weight, pool)
    if level < rounds:
        fill_sends(level, rows, columns, blocks, peers, downs, pool, outs)
    else:
        outs[0][...] = pool[pl.ds(0, blocks)]


def shards(
    residual, kin_inverse, cell_weight, upwind_frac, block_level, send_in, send_down, upwind_slot
):
    blocks, species, cells = residual.shape
    sections, groups = lax.axis_size("section"), lax.axis_size("blk")
    rows, columns = split_of(groups)
    rounds = send_in.shape[1]
    peers = send_in.transpose(1, 0, 2)
    downs = send_down.transpose(1, 0, 2)
    slots = upwind_slot.transpose(1, 0)
    kin_turned = kin_inverse.transpose(1, 2, 0)
    smem = pl.BlockSpec(memory_space=pltpu.SMEM)
    vmem = pl.BlockSpec(memory_space=pltpu.VMEM)
    hbm = pl.BlockSpec(memory_space=pltpu.HBM)
    params = pltpu.CompilerParams(vmem_limit_bytes=40 * 1024 * 1024)
    pool_shape = jax.ShapeDtypeStruct((blocks + 1 + 2 * rounds * groups, species, cells), jnp.float32)
    kin_shape = jax.ShapeDtypeStruct((blocks, species, species), jnp.float32)
    half = halves_of(rows)
    send_shapes = [jax.ShapeDtypeStruct((rows, species, cells), jnp.float32)] * (2 * columns - 1)
    send_shapes += [jax.ShapeDtypeStruct((half, species, cells), jnp.float32)] * (rows // half)
    to_first = (block_level, kin_turned, residual, cell_weight, peers, downs, slots, upwind_frac)
    held = (peers, downs, slots, residual, cell_weight, upwind_frac)
    held_shapes = [jax.ShapeDtypeStruct(((rounds + 1) * (blocks + 1),), jnp.int32)]
    held_shapes += [jax.ShapeDtypeStruct(x.shape, x.dtype) for x in held]
    pool, kin, *outs = pl.pallas_call(
        functools.partial(first_level, rows, columns),
        in_specs=[hbm] * len(to_first),
        out_specs=[vmem] * (2 + len(held_shapes) + len(send_shapes)),
        out_shape=[pool_shape, kin_shape] + held_shapes + send_shapes,
        scratch_shapes=[
            pltpu.SMEM(held_shapes[0].shape, jnp.int32),
            pltpu.SMEM(block_level.shape, jnp.int32),
            pltpu.VMEM(kin_turned.shape, jnp.float32),
            pltpu.SMEM(peers.shape, jnp.int32),
            pltpu.SMEM(downs.shape, jnp.int32),
            pltpu.SemaphoreType.DMA((11,)),
        ],
        compiler_params=params,
        name="first_level",
    )(*(pltpu.with_memory_space_constraint(x, pltpu.HBM) for x in to_first))
    held, outs = outs[: len(held_shapes)], outs[len(held_shapes) :]
    for level in range(1, rounds + 1):
        over_columns = [moved(outs[c - 1], sections, rows, columns, (0, 0, c)) for c in range(1, columns)]
        from_above = [moved(outs[columns - 1 + c], sections, rows, columns, (1, 0, c)) for c in range(columns)]
        over_columns, from_above = lax.optimization_barrier((over_columns, from_above))
        own_column = outs[2 * columns - 1 :]
        if half < rows:
            own_column[1] = moved(own_column[1], sections, rows, columns, (0, half, 0))
        arrived = []
        for step in range(rows - 1, 0, -1):
            part = [value[step] for value in over_columns + from_above]
            if step < half:
                part += [value[step] for value in own_column]
            arrived.append(moved(jnp.stack(part), sections, rows, columns, (0, step, 0)))
        if level < rounds:
            out_shapes = send_shapes
        else:
            out_shapes = [jax.ShapeDtypeStruct(residual.shape, residual.dtype)]
        operands = held + [kin] + from_above + over_columns + own_column + arrived + [pool]
        pool, *outs = pl.pallas_call(
            functools.partial(later_level, level, rows, columns),
            in_specs=[smem] * 4 + [vmem] * (len(operands) - 4),
            out_specs=[vmem] * (1 + len(out_shapes)),
            out_shape=[pool_shape] + out_shapes,
            input_output_aliases={len(operands) - 1: 0},
            compiler_params=params,
            name="later_level",
        )(*operands)
    return outs[0]


def solution(mesh):
    return jax.shard_map(
        shards,
        mesh=mesh,
        in_specs=(
            P(("section", "blk"), None, None),
            P(("section", "blk"), None, None),
            P(("section", "blk"), None),
            P(("section", "blk"), None, None),
            P(("section", "blk")),
            P(("section", "blk"), None, None),
            P(("section", "blk"), None, None),
            P(("section", "blk"), None),
        ),
        out_specs=P(("section", "blk"), None, None),
        check_vma=False,
    )
```

```python
import functools

import jax
import jax.numpy as jnp
from jax import lax
from jax.experimental import pallas as pl
from jax.experimental.pallas import tpu as pltpu
from jax.sharding import PartitionSpec as P


def split_of(groups):
    columns = max(c for c in range(1, groups + 1) if groups % c == 0 and c * c <= groups)
    return groups // columns, columns


def stepped(row, step, rows, back=False):
    if rows & (rows - 1) == 0:
        return row ^ step
    return (row + (rows - step if back else step)) % rows


def moved(value, sections, rows, columns, steps):
    groups = rows * columns
    pairs = []
    for section in range(sections):
        for row in range(rows):
            for column in range(columns):
                target = stepped(row, steps[1], rows) * columns + (column + steps[2]) % columns
                below = (section + steps[0]) % sections
                pairs.append((section * groups + row * columns + column, below * groups + target))
    return lax.ppermute(value, ("section", "blk"), pairs)


def halves_of(rows):
    return rows // 2 if rows > 1 and rows & (rows - 1) == 0 else rows


def row_steps(rows):
    half = halves_of(rows)
    return list(range(half, rows)) + list(range(1, half))


def wrapped(value, count):
    return jnp.where(value >= count, value - count, value)


def sort_blocks(blocks, levels, plan):
    stride = blocks + 1
    count = plan.shape[0] // stride
    together = 4 if blocks % 4 == 0 else 1

    def place(step, ends):
        for i in range(together):
            block = step * together + i
            level = levels[block]
            for end in ends:
                plan[end] = block
            ends = tuple(end + jnp.where(level == own, 1, 0) for own, end in enumerate(ends))
        return ends

    ends = lax.fori_loop(0, blocks // together, place, tuple(jnp.int32(own * stride) for own in range(count)))
    for own, end in enumerate(ends):
        plan[own * stride + blocks] = end - own * stride


def solve_blocks(level, blocks, plan, inflow_of, kin, weight, pool):
    first = level * (blocks + 1)
    count = plan[first + blocks]
    ids = [plan[first + jnp.minimum(i, count - 1)] for i in range(blocks * 8 // 24)]
    solved = []
    for block in ids:
        mixed = jnp.dot(
            kin[block], inflow_of(block), precision=lax.Precision.HIGH, preferred_element_type=jnp.float32
        )
        solved.append(weight[pl.ds(block, 1), :] * mixed)
    for block, value in zip(ids, solved):
        pool[block] = value


def fill_sends(level, rows, columns, blocks, peers, downs, pool, outs):
    here = lax.axis_index("blk")
    row, column = here // columns, lax.rem(here, columns)
    ends = lax.axis_index("section") == lax.axis_size("section") - 1
    half = halves_of(rows)
    for row_step in range(rows):
        to_row = stepped(row, row_step, rows)
        for column_step in range(columns):
            target = to_row * columns + wrapped(column + column_step, columns)
            outs[columns - 1 + column_step][row_step] = pool[jnp.where(ends, blocks, downs[level, 0, target])]
            peer = pool[peers[level, 0, target]]
            if column_step:
                outs[column_step - 1][row_step] = peer
            else:
                outs[2 * columns - 1 + row_step // half][row_step % half] = peer


def first_level(rows, columns, *refs):
    refs = list(refs)
    levels_in, kin_in, residual_in, weight_in, peers_in, downs_in, slots_in, frac_in = (refs.pop(0) for _ in range(8))
    pool, kin, plan_out, peers_out, downs_out, slots_out, residual, weight, frac = (refs.pop(0) for _ in range(9))
    outs = [refs.pop(0) for _ in range(2 * columns - 1 + rows // halves_of(rows))]
    plan, levels, kin_here, peers, downs, sems = refs
    pairs = [(levels_in, levels), (kin_in, kin_here), (residual_in, residual), (weight_in, weight)]
    pairs += [(peers_in, peers), (downs_in, downs)]
    pairs += [(peers_in, peers_out), (downs_in, downs_out), (slots_in, slots_out), (frac_in, frac)]
    pairs += [(plan, plan_out)]
    copies = [pltpu.make_async_copy(source, target, sems.at[i]) for i, (source, target) in enumerate(pairs)]
    for copy in copies[:-1]:
        copy.start()
    blocks = residual.shape[0]
    pool[blocks] = jnp.zeros(pool.shape[1:], pool.dtype)
    copies[0].wait()
    sort_blocks(blocks, levels, plan)
    copies[-1].start()
    copies[1].wait()
    for i in range(kin.shape[1]):
        kin[:, i, :] = jnp.transpose(kin_here[i])
    for copy in copies[2:6]:
        copy.wait()

    solve_blocks(0, blocks, plan, lambda block: residual[block], kin, weight, pool)
    fill_sends(0, rows, columns, blocks, peers, downs, pool, outs)
    for copy in copies[6:]:
        copy.wait()


def later_level(level, rows, columns, plan, peers, downs, slots, residual, weight, frac, kin, *refs):
    refs = list(refs)
    half = halves_of(rows)
    from_above = [refs.pop(0) for _ in range(columns)]
    over_columns = [None] + [refs.pop(0) for _ in range(1, columns)]
    own_column = [refs.pop(0) for _ in range(rows // half)]
    arrived = {step: refs.pop(0) for step in row_steps(rows)}
    refs.pop(0)
    pool = refs.pop(0)
    outs = refs
    blocks, upw = residual.shape[0], slots.shape[0]
    rounds, groups = peers.shape[0], rows * columns
    here = lax.axis_index("blk")
    row, column = here // columns, lax.rem(here, columns)
    peers_first = blocks + 1 + (level - 1) * groups
    downs_first = peers_first + rounds * groups
    for row_step in range(rows):
        from_row = stepped(row, row_step, rows, back=True)
        for column_step in range(columns):
            source = from_row * columns + wrapped(column + columns - column_step, columns)
            down = arrived[row_step].at[columns - 1 + column_step] if row_step else from_above[column_step].at[0]
            if column_step:
                peer = arrived[row_step].at[column_step - 1] if row_step else over_columns[column_step].at[0]
            else:
                at, rest = row_step // half, row_step % half
                peer = arrived[rest].at[2 * columns - 1 + at] if rest else own_column[at].at[0]
            pool[downs_first + source] = down[...]
            pool[peers_first + source] = peer[...]

    def inflow_of(block):
        inflow = residual[block]
        parts = frac[block]
        for k in range(upw):
            inflow = inflow + parts[k : k + 1, :] * pool[slots[k, block]]
        return inflow

    solve_blocks(level, blocks, plan, inflow_of, kin, weight, pool)
    if level < rounds:
        fill_sends(level, rows, columns, blocks, peers, downs, pool, outs)
    else:
        outs[0][...] = pool[pl.ds(0, blocks)]


def shards(
    residual, kin_inverse, cell_weight, upwind_frac, block_level, send_in, send_down, upwind_slot
):
    blocks, species, cells = residual.shape
    sections, groups = lax.axis_size("section"), lax.axis_size("blk")
    rows, columns = split_of(groups)
    rounds = send_in.shape[1]
    peers = send_in.transpose(1, 0, 2)
    downs = send_down.transpose(1, 0, 2)
    slots = upwind_slot.transpose(1, 0)
    kin_turned = kin_inverse.transpose(1, 2, 0)
    smem = pl.BlockSpec(memory_space=pltpu.SMEM)
    vmem = pl.BlockSpec(memory_space=pltpu.VMEM)
    hbm = pl.BlockSpec(memory_space=pltpu.HBM)
    params = pltpu.CompilerParams(vmem_limit_bytes=40 * 1024 * 1024)
    pool_shape = jax.ShapeDtypeStruct((blocks + 1 + 2 * rounds * groups, species, cells), jnp.float32)
    kin_shape = jax.ShapeDtypeStruct((blocks, species, species), jnp.float32)
    half = halves_of(rows)
    send_shapes = [jax.ShapeDtypeStruct((rows, species, cells), jnp.float32)] * (2 * columns - 1)
    send_shapes += [jax.ShapeDtypeStruct((half, species, cells), jnp.float32)] * (rows // half)
    to_first = (block_level, kin_turned, residual, cell_weight, peers, downs, slots, upwind_frac)
    held = (peers, downs, slots, residual, cell_weight, upwind_frac)
    held_shapes = [jax.ShapeDtypeStruct(((rounds + 1) * (blocks + 1),), jnp.int32)]
    held_shapes += [jax.ShapeDtypeStruct(x.shape, x.dtype) for x in held]
    pool, kin, *outs = pl.pallas_call(
        functools.partial(first_level, rows, columns),
        in_specs=[hbm] * len(to_first),
        out_specs=[vmem] * (2 + len(held_shapes) + len(send_shapes)),
        out_shape=[pool_shape, kin_shape] + held_shapes + send_shapes,
        scratch_shapes=[
            pltpu.SMEM(held_shapes[0].shape, jnp.int32),
            pltpu.SMEM(block_level.shape, jnp.int32),
            pltpu.VMEM(kin_turned.shape, jnp.float32),
            pltpu.SMEM(peers.shape, jnp.int32),
            pltpu.SMEM(downs.shape, jnp.int32),
            pltpu.SemaphoreType.DMA((11,)),
        ],
        compiler_params=params,
        name="first_level",
    )(*(pltpu.with_memory_space_constraint(x, pltpu.HBM) for x in to_first))
    held, outs = outs[: len(held_shapes)], outs[len(held_shapes) :]
    for level in range(1, rounds + 1):
        over_columns = [moved(outs[c - 1], sections, rows, columns, (0, 0, c)) for c in range(1, columns)]
        from_above = [moved(outs[columns - 1 + c], sections, rows, columns, (1, 0, c)) for c in range(columns)]
        over_columns, from_above = lax.optimization_barrier((over_columns, from_above))
        own_column = outs[2 * columns - 1 :]
        if half < rows:
            own_column[1] = moved(own_column[1], sections, rows, columns, (0, half, 0))
        arrived = []
        for step in row_steps(rows):
            part = [value[step] for value in over_columns + from_above]
            if step < half:
                part += [value[step] for value in own_column]
            arrived.append(moved(jnp.stack(part), sections, rows, columns, (0, step, 0)))
        if level < rounds:
            out_shapes = send_shapes
        else:
            out_shapes = [jax.ShapeDtypeStruct(residual.shape, residual.dtype)]
        operands = held + [kin] + from_above + over_columns + own_column + arrived + [pool]
        pool, *outs = pl.pallas_call(
            functools.partial(later_level, level, rows, columns),
            in_specs=[smem] * 4 + [vmem] * (len(operands) - 4),
            out_specs=[vmem] * (1 + len(out_shapes)),
            out_shape=[pool_shape] + out_shapes,
            input_output_aliases={len(operands) - 1: 0},
            compiler_params=params,
            name="later_level",
        )(*operands)
    return outs[0]


def solution(mesh):
    return jax.shard_map(
        shards,
        mesh=mesh,
        in_specs=(
            P(("section", "blk"), None, None),
            P(("section", "blk"), None, None),
            P(("section", "blk"), None),
            P(("section", "blk"), None, None),
            P(("section", "blk")),
            P(("section", "blk"), None, None),
            P(("section", "blk"), None, None),
            P(("section", "blk"), None),
        ),
        out_specs=P(("section", "blk"), None, None),
        check_vma=False,
    )
```

```python
import functools

import jax
import jax.numpy as jnp
from jax import lax
from jax.experimental import pallas as pl
from jax.experimental.pallas import tpu as pltpu
from jax.sharding import PartitionSpec as P


def split_of(groups):
    columns = max(c for c in range(1, groups + 1) if groups % c == 0 and c * c <= groups)
    return groups // columns, columns


def stepped(row, step, rows, back=False):
    if rows & (rows - 1) == 0:
        return row ^ step
    return (row + (rows - step if back else step)) % rows


def moved(value, sections, rows, columns, steps):
    groups = rows * columns
    pairs = []
    for section in range(sections):
        for row in range(rows):
            for column in range(columns):
                target = stepped(row, steps[1], rows) * columns + (column + steps[2]) % columns
                below = (section + steps[0]) % sections
                pairs.append((section * groups + row * columns + column, below * groups + target))
    return lax.ppermute(value, ("section", "blk"), pairs)


def halves_of(rows):
    return rows // 2 if rows > 1 and rows & (rows - 1) == 0 else rows


def wrapped(value, count):
    return jnp.where(value >= count, value - count, value)


def sort_blocks(blocks, levels, plan):
    stride = blocks + 1
    count = plan.shape[0] // stride
    together = 4 if blocks % 4 == 0 else 1

    def place(step, ends):
        for i in range(together):
            block = step * together + i
            level = levels[block]
            for end in ends:
                plan[end] = block
            ends = tuple(end + jnp.where(level == own, 1, 0) for own, end in enumerate(ends))
        return ends

    ends = lax.fori_loop(0, blocks // together, place, tuple(jnp.int32(own * stride) for own in range(count)))
    for own, end in enumerate(ends):
        plan[own * stride + blocks] = end - own * stride


def solve_blocks(level, blocks, plan, inflow_of, kin, weight, pool):
    first = level * (blocks + 1)
    count = plan[first + blocks]
    ids = [plan[first + jnp.minimum(i, count - 1)] for i in range(blocks * 8 // 24)]
    solved = []
    for block in ids:
        mixed = jnp.dot(
            kin[block], inflow_of(block), precision=lax.Precision.HIGH, preferred_element_type=jnp.float32
        )
        solved.append(weight[pl.ds(block, 1), :] * mixed)
    for block, value in zip(ids, solved):
        pool[block] = value


def fill_sends(level, rows, columns, blocks, peers, downs, pool, outs):
    here = lax.axis_index("blk")
    row, column = here // columns, lax.rem(here, columns)
    ends = lax.axis_index("section") == lax.axis_size("section") - 1
    half = halves_of(rows)
    for row_step in range(rows):
        to_row = stepped(row, row_step, rows)
        for column_step in range(columns):
            target = to_row * columns + wrapped(column + column_step, columns)
            outs[columns - 1 + column_step][row_step] = pool[jnp.where(ends, blocks, downs[level, 0, target])]
            peer = pool[peers[level, 0, target]]
            if column_step:
                outs[column_step - 1][row_step] = peer
            else:
                outs[2 * columns - 1 + row_step // half][row_step % half] = peer


def first_level(rows, columns, *refs):
    refs = list(refs)
    levels_in, kin_in, residual_in, weight_in, peers_in, downs_in, slots_in, frac_in = (refs.pop(0) for _ in range(8))
    pool, kin, plan_out, peers_out, downs_out, slots_out, residual, weight, frac = (refs.pop(0) for _ in range(9))
    outs = [refs.pop(0) for _ in range(2 * columns - 1 + rows // halves_of(rows))]
    plan, levels, kin_here, peers, downs, sems = refs
    pairs = [(levels_in, levels), (kin_in, kin_here), (residual_in, residual), (weight_in, weight)]
    pairs += [(peers_in, peers), (downs_in, downs)]
    pairs += [(peers_in, peers_out), (downs_in, downs_out), (slots_in, slots_out), (frac_in, frac)]
    pairs += [(plan, plan_out)]
    copies = [pltpu.make_async_copy(source, target, sems.at[i]) for i, (source, target) in enumerate(pairs)]
    for copy in copies[:-1]:
        copy.start()
    blocks = residual.shape[0]
    pool[blocks] = jnp.zeros(pool.shape[1:], pool.dtype)
    copies[0].wait()
    sort_blocks(blocks, levels, plan)
    copies[-1].start()
    copies[1].wait()
    for i in range(kin.shape[1]):
        kin[:, i, :] = jnp.transpose(kin_here[i])
    for copy in copies[2:6]:
        copy.wait()

    solve_blocks(0, blocks, plan, lambda block: residual[block], kin, weight, pool)
    fill_sends(0, rows, columns, blocks, peers, downs, pool, outs)
    for copy in copies[6:]:
        copy.wait()


def later_level(level, rows, columns, plan, peers, downs, slots, residual, weight, frac, kin, *refs):
    refs = list(refs)
    half = halves_of(rows)
    from_above = [refs.pop(0) for _ in range(columns)]
    over_columns = [None] + [refs.pop(0) for _ in range(1, columns)]
    own_column = [refs.pop(0) for _ in range(rows // half)]
    arrived = {step: refs.pop(0) for step in range(rows - 1, 0, -1)}
    refs.pop(0)
    pool = refs.pop(0)
    outs = refs
    blocks, upw = residual.shape[0], slots.shape[0]
    rounds, groups = peers.shape[0], rows * columns
    here = lax.axis_index("blk")
    row, column = here // columns, lax.rem(here, columns)
    peers_first = blocks + 1 + (level - 1) * groups
    downs_first = peers_first + rounds * groups
    for row_step in range(rows):
        from_row = stepped(row, row_step, rows, back=True)
        for column_step in range(columns):
            source = from_row * columns + wrapped(column + columns - column_step, columns)
            down = arrived[row_step].at[columns - 1 + column_step] if row_step else from_above[column_step].at[0]
            if column_step:
                peer = arrived[row_step].at[column_step - 1] if row_step else over_columns[column_step].at[0]
            else:
                at, rest = row_step // half, row_step % half
                peer = arrived[rest].at[2 * columns - 1 + at] if rest else own_column[at].at[0]
            pool[downs_first + source] = down[...]
            pool[peers_first + source] = peer[...]

    def inflow_of(block):
        inflow = residual[block]
        parts = frac[block]
        for k in range(upw):
            inflow = inflow + parts[k : k + 1, :] * pool[slots[k, block]]
        return inflow

    solve_blocks(level, blocks, plan, inflow_of, kin, weight, pool)
    if level < rounds:
        fill_sends(level, rows, columns, blocks, peers, downs, pool, outs)
    else:
        outs[0][...] = pool[pl.ds(0, blocks)]


def shards(
    residual, kin_inverse, cell_weight, upwind_frac, block_level, send_in, send_down, upwind_slot
):
    blocks, species, cells = residual.shape
    sections, groups = lax.axis_size("section"), lax.axis_size("blk")
    rows, columns = split_of(groups)
    rounds = send_in.shape[1]
    peers = send_in.transpose(1, 0, 2)
    downs = send_down.transpose(1, 0, 2)
    slots = upwind_slot.transpose(1, 0)
    kin_turned = kin_inverse.transpose(1, 2, 0)
    smem = pl.BlockSpec(memory_space=pltpu.SMEM)
    vmem = pl.BlockSpec(memory_space=pltpu.VMEM)
    hbm = pl.BlockSpec(memory_space=pltpu.HBM)
    params = pltpu.CompilerParams(vmem_limit_bytes=40 * 1024 * 1024)
    pool_shape = jax.ShapeDtypeStruct((blocks + 1 + 2 * rounds * groups, species, cells), jnp.float32)
    kin_shape = jax.ShapeDtypeStruct((blocks, species, species), jnp.float32)
    half = halves_of(rows)
    send_shapes = [jax.ShapeDtypeStruct((rows, species, cells), jnp.float32)] * (2 * columns - 1)
    send_shapes += [jax.ShapeDtypeStruct((half, species, cells), jnp.float32)] * (rows // half)
    to_first = (block_level, kin_turned, residual, cell_weight, peers, downs, slots, upwind_frac)
    held = (peers, downs, slots, residual, cell_weight, upwind_frac)
    held_shapes = [jax.ShapeDtypeStruct(((rounds + 1) * (blocks + 1),), jnp.int32)]
    held_shapes += [jax.ShapeDtypeStruct(x.shape, x.dtype) for x in held]
    pool, kin, *outs = pl.pallas_call(
        functools.partial(first_level, rows, columns),
        in_specs=[hbm] * len(to_first),
        out_specs=[vmem] * (2 + len(held_shapes) + len(send_shapes)),
        out_shape=[pool_shape, kin_shape] + held_shapes + send_shapes,
        scratch_shapes=[
            pltpu.SMEM(held_shapes[0].shape, jnp.int32),
            pltpu.SMEM(block_level.shape, jnp.int32),
            pltpu.VMEM(kin_turned.shape, jnp.float32),
            pltpu.SMEM(peers.shape, jnp.int32),
            pltpu.SMEM(downs.shape, jnp.int32),
            pltpu.SemaphoreType.DMA((11,)),
        ],
        compiler_params=params,
        name="first_level",
    )(*(pltpu.with_memory_space_constraint(x, pltpu.HBM) for x in to_first))
    held, outs = outs[: len(held_shapes)], outs[len(held_shapes) :]
    for level in range(1, rounds + 1):
        over_columns = [moved(outs[c - 1], sections, rows, columns, (0, 0, c)) for c in range(1, columns)]
        from_above = [moved(outs[columns - 1 + c], sections, rows, columns, (1, 0, c)) for c in range(columns)]
        own_column = outs[2 * columns - 1 :]
        over_columns, own_column = lax.optimization_barrier((over_columns, own_column))
        over_columns, from_above = lax.optimization_barrier((over_columns, from_above))
        if half < rows:
            own_column[1] = moved(own_column[1], sections, rows, columns, (0, half, 0))
        arrived = []
        for step in range(rows - 1, 0, -1):
            part = [value[step] for value in over_columns + from_above]
            if step < half:
                part += [value[step] for value in own_column]
            arrived.append(moved(jnp.stack(part), sections, rows, columns, (0, step, 0)))
        if level < rounds:
            out_shapes = send_shapes
        else:
            out_shapes = [jax.ShapeDtypeStruct(residual.shape, residual.dtype)]
        operands = held + [kin] + from_above + over_columns + own_column + arrived + [pool]
        pool, *outs = pl.pallas_call(
            functools.partial(later_level, level, rows, columns),
            in_specs=[smem] * 4 + [vmem] * (len(operands) - 4),
            out_specs=[vmem] * (1 + len(out_shapes)),
            out_shape=[pool_shape] + out_shapes,
            input_output_aliases={len(operands) - 1: 0},
            compiler_params=params,
            name="later_level",
        )(*operands)
    return outs[0]


def solution(mesh):
    return jax.shard_map(
        shards,
        mesh=mesh,
        in_specs=(
            P(("section", "blk"), None, None),
            P(("section", "blk"), None, None),
            P(("section", "blk"), None),
            P(("section", "blk"), None, None),
            P(("section", "blk")),
            P(("section", "blk"), None, None),
            P(("section", "blk"), None, None),
            P(("section", "blk"), None),
        ),
        out_specs=P(("section", "blk"), None, None),
        check_vma=False,
    )
```

```python
import functools

import jax
import jax.numpy as jnp
from jax import lax
from jax.experimental import pallas as pl
from jax.experimental.pallas import tpu as pltpu
from jax.sharding import PartitionSpec as P


def split_of(groups):
    columns = max(c for c in range(1, groups + 1) if groups % c == 0 and c * c <= groups)
    return groups // columns, columns


def stepped(row, step, rows, back=False):
    if rows & (rows - 1) == 0:
        return row ^ step
    return (row + (rows - step if back else step)) % rows


def moved(value, sections, rows, columns, steps):
    groups = rows * columns
    pairs = []
    for section in range(sections):
        for row in range(rows):
            for column in range(columns):
                target = stepped(row, steps[1], rows) * columns + (column + steps[2]) % columns
                below = (section + steps[0]) % sections
                pairs.append((section * groups + row * columns + column, below * groups + target))
    return lax.ppermute(value, ("section", "blk"), pairs)


def halves_of(rows):
    return rows // 2 if rows > 1 and rows & (rows - 1) == 0 else rows


def wrapped(value, count):
    return jnp.where(value >= count, value - count, value)


def sort_blocks(blocks, levels, plan):
    stride = blocks + 1
    count = plan.shape[0] // stride
    together = 4 if blocks % 4 == 0 else 1

    def place(step, ends):
        for i in range(together):
            block = step * together + i
            level = levels[block]
            for end in ends:
                plan[end] = block
            ends = tuple(end + jnp.where(level == own, 1, 0) for own, end in enumerate(ends))
        return ends

    ends = lax.fori_loop(0, blocks // together, place, tuple(jnp.int32(own * stride) for own in range(count)))
    for own, end in enumerate(ends):
        plan[own * stride + blocks] = end - own * stride


def solve_blocks(level, blocks, plan, inflow_of, kin, weight, pool):
    first = level * (blocks + 1)
    count = plan[first + blocks]
    ids = [plan[first + jnp.minimum(i, count - 1)] for i in range(blocks * 8 // 24)]
    solved = []
    for block in ids:
        mixed = jnp.dot(
            kin[block], inflow_of(block), precision=lax.Precision.HIGH, preferred_element_type=jnp.float32
        )
        solved.append(weight[pl.ds(block, 1), :] * mixed)
    for block, value in zip(ids, solved):
        pool[block] = value


def fill_sends(level, rows, columns, blocks, peers, downs, pool, outs):
    here = lax.axis_index("blk")
    row, column = here // columns, lax.rem(here, columns)
    ends = lax.axis_index("section") == lax.axis_size("section") - 1
    half = halves_of(rows)
    for row_step in range(rows):
        to_row = stepped(row, row_step, rows)
        for column_step in range(columns):
            target = to_row * columns + wrapped(column + column_step, columns)
            outs[columns - 1 + column_step][row_step] = pool[jnp.where(ends, blocks, downs[level, 0, target])]
            peer = pool[peers[level, 0, target]]
            if column_step:
                outs[column_step - 1][row_step] = peer
            else:
                outs[2 * columns - 1 + row_step // half][row_step % half] = peer


def first_level(rows, columns, *refs):
    refs = list(refs)
    levels_in, kin_in, residual_in, weight_in, peers_in, downs_in, slots_in, frac_in = (refs.pop(0) for _ in range(8))
    pool, kin, plan_out, peers_out, downs_out, slots_out, residual, weight, frac = (refs.pop(0) for _ in range(9))
    outs = [refs.pop(0) for _ in range(2 * columns - 1 + rows // halves_of(rows))]
    plan, levels, kin_here, peers, downs, sems = refs
    pairs = [(levels_in, levels), (kin_in, kin_here), (residual_in, residual), (weight_in, weight)]
    pairs += [(peers_in, peers), (downs_in, downs)]
    pairs += [(peers_in, peers_out), (downs_in, downs_out), (slots_in, slots_out), (frac_in, frac)]
    pairs += [(plan, plan_out)]
    copies = [pltpu.make_async_copy(source, target, sems.at[i]) for i, (source, target) in enumerate(pairs)]
    for copy in copies[:-1]:
        copy.start()
    blocks = residual.shape[0]
    pool[blocks] = jnp.zeros(pool.shape[1:], pool.dtype)
    copies[0].wait()
    sort_blocks(blocks, levels, plan)
    copies[-1].start()
    copies[1].wait()
    for i in range(kin.shape[1]):
        kin[:, i, :] = jnp.transpose(kin_here[i])
    for copy in copies[2:6]:
        copy.wait()

    solve_blocks(0, blocks, plan, lambda block: residual[block], kin, weight, pool)
    fill_sends(0, rows, columns, blocks, peers, downs, pool, outs)
    for copy in copies[6:]:
        copy.wait()


def later_level(level, rows, columns, plan, peers, downs, slots, residual, weight, frac, kin, *refs):
    refs = list(refs)
    half = halves_of(rows)
    from_above = [refs.pop(0) for _ in range(columns)]
    over_columns = [None] + [refs.pop(0) for _ in range(1, columns)]
    own_column = [refs.pop(0) for _ in range(rows // half)]
    arrived = {step: refs.pop(0) for step in range(rows - 1, 0, -1)}
    refs.pop(0)
    pool = refs.pop(0)
    outs = refs
    blocks, upw = residual.shape[0], slots.shape[0]
    rounds, groups = peers.shape[0], rows * columns
    here = lax.axis_index("blk")
    row, column = here // columns, lax.rem(here, columns)
    peers_first = blocks + 1 + (level - 1) * groups
    downs_first = peers_first + rounds * groups
    for row_step in range(rows):
        from_row = stepped(row, row_step, rows, back=True)
        for column_step in range(columns):
            source = from_row * columns + wrapped(column + columns - column_step, columns)
            down = arrived[row_step].at[column_step] if row_step else from_above[column_step].at[0]
            if column_step:
                peer = arrived[row_step].at[columns - 1 + column_step] if row_step else over_columns[column_step].at[0]
            else:
                at, rest = row_step // half, row_step % half
                peer = arrived[rest].at[2 * columns - 1 + at] if rest else own_column[at].at[0]
            pool[downs_first + source] = down[...]
            pool[peers_first + source] = peer[...]

    def inflow_of(block):
        inflow = residual[block]
        parts = frac[block]
        for k in range(upw):
            inflow = inflow + parts[k : k + 1, :] * pool[slots[k, block]]
        return inflow

    solve_blocks(level, blocks, plan, inflow_of, kin, weight, pool)
    if level < rounds:
        fill_sends(level, rows, columns, blocks, peers, downs, pool, outs)
    else:
        outs[0][...] = pool[pl.ds(0, blocks)]


def shards(
    residual, kin_inverse, cell_weight, upwind_frac, block_level, send_in, send_down, upwind_slot
):
    blocks, species, cells = residual.shape
    sections, groups = lax.axis_size("section"), lax.axis_size("blk")
    rows, columns = split_of(groups)
    rounds = send_in.shape[1]
    peers = send_in.transpose(1, 0, 2)
    downs = send_down.transpose(1, 0, 2)
    slots = upwind_slot.transpose(1, 0)
    kin_turned = kin_inverse.transpose(1, 2, 0)
    smem = pl.BlockSpec(memory_space=pltpu.SMEM)
    vmem = pl.BlockSpec(memory_space=pltpu.VMEM)
    hbm = pl.BlockSpec(memory_space=pltpu.HBM)
    params = pltpu.CompilerParams(vmem_limit_bytes=40 * 1024 * 1024)
    pool_shape = jax.ShapeDtypeStruct((blocks + 1 + 2 * rounds * groups, species, cells), jnp.float32)
    kin_shape = jax.ShapeDtypeStruct((blocks, species, species), jnp.float32)
    half = halves_of(rows)
    send_shapes = [jax.ShapeDtypeStruct((rows, species, cells), jnp.float32)] * (2 * columns - 1)
    send_shapes += [jax.ShapeDtypeStruct((half, species, cells), jnp.float32)] * (rows // half)
    to_first = (block_level, kin_turned, residual, cell_weight, peers, downs, slots, upwind_frac)
    held = (peers, downs, slots, residual, cell_weight, upwind_frac)
    held_shapes = [jax.ShapeDtypeStruct(((rounds + 1) * (blocks + 1),), jnp.int32)]
    held_shapes += [jax.ShapeDtypeStruct(x.shape, x.dtype) for x in held]
    pool, kin, *outs = pl.pallas_call(
        functools.partial(first_level, rows, columns),
        in_specs=[hbm] * len(to_first),
        out_specs=[vmem] * (2 + len(held_shapes) + len(send_shapes)),
        out_shape=[pool_shape, kin_shape] + held_shapes + send_shapes,
        scratch_shapes=[
            pltpu.SMEM(held_shapes[0].shape, jnp.int32),
            pltpu.SMEM(block_level.shape, jnp.int32),
            pltpu.VMEM(kin_turned.shape, jnp.float32),
            pltpu.SMEM(peers.shape, jnp.int32),
            pltpu.SMEM(downs.shape, jnp.int32),
            pltpu.SemaphoreType.DMA((11,)),
        ],
        compiler_params=params,
        name="first_level",
    )(*(pltpu.with_memory_space_constraint(x, pltpu.HBM) for x in to_first))
    held, outs = outs[: len(held_shapes)], outs[len(held_shapes) :]
    for level in range(1, rounds + 1):
        over_columns = [moved(outs[c - 1], sections, rows, columns, (0, 0, c)) for c in range(1, columns)]
        from_above = [moved(outs[columns - 1 + c], sections, rows, columns, (1, 0, c)) for c in range(columns)]
        from_above = lax.optimization_barrier(from_above)
        own_column = outs[2 * columns - 1 :]
        if half < rows:
            own_column[1] = moved(own_column[1], sections, rows, columns, (0, half, 0))
        arrived = []
        for step in range(rows - 1, 0, -1):
            part = [value[step] for value in from_above + over_columns]
            if step < half:
                part += [value[step] for value in own_column]
            arrived.append(moved(jnp.stack(part), sections, rows, columns, (0, step, 0)))
        if level < rounds:
            out_shapes = send_shapes
        else:
            out_shapes = [jax.ShapeDtypeStruct(residual.shape, residual.dtype)]
        operands = held + [kin] + from_above + over_columns + own_column + arrived + [pool]
        pool, *outs = pl.pallas_call(
            functools.partial(later_level, level, rows, columns),
            in_specs=[smem] * 4 + [vmem] * (len(operands) - 4),
            out_specs=[vmem] * (1 + len(out_shapes)),
            out_shape=[pool_shape] + out_shapes,
            input_output_aliases={len(operands) - 1: 0},
            compiler_params=params,
            name="later_level",
        )(*operands)
    return outs[0]


def solution(mesh):
    return jax.shard_map(
        shards,
        mesh=mesh,
        in_specs=(
            P(("section", "blk"), None, None),
            P(("section", "blk"), None, None),
            P(("section", "blk"), None),
            P(("section", "blk"), None, None),
            P(("section", "blk")),
            P(("section", "blk"), None, None),
            P(("section", "blk"), None, None),
            P(("section", "blk"), None),
        ),
        out_specs=P(("section", "blk"), None, None),
        check_vma=False,
    )
```
